128 devices in a mesh: dp: 4 (over z), tp: 32 (over y, x, core).
Axes of the slice: x: 4, y: 4, z: 4, core: 2. Of those that a mesh axis runs over, the one named last changes fastest.
Arguments:
- layer_input: bfloat16 [512, 7168], P(('dp', 'tp')), may hold values from -16 to 16
- query: bfloat16 [512, 64, 576], P(('dp', 'tp')), may hold values from -48 to 48
- cache: bfloat16 [512, 2048, 576], P(('dp', 'tp')), may hold values from -8 to 8
- lengths: int32 [512], P(('dp', 'tp')), may hold values from 2 to 2048, as said below
- counts: int32 [128], P(('dp', 'tp')), may hold values from 1 to 4, as said below
- value_weight: bfloat16 [64, 512, 128], P('tp'), may hold values from -0.25 to 0.25
- output_weight: bfloat16 [8192, 7168], P('tp'), may hold values from -0.0625 to 0.0625
- norm_gain: float32 [7168], replicated, may hold values from 0.1 to 1.9
- gate_weight: bfloat16 [7168, 9216], P(None, 'tp'), may hold values from -0.0625 to 0.0625
- up_weight: bfloat16 [7168, 9216], P(None, 'tp'), may hold values from -0.0625 to 0.0625
- down_weight: bfloat16 [9216, 7168], P('tp', 'dp'), may hold values from -0.0625 to 0.0625
Outputs:
- layer_output: bfloat16 [512, 7168], P(('dp', 'tp'))
The draws below stay inside these ranges and needn't reach their ends.
Inputs may be any that keep to these rules, and one draw needn't show every extreme that they name: `counts`: one device holds 4 live slots and another one. `lengths`: on every device some live slot has 2048 valid positions.
All inputs are finite; a program needn't handle non-finite values.
Results may differ from the reference program's by a relative error of at most 0.014.
Values may be sent and summed in bfloat16 or wider, within the bound.
No kernel may reach another device: no remote copies, remote signals or barrier semaphores. Data moves between devices by JAX's collectives and lax.ppermute only.
A program may use at most 128 MiB of HBM per device.

```python
import math
import jax
import jax.numpy as jnp
from jax import lax

D = 7168
FF = 9216
H = 64
LAT = 512
ROPE = 64
HEAD = 128
CTX = 2048
ROWS = 4
OWNERS = 128
SLOTS = 512


def shared_counts(key):
    key = jax.random.fold_in(key, 501)
    first_key, second_key, third_key = jax.random.split(key, 3)
    counts = jax.random.randint(first_key, (OWNERS,), 1, ROWS + 1)
    fullest = jax.random.randint(second_key, (), 0, OWNERS)
    emptiest = (fullest + 1 + jax.random.randint(third_key, (), 0, OWNERS - 1)) % OWNERS
    return counts.at[fullest].set(ROWS).at[emptiest].set(1)


def shared_keys(key):
    key = jax.random.fold_in(key, 611)
    first_key, second_key = jax.random.split(key, 2)
    leading = jnp.clip(jax.random.normal(first_key, (SLOTS, 2, LAT + ROPE), jnp.float32), -4.0, 4.0)
    latent_part = (jnp.arange(LAT + ROPE) < LAT).astype(jnp.float32)
    offset = 0.6 * jnp.clip(jax.random.normal(second_key, (SLOTS, 1, LAT + ROPE), jnp.float32), -4.0, 4.0) * latent_part
    return (leading, offset)


def draw_counts(key, part):
    return shared_counts(key)


def draw_lengths(key, part):
    counts = shared_counts(key)
    key = jax.random.fold_in(key, 13)
    first_key, second_key = jax.random.split(key, 2)
    lengths = jax.random.randint(first_key, (SLOTS,), 2, CTX + 1)
    picks = jax.random.randint(second_key, (OWNERS,), 0, 65536) % counts
    longest = jnp.arange(OWNERS, dtype=jnp.int32) * ROWS + picks
    return lengths.at[longest].set(CTX)


def draw_cache(key, part):
    leading, offset = shared_keys(key)
    key = jax.random.fold_in(key, 17)
    first_key = jax.random.fold_in(key, 0)
    noise = jnp.clip(jax.random.normal(first_key, (SLOTS, CTX, LAT + ROPE), jnp.float32), -4.0, 4.0)
    noise = jnp.concatenate([leading, noise[:, 2:]], axis=1)
    return (noise + offset).astype(jnp.bfloat16)


def draw_query(key, part):
    key = jax.random.fold_in(key, 19)
    first_key = jax.random.fold_in(key, 0)
    drawn = jnp.clip(jax.random.normal(first_key, (SLOTS, H, LAT + ROPE), jnp.float32), -4.0, 4.0)
    return drawn.astype(jnp.bfloat16)


def draw_layer_input(key, part):
    key = jax.random.fold_in(key, 23)
    first_key, second_key = jax.random.split(key, 2)
    base = jnp.clip(jax.random.normal(first_key, (SLOTS, D), jnp.float32), -4.0, 4.0)
    scales = jnp.exp(jax.random.uniform(second_key, (SLOTS, 1), jnp.float32, math.log(0.3), math.log(3.0)))
    return (base * scales).astype(jnp.bfloat16)


def levels(stream_key, extent, cuts, smallest, largest):
    loudness = 1.0
    for dim, blocks in cuts:
        draws = jax.random.uniform(jax.random.fold_in(jax.random.fold_in(stream_key, 6), dim), (blocks,), jnp.float32, smallest / len(cuts), largest / len(cuts))
        loudness = loudness * jnp.repeat(jnp.exp(draws), extent[dim] // blocks).reshape((-1,) + (1,) * (len(extent) - 1 - dim))
    return loudness


def scatter_about(key, dims, spread, reach, cuts=(), kind=jnp.bfloat16):
    values = jax.random.normal(key, dims, jnp.float32) * spread
    if len(cuts) > 0:
        values = levels(key, dims, cuts, -0.22, 0.18) * values
    return jnp.clip(values, min=-reach, max=reach).astype(kind)


def setup_inputs(seed: int = 0) -> dict:
    arg_keys = jax.random.split(jax.random.key(seed), 12)
    return {
        "layer_input": draw_layer_input(jax.random.fold_in(arg_keys[11], 71), 0),
        "query": draw_query(jax.random.fold_in(arg_keys[11], 71), 0),
        "cache": draw_cache(jax.random.fold_in(arg_keys[11], 71), 0),
        "lengths": draw_lengths(jax.random.fold_in(arg_keys[11], 71), 0),
        "counts": draw_counts(jax.random.fold_in(arg_keys[11], 71), 0),
        "value_weight": scatter_about(arg_keys[5], (H, LAT, HEAD), LAT ** -0.5, 0.25, ((0, 32),)),
        "output_weight": scatter_about(arg_keys[6], (H * HEAD, D), (H * HEAD) ** -0.5, 0.0625, ((0, 32),)),
        "norm_gain": jnp.clip(1.0 + 0.18 * jax.random.normal(arg_keys[7], (D,), jnp.float32), 0.1, 1.9),
        "gate_weight": scatter_about(arg_keys[8], (D, FF), D ** -0.5, 0.0625, ((1, 32),)),
        "up_weight": scatter_about(arg_keys[9], (D, FF), D ** -0.5, 0.0625, ((1, 32),)),
        "down_weight": scatter_about(arg_keys[10], (FF, D), FF ** -0.5, 0.0625, ((0, 32), (1, 4))),
    }


score_scale = 1.0 / 192.0 ** 0.5
norm_eps = 1e-06

def attend_one(items):
    question, stored, valid = items
    positions = jnp.arange(CTX, dtype=jnp.int32)
    visible = positions[None, :] < valid
    scores = jnp.einsum('hc,tc->ht', question.astype(jnp.float32), stored.astype(jnp.float32)) * score_scale
    scores = jnp.where(visible, scores, jnp.float32(-1e+30))
    peak = lax.optimization_barrier(jnp.max(scores, axis=1, keepdims=True))
    raised = jnp.where(visible, jnp.exp(scores - peak), jnp.float32(0.0))
    attention = (raised / lax.optimization_barrier(jnp.sum(raised, axis=1, keepdims=True))).astype(jnp.bfloat16)
    latent = jnp.einsum('ht,ta->ha', attention.astype(jnp.float32), stored[:, :LAT].astype(jnp.float32))
    return latent.astype(jnp.bfloat16)

def normalize(residual, norm_gain):
    wide = residual.astype(jnp.float32)
    square_mean = lax.optimization_barrier(jnp.mean(wide * wide, axis=1, keepdims=True))
    return (wide * lax.rsqrt(square_mean + norm_eps) * norm_gain[None, :]).astype(jnp.bfloat16)

def reference(layer_input, query, cache, lengths, counts, value_weight, output_weight, norm_gain, gate_weight, up_weight, down_weight):
    latent = lax.map(attend_one, (query, cache, lengths))
    values = jnp.einsum('rha,had->rhd', latent.astype(jnp.float32), value_weight.astype(jnp.float32)).astype(jnp.bfloat16)
    attended = jnp.dot(values.reshape(values.shape[0], H * HEAD), output_weight, preferred_element_type=jnp.float32)
    residual = (layer_input.astype(jnp.float32) + attended).astype(jnp.bfloat16)
    normed = normalize(residual, norm_gain)
    gate = jnp.dot(normed, gate_weight, preferred_element_type=jnp.float32)
    upward = jnp.dot(normed, up_weight, preferred_element_type=jnp.float32)
    inner = (jax.nn.silu(gate) * upward).astype(jnp.bfloat16)
    feed = jnp.dot(inner, down_weight, preferred_element_type=jnp.float32)
    slot_index = jnp.arange(SLOTS, dtype=jnp.int32)
    live = slot_index % ROWS < counts[slot_index // ROWS]
    mixed = residual.astype(jnp.float32) + feed
    return jnp.where(live[:, None], mixed, jnp.float32(0.0)).astype(jnp.bfloat16)
```

```python
import jax
import jax.numpy as jnp
from jax import lax
from jax.sharding import PartitionSpec as P

score_scale = 1.0 / 192.0**0.5
norm_eps = 1e-06


def core_swap(x, width):
    return lax.ppermute(x, "tp", [(i, i ^ 1) for i in range(width)])


def between_chips(x, width):
    groups = [[2 * chip + core for chip in range(width // 2)] for core in range(2)]
    return lax.all_to_all(x, "tp", 0, 0, tiled=True, axis_index_groups=groups)


def attend(query, cache, lengths, latent_width):
    positions = jnp.arange(cache.shape[1], dtype=jnp.int32)
    visible = positions[None, None, :] < lengths[:, None, None]
    scores = (
        jnp.einsum("rhc,rtc->rht", query, cache, preferred_element_type=jnp.float32) * score_scale
    )
    scores = jnp.where(visible, scores, jnp.float32(-1e30))
    peak = jnp.max(scores, axis=2, keepdims=True)
    raised = jnp.where(visible, jnp.exp(scores - peak), jnp.float32(0.0))
    attention = (raised / jnp.sum(raised, axis=2, keepdims=True)).astype(jnp.bfloat16)
    return jnp.einsum(
        "rht,rta->rha", attention, cache[:, :, :latent_width], preferred_element_type=jnp.float32
    ).astype(jnp.bfloat16)


def on_device(
    layer_input,
    query,
    cache,
    lengths,
    counts,
    value_weight,
    output_weight,
    norm_gain,
    gate_weight,
    up_weight,
    down_weight,
    width,
):
    slots, model = layer_input.shape
    half = model // 2
    chips = width // 2
    heads_here, latent_width, head = value_weight.shape
    heads = 2 * heads_here
    chip_slots = 2 * slots
    rows = chips * chip_slots
    core = lax.axis_index("tp") % 2
    upper = core == 1

    down_parts = lax.all_gather(down_weight, "dp", axis=0, tiled=False)
    value_other = core_swap(value_weight, width)
    output_mine = lax.dynamic_slice_in_dim(output_weight, core * half, half, 1)
    output_other = core_swap(
        lax.dynamic_slice_in_dim(output_weight, (1 - core) * half, half, 1), width
    )
    input_mine = lax.dynamic_slice_in_dim(layer_input, core * half, half, 1)
    input_other = core_swap(
        lax.dynamic_slice_in_dim(layer_input, (1 - core) * half, half, 1), width
    )

    latent = attend(query, cache, lengths, latent_width)
    leaving = latent.reshape(slots, chips, heads, latent_width).transpose(1, 2, 0, 3)
    arrived = between_chips(leaving, width)
    arrived_other = core_swap(arrived, width)

    lower_heads = jnp.stack(
        [
            jnp.where(upper, arrived[:, heads_here:], arrived[:, :heads_here]),
            jnp.where(upper, arrived_other[:, heads_here:], arrived_other[:, :heads_here]),
        ],
        axis=1,
    )
    upper_heads = jnp.stack(
        [
            jnp.where(upper, arrived[:, :heads_here], arrived[:, heads_here:]),
            jnp.where(upper, arrived_other[:, :heads_here], arrived_other[:, heads_here:]),
        ],
        axis=1,
    )

    def project(part, weight):
        out = jnp.einsum("pohra,had->porhd", part, weight, preferred_element_type=jnp.float32)
        return out.astype(jnp.bfloat16).reshape(rows, heads_here * head)

    values_mine = project(lower_heads, value_weight)
    values_other = project(upper_heads, value_other)
    attended_part = jnp.dot(
        values_mine, output_mine, preferred_element_type=jnp.float32
    ) + jnp.dot(values_other, output_other, preferred_element_type=jnp.float32)
    attended_part = attended_part.astype(jnp.bfloat16).reshape(chips, chip_slots, half)
    attended = jnp.sum(between_chips(attended_part, width).astype(jnp.float32), axis=0)
    residual_mine = (input_mine.astype(jnp.float32) + attended[:slots]).astype(jnp.bfloat16)
    residual_other = (input_other.astype(jnp.float32) + attended[slots:]).astype(jnp.bfloat16)
    residual = jnp.where(
        upper,
        jnp.concatenate([residual_other, residual_mine], axis=0),
        jnp.concatenate([residual_mine, residual_other], axis=0),
    )

    gathered = between_chips(
        jnp.broadcast_to(residual[None], (chips, chip_slots, half)), width
    ).reshape(rows, half)
    gathered_other = core_swap(gathered, width)
    wide_mine = gathered.astype(jnp.float32)
    wide_other = gathered_other.astype(jnp.float32)
    square_mean = (
        jnp.sum(wide_mine * wide_mine, axis=1, keepdims=True)
        + jnp.sum(wide_other * wide_other, axis=1, keepdims=True)
    ) / model
    scale = lax.rsqrt(square_mean + norm_eps)
    wide = jnp.concatenate(
        [
            jnp.where(upper, wide_other, wide_mine),
            jnp.where(upper, wide_mine, wide_other),
        ],
        axis=1,
    )
    normed = (wide * scale * norm_gain[None, :]).astype(jnp.bfloat16)
    gate = jnp.dot(normed, gate_weight, preferred_element_type=jnp.float32)
    upward = jnp.dot(normed, up_weight, preferred_element_type=jnp.float32)
    inner = (jax.nn.silu(gate) * upward).astype(jnp.bfloat16)
    inner_other = core_swap(inner, width)

    cut = down_parts.shape[0] // 2
    down_mine = lax.dynamic_slice_in_dim(down_parts, core * cut, cut, 0)
    down_other = core_swap(
        lax.dynamic_slice_in_dim(down_parts, (1 - core) * cut, cut, 0), width
    )
    feed_part = jnp.concatenate(
        [
            jnp.dot(inner, down_mine[s], preferred_element_type=jnp.float32)
            + jnp.dot(inner_other, down_other[s], preferred_element_type=jnp.float32)
            for s in range(cut)
        ],
        axis=1,
    )
    feed_part = feed_part.astype(jnp.bfloat16).reshape(chips, chip_slots, half)
    feed = jnp.sum(between_chips(feed_part, width).astype(jnp.float32), axis=0)
    mixed = (residual.astype(jnp.float32) + feed).astype(jnp.bfloat16)
    kept = lax.dynamic_slice_in_dim(mixed, core * slots, slots, 0)
    got = core_swap(lax.dynamic_slice_in_dim(mixed, (1 - core) * slots, slots, 0), width)
    out = jnp.where(
        upper,
        jnp.concatenate([got, kept], axis=1),
        jnp.concatenate([kept, got], axis=1),
    )
    live = jnp.arange(slots, dtype=jnp.int32) < counts[0]
    return jnp.where(live[:, None], out, jnp.bfloat16(0.0))


def solution(mesh):
    placed = (
        P(("dp", "tp"), None),
        P(("dp", "tp"), None, None),
        P(("dp", "tp"), None, None),
        P(("dp", "tp")),
        P(("dp", "tp")),
        P("tp", None, None),
        P("tp", None),
        P(),
        P(None, "tp"),
        P(None, "tp"),
        P("tp", "dp"),
    )
    width = mesh.shape["tp"]
    return jax.shard_map(
        lambda *args: on_device(*args, width),
        mesh=mesh,
        in_specs=placed,
        out_specs=P(("dp", "tp"), None),
        check_vma=False,
    )
```

```python
import math

import jax
import jax.numpy as jnp
from jax import lax
from jax.sharding import PartitionSpec as P

score_scale = 1.0 / 192.0**0.5
norm_eps = 1e-06


def core_swap(x, width):
    return lax.ppermute(x, "tp", [(i, i ^ 1) for i in range(width)])


def between_chips(x, width):
    groups = [[2 * chip + core for chip in range(width // 2)] for core in range(2)]
    return lax.all_to_all(x, "tp", 0, 0, tiled=True, axis_index_groups=groups)


def ring(parts, axis, side, sign):
    out = [parts[0]]
    for k in range(1, side):
        pairs = []
        for y in range(side):
            for x in range(side):
                at = ((y + sign * k) % side, x) if axis == 0 else (y, (x + sign * k) % side)
                for core in range(2):
                    pairs.append(((y * side + x) * 2 + core, (at[0] * side + at[1]) * 2 + core))
        out.append(lax.ppermute(parts[k], "tp", pairs))
    return out


def down_pieces(down_weight, width):
    out = []
    for k in range(4):
        pairs = []
        for layer in range(4):
            for place in range(width):
                chip, core = divmod(place, 2)
                cut, row_core = (layer >> 1) ^ (k >> 1), (layer & 1) ^ (k & 1)
                pairs.append(((2 * core + cut) * width + 2 * chip + row_core, layer * width + place))
        out.append(lax.ppermute(down_weight, ("dp", "tp"), pairs))
    return out


def total(parts):
    wide = parts[0].astype(jnp.float32)
    for part in parts[1:]:
        wide = wide + part.astype(jnp.float32)
    return wide


def attend(query, cache, lengths, latent_width):
    positions = jnp.arange(cache.shape[1], dtype=jnp.int32)
    visible = positions[None, None, :] < lengths[:, None, None]
    scores = (
        jnp.einsum("rhc,rtc->rht", query, cache, preferred_element_type=jnp.float32) * score_scale
    )
    scores = jnp.where(visible, scores, jnp.float32(-1e30))
    peak = jnp.max(scores, axis=2, keepdims=True)
    raised = jnp.where(visible, jnp.exp(scores - peak), jnp.float32(0.0))
    attention = (raised / jnp.sum(raised, axis=2, keepdims=True)).astype(jnp.bfloat16)
    return jnp.einsum(
        "rht,rta->rha", attention, cache[:, :, :latent_width], preferred_element_type=jnp.float32
    ).astype(jnp.bfloat16)


def on_device(
    layer_input,
    query,
    cache,
    lengths,
    counts,
    value_weight,
    output_weight,
    norm_gain,
    gate_weight,
    up_weight,
    down_weight,
    width,
):
    slots, model = layer_input.shape
    half = model // 2
    chips = width // 2
    side = math.isqrt(chips)
    heads_here, latent_width, head = value_weight.shape
    heads = 2 * heads_here
    chip_slots = 2 * slots
    rows = chips * chip_slots
    line = side * chip_slots
    place = lax.axis_index("tp")
    core = place % 2
    upper = core == 1
    at_y = place // (2 * side)
    at_x = (place // 2) % side
    layer = lax.axis_index("dp")

    pieces = down_pieces(down_weight, width)
    value_other = core_swap(value_weight, width)
    output_mine = lax.dynamic_slice_in_dim(output_weight, core * half, half, 1)
    output_other = core_swap(
        lax.dynamic_slice_in_dim(output_weight, (1 - core) * half, half, 1), width
    )
    input_mine = lax.dynamic_slice_in_dim(layer_input, core * half, half, 1)
    input_other = core_swap(
        lax.dynamic_slice_in_dim(layer_input, (1 - core) * half, half, 1), width
    )
    input_chip = jnp.where(
        upper,
        jnp.concatenate([input_other, input_mine], axis=0),
        jnp.concatenate([input_mine, input_other], axis=0),
    ).astype(jnp.float32)

    latent = attend(query, cache, lengths, latent_width)
    leaving = latent.reshape(slots, chips, heads, latent_width).transpose(1, 2, 0, 3)
    arrived = between_chips(leaving, width)
    arrived_other = core_swap(arrived, width)

    first = jnp.where(upper, arrived_other, arrived)
    second = jnp.where(upper, arrived, arrived_other)
    both = jnp.stack([first, second], axis=1)
    heads_mine = jnp.where(upper, both[:, :, heads_here:], both[:, :, :heads_here])
    heads_other = jnp.where(upper, both[:, :, :heads_here], both[:, :, heads_here:])

    def project(part, weight):
        out = jnp.einsum("pohra,had->porhd", part, weight, preferred_element_type=jnp.float32)
        flat = out.astype(jnp.bfloat16).reshape(rows, heads_here * head)
        return lax.dynamic_slice_in_dim(jnp.concatenate([flat, flat]), at_y * line, rows, 0)

    values_mine = project(heads_mine, value_weight)
    values_other = project(heads_other, value_other)
    attended_part = jnp.dot(
        values_mine, output_mine, preferred_element_type=jnp.float32
    ) + jnp.dot(values_other, output_other, preferred_element_type=jnp.float32)
    attended_part = attended_part.astype(jnp.bfloat16).reshape(side, line, half)

    summed = total(ring([attended_part[k] for k in range(side)], 0, side, 1))
    own_rows = (jnp.arange(side) == at_x)[:, None, None]
    summed = summed.reshape(side, chip_slots, half) + jnp.where(own_rows, input_chip[None], 0.0)
    summed = summed.astype(jnp.bfloat16).reshape(line, half)
    residual_line = total(ring([summed] * side, 1, side, 1)).astype(jnp.bfloat16)
    residual_mine = ring([residual_line] * side, 0, side, -1)
    residual_other = [core_swap(part, width) for part in residual_mine]
    wide_mine = jnp.concatenate(residual_mine, axis=0).astype(jnp.float32)
    wide_other = jnp.concatenate(residual_other, axis=0).astype(jnp.float32)
    square_mean = (
        jnp.sum(wide_mine * wide_mine, axis=1, keepdims=True)
        + jnp.sum(wide_other * wide_other, axis=1, keepdims=True)
    ) / model
    scale = lax.rsqrt(square_mean + norm_eps)
    wide = jnp.concatenate(
        [
            jnp.where(upper, wide_other, wide_mine),
            jnp.where(upper, wide_mine, wide_other),
        ],
        axis=1,
    )
    normed = (wide * scale * norm_gain[None, :]).astype(jnp.bfloat16)
    gate = jnp.dot(normed, gate_weight, preferred_element_type=jnp.float32)
    upward = jnp.dot(normed, up_weight, preferred_element_type=jnp.float32)
    inner = (jax.nn.silu(gate) * upward).astype(jnp.bfloat16)
    inner_other = core_swap(inner, width)

    same = core == layer % 2
    inner_even = jnp.where(same, inner, inner_other)
    inner_odd = jnp.where(same, inner_other, inner)
    feed_part = jnp.concatenate(
        [
            jnp.dot(inner_even, pieces[2 * s], preferred_element_type=jnp.float32)
            + jnp.dot(inner_odd, pieces[2 * s + 1], preferred_element_type=jnp.float32)
            for s in range(2)
        ],
        axis=1,
    )
    feed_part = feed_part.astype(jnp.bfloat16).reshape(side, line, half)
    feed_line = total(ring([feed_part[k] for k in range(side)], 0, side, 1)).astype(jnp.bfloat16)
    feed = total(
        ring(
            [
                lax.dynamic_slice_in_dim(
                    feed_line, (at_x + k) % side * chip_slots, chip_slots, 0
                )
                for k in range(side)
            ],
            1,
            side,
            1,
        )
    )
    cut = half // 2
    feed = jnp.where(
        layer // 2 == 1, jnp.concatenate([feed[:, cut:], feed[:, :cut]], axis=1), feed
    )
    residual = lax.dynamic_slice_in_dim(residual_line, at_x * chip_slots, chip_slots, 0)
    mixed = (residual.astype(jnp.float32) + feed).astype(jnp.bfloat16)
    kept = lax.dynamic_slice_in_dim(mixed, core * slots, slots, 0)
    got = core_swap(lax.dynamic_slice_in_dim(mixed, (1 - core) * slots, slots, 0), width)
    out = jnp.where(
        upper,
        jnp.concatenate([got, kept], axis=1),
        jnp.concatenate([kept, got], axis=1),
    )
    live = jnp.arange(slots, dtype=jnp.int32) < counts[0]
    return jnp.where(live[:, None], out, jnp.bfloat16(0.0))


def solution(mesh):
    placed = (
        P(("dp", "tp"), None),
        P(("dp", "tp"), None, None),
        P(("dp", "tp"), None, None),
        P(("dp", "tp")),
        P(("dp", "tp")),
        P("tp", None, None),
        P("tp", None),
        P(),
        P(None, "tp"),
        P(None, "tp"),
        P("tp", "dp"),
    )
    width = mesh.shape["tp"]
    return jax.shard_map(
        lambda *args: on_device(*args, width),
        mesh=mesh,
        in_specs=placed,
        out_specs=P(("dp", "tp"), None),
        check_vma=False,
    )
```

```python
import jax
import jax.numpy as jnp
from jax import lax
from jax.experimental import pallas as pl
from jax.experimental.pallas import tpu as pltpu
from jax.sharding import PartitionSpec as P

score_scale = 1.0 / 192.0**0.5
norm_eps = 1e-06


def core_swap(x, width):
    return lax.ppermute(x, "tp", [(i, i ^ 1) for i in range(width)])


def between_chips(x, width):
    groups = [[2 * chip + core for chip in range(width // 2)] for core in range(2)]
    return lax.all_to_all(x, "tp", 0, 0, tiled=True, axis_index_groups=groups)


def down_pieces(down_weight, width):
    out = []
    for k in range(4):
        pairs = []
        for layer in range(4):
            for place in range(width):
                chip, core = divmod(place, 2)
                cut, row_core = (layer >> 1) ^ (k >> 1), (layer & 1) ^ (k & 1)
                pairs.append(((2 * core + cut) * width + 2 * chip + row_core, layer * width + place))
        out.append(lax.ppermute(down_weight, ("dp", "tp"), pairs))
    return out


def attend(query, cache, lengths, counts, latent_width, chips):
    slots, heads, wide = query.shape
    ctx = cache.shape[1]
    group = heads // chips
    rows = slots * heads

    def kernel(lengths_ref, counts_ref, q_ref, cache_ref, out_ref, latent_ref):
        slot = pl.program_id(0)
        at = pl.ds(pl.multiple_of(slot * heads, heads), heads)

        @pl.when(slot < counts_ref[0])
        def _():
            scores = jnp.dot(q_ref[0], cache_ref[0], preferred_element_type=jnp.float32)
            place = lax.broadcasted_iota(jnp.int32, scores.shape, 1)
            scores = jnp.where(place < lengths_ref[slot], scores * score_scale, -1e30)
            raised = jnp.exp(scores - jnp.max(scores, axis=1, keepdims=True))
            latent = lax.dot_general(
                raised.astype(jnp.bfloat16),
                cache_ref[0, :latent_width, :],
                (((1,), (1,)), ((), ())),
                preferred_element_type=jnp.float32,
            )
            latent = latent / jnp.sum(raised, axis=1, keepdims=True)
            latent_ref[at, :] = latent.astype(jnp.bfloat16)

        @pl.when(slot >= counts_ref[0])
        def _():
            latent_ref[at, :] = jnp.zeros((heads, latent_width), jnp.bfloat16)

        @pl.when(slot == slots - 1)
        def _():
            to = lax.broadcasted_iota(jnp.int32, (rows, rows), 0)
            source = to // group % slots * heads + to // (slots * group) * group + to % group
            pick = source == lax.broadcasted_iota(jnp.int32, (rows, rows), 1)
            out_ref[...] = jnp.dot(
                pick.astype(jnp.bfloat16), latent_ref[...], preferred_element_type=jnp.float32
            ).astype(jnp.bfloat16)

    def last(slot, lengths_ref, counts_ref):
        return (jnp.minimum(slot, counts_ref[0] - 1), 0, 0)

    out = pl.pallas_call(
        kernel,
        grid_spec=pltpu.PrefetchScalarGridSpec(
            num_scalar_prefetch=2,
            grid=(slots,),
            in_specs=[pl.BlockSpec((1, heads, wide), last), pl.BlockSpec((1, wide, ctx), last)],
            out_specs=pl.BlockSpec((rows, latent_width), lambda slot, *refs: (0, 0)),
            scratch_shapes=[pltpu.VMEM((rows, latent_width), jnp.bfloat16)],
        ),
        out_shape=jax.ShapeDtypeStruct((rows, latent_width), jnp.bfloat16),
        compiler_params=pltpu.CompilerParams(vmem_limit_bytes=32 * 2**20),
        cost_estimate=pl.CostEstimate(
            flops=2 * rows * ctx * (wide + latent_width),
            bytes_accessed=2 * cache.size,
            transcendentals=rows * ctx,
        ),
    )(lengths, counts, query, jnp.swapaxes(cache, 1, 2))
    return out.reshape(chips, slots * group, latent_width)


def project(mine, other, value_mine, value_other, output_mine, output_other, core, slots):
    chips, pairs, latent_width = mine.shape
    heads_here, _, head = value_mine.shape
    heads = 2 * heads_here
    depth, model = output_mine.shape
    half = model // 2
    block = 512
    rows = 2 * chips * slots
    lines = chips * pairs

    def kernel(core_ref, mine_ref, other_ref, vm_ref, vo_ref, om_ref, oo_ref, out_ref, value_ref):
        core = core_ref[0]

        @pl.when(pl.program_id(0) == 0)
        def _():
            to = lax.broadcasted_iota(jnp.int32, (rows, lines), 0)
            line = lax.broadcasted_iota(jnp.int32, (rows, lines), 1)
            chip, row_core, slot = to // (2 * slots), to // slots % 2, to % slots
            own = row_core == core
            source = chip * pairs + slot * heads
            for index in range(heads):
                side, weight_ref = (core, vm_ref) if index < heads_here else (1 - core, vo_ref)
                place = index % heads_here
                hit = line == source + side * heads_here + place
                rows_mine = jnp.where(hit & own, 1.0, 0.0).astype(jnp.bfloat16)
                rows_other = jnp.where(hit & ~own, 1.0, 0.0).astype(jnp.bfloat16)
                picked = jnp.dot(
                    rows_mine, mine_ref[...], preferred_element_type=jnp.float32
                ) + jnp.dot(rows_other, other_ref[...], preferred_element_type=jnp.float32)
                value_ref[:, index * head : (index + 1) * head] = jnp.dot(
                    picked.astype(jnp.bfloat16),
                    weight_ref[place],
                    preferred_element_type=jnp.float32,
                ).astype(jnp.bfloat16)

        out_ref[...] = (
            jnp.dot(value_ref[:, :depth], om_ref[...], preferred_element_type=jnp.float32)
            + jnp.dot(value_ref[:, depth:], oo_ref[...], preferred_element_type=jnp.float32)
        ).astype(jnp.bfloat16)

    steps = half // block
    whole = lambda *shape: pl.BlockSpec(shape, lambda j, core_ref: (0,) * len(shape))
    weight = pl.BlockSpec((depth, block), lambda j, core_ref: (0, core_ref[0] * steps + j))
    return pl.pallas_call(
        kernel,
        grid_spec=pltpu.PrefetchScalarGridSpec(
            num_scalar_prefetch=1,
            grid=(steps,),
            in_specs=[
                whole(lines, latent_width),
                whole(lines, latent_width),
                whole(heads_here, latent_width, head),
                whole(heads_here, latent_width, head),
                weight,
                weight,
            ],
            out_specs=pl.BlockSpec((rows, block), lambda j, core_ref: (0, j)),
            scratch_shapes=[pltpu.VMEM((rows, 2 * depth), jnp.bfloat16)],
        ),
        out_shape=jax.ShapeDtypeStruct((rows, half), jnp.bfloat16),
        compiler_params=pltpu.CompilerParams(vmem_limit_bytes=16 * 2**20),
        cost_estimate=pl.CostEstimate(
            flops=4 * rows * depth * half, bytes_accessed=4 * depth * half, transcendentals=0
        ),
    )(
        core.reshape(1),
        mine.reshape(lines, latent_width),
        other.reshape(lines, latent_width),
        value_mine,
        value_other,
        output_mine,
        output_other,
    )


def gated(residual, gain, gate_weight, up_weight, side, before):
    rows, half = residual.shape
    units = gate_weight.shape[1]
    block = 512
    steps = half // block
    finish = before is not None

    def kernel(side_ref, res_ref, gain_ref, gate_ref, up_ref, *refs):
        j = pl.program_id(0)
        if finish:
            gate_before, up_before, square_before, out_ref, gate_sum, up_sum, square_sum = refs
        else:
            gate_sum, up_sum, square_sum = refs

        @pl.when(j == 0)
        def _():
            if finish:
                gate_sum[...] = gate_before[...]
                up_sum[...] = up_before[...]
                square_sum[...] = square_before[...]
            else:
                gate_sum[...] = jnp.zeros_like(gate_sum)
                up_sum[...] = jnp.zeros_like(up_sum)
                square_sum[...] = jnp.zeros_like(square_sum)

        wide = res_ref[...].astype(jnp.float32)
        scaled = (wide * gain_ref[...]).astype(jnp.bfloat16)
        squares = wide * wide
        part = squares[:, :128]
        for k in range(1, block // 128):
            part = part + squares[:, k * 128 : (k + 1) * 128]
        square_sum[...] += part
        across = (((1,), (1,)), ((), ()))
        gate_sum[...] += lax.dot_general(
            scaled, gate_ref[...], across, preferred_element_type=jnp.float32
        )
        up_sum[...] += lax.dot_general(
            scaled, up_ref[...], across, preferred_element_type=jnp.float32
        )

        if finish:

            @pl.when(j == steps - 1)
            def _():
                mean = jnp.sum(square_sum[...], axis=1, keepdims=True) / (2 * half)
                scale = lax.rsqrt(mean + norm_eps)
                gate = gate_sum[...] * scale
                out_ref[...] = (gate / (1.0 + jnp.exp(-gate)) * (up_sum[...] * scale)).astype(
                    jnp.bfloat16
                )

    sums = [
        jax.ShapeDtypeStruct((rows, units), jnp.float32),
        jax.ShapeDtypeStruct((rows, units), jnp.float32),
        jax.ShapeDtypeStruct((rows, 128), jnp.float32),
    ]
    whole = [pl.BlockSpec(leaf.shape, lambda j, side_ref: (0, 0)) for leaf in sums]
    feature = lambda lines: pl.BlockSpec(
        (lines, block), lambda j, side_ref: (0, side_ref[0] * steps + j)
    )
    in_specs = [
        pl.BlockSpec((rows, block), lambda j, side_ref: (0, j)),
        feature(1),
        feature(units),
        feature(units),
    ]
    operands = [residual, gain[None, :], gate_weight.T, up_weight.T]
    return pl.pallas_call(
        kernel,
        grid_spec=pltpu.PrefetchScalarGridSpec(
            num_scalar_prefetch=1,
            grid=(steps,),
            in_specs=in_specs + (whole if finish else []),
            out_specs=whole[0] if finish else whole,
            scratch_shapes=[pltpu.VMEM(leaf.shape, leaf.dtype) for leaf in sums] if finish else [],
        ),
        out_shape=jax.ShapeDtypeStruct((rows, units), jnp.bfloat16) if finish else sums,
        compiler_params=pltpu.CompilerParams(vmem_limit_bytes=16 * 2**20),
        cost_estimate=pl.CostEstimate(
            flops=4 * rows * half * units, bytes_accessed=4 * half * units, transcendentals=0
        ),
    )(side.reshape(1), *operands, *(before or []))


def feed_forward(even, odd, pieces):
    rows, units = even.shape
    cut = pieces[0].shape[1]
    block = cut // 2

    def kernel(even_ref, odd_ref, a_ref, b_ref, c_ref, d_ref, out_ref):
        def write(first_ref, second_ref):
            out_ref[...] = (
                jnp.dot(even_ref[...], first_ref[...], preferred_element_type=jnp.float32)
                + jnp.dot(odd_ref[...], second_ref[...], preferred_element_type=jnp.float32)
            ).astype(jnp.bfloat16)

        @pl.when(pl.program_id(0) < 2)
        def _():
            write(a_ref, b_ref)

        @pl.when(pl.program_id(0) >= 2)
        def _():
            write(c_ref, d_ref)

    whole = pl.BlockSpec((rows, units), lambda j: (0, 0))
    early = pl.BlockSpec((units, block), lambda j: (0, jnp.minimum(j, 1)))
    late = pl.BlockSpec((units, block), lambda j: (0, jnp.maximum(j - 2, 0)))
    return pl.pallas_call(
        kernel,
        grid=(4,),
        in_specs=[whole, whole, early, early, late, late],
        out_specs=pl.BlockSpec((rows, block), lambda j: (0, j)),
        out_shape=jax.ShapeDtypeStruct((rows, 2 * cut), jnp.bfloat16),
        compiler_params=pltpu.CompilerParams(vmem_limit_bytes=16 * 2**20),
        cost_estimate=pl.CostEstimate(
            flops=8 * rows * units * cut, bytes_accessed=8 * units * cut, transcendentals=0
        ),
    )(even, odd, *pieces)


def on_device(
    layer_input,
    query,
    cache,
    lengths,
    counts,
    value_weight,
    output_weight,
    norm_gain,
    gate_weight,
    up_weight,
    down_weight,
    width,
):
    slots, model = layer_input.shape
    half = model // 2
    chips = width // 2

    heads_here, latent_width, head = value_weight.shape
    chip_slots = 2 * slots
    rows = chips * chip_slots
    place = lax.axis_index("tp")
    core = place % 2
    upper = core == 1
    layer = lax.axis_index("dp")

    pieces = down_pieces(down_weight, width)
    value_other = core_swap(value_weight, width)
    output_other = core_swap(output_weight, width)
    input_mine = lax.dynamic_slice_in_dim(layer_input, core * half, half, 1)
    input_other = core_swap(
        lax.dynamic_slice_in_dim(layer_input, (1 - core) * half, half, 1), width
    )
    input_chip = jnp.where(
        upper,
        jnp.concatenate([input_other, input_mine], axis=0),
        jnp.concatenate([input_mine, input_other], axis=0),
    ).astype(jnp.float32)

    latent = attend(query, cache, lengths, counts, latent_width, chips)
    arrived = between_chips(latent, width)
    arrived, pieces[0], pieces[1] = lax.optimization_barrier((arrived, pieces[0], pieces[1]))
    arrived_other = core_swap(arrived, width)
    attended_part = project(
        arrived, arrived_other, value_weight, value_other, output_weight, output_other, core, slots
    )
    attended_parts = between_chips(attended_part.reshape(chips, chip_slots, half), width)
    attended_parts, pieces[2], pieces[3] = lax.optimization_barrier(
        (attended_parts, pieces[2], pieces[3])
    )
    attended = jnp.sum(attended_parts.astype(jnp.float32), axis=0)
    residual = (input_chip + attended).astype(jnp.bfloat16)
    gathered = between_chips(
        jnp.broadcast_to(residual[None], (chips, chip_slots, half)), width
    ).reshape(rows, half)
    gathered_other = core_swap(gathered, width)
    sums = gated(gathered, norm_gain, gate_weight, up_weight, core, None)
    inner = gated(gathered_other, norm_gain, gate_weight, up_weight, 1 - core, sums)
    inner_other = core_swap(inner, width)

    same = core == layer % 2
    feed_part = feed_forward(
        jnp.where(same, inner, inner_other), jnp.where(same, inner_other, inner), pieces
    )
    feed_parts = between_chips(feed_part.reshape(chips, chip_slots, half), width)
    feed = jnp.sum(feed_parts.astype(jnp.float32), axis=0)
    cut = half // 2
    feed = jnp.where(
        layer // 2 == 1, jnp.concatenate([feed[:, cut:], feed[:, :cut]], axis=1), feed
    )
    mixed = (residual.astype(jnp.float32) + feed).astype(jnp.bfloat16)
    kept = lax.dynamic_slice_in_dim(mixed, core * slots, slots, 0)
    got = core_swap(lax.dynamic_slice_in_dim(mixed, (1 - core) * slots, slots, 0), width)
    out = jnp.where(
        upper,
        jnp.concatenate([got, kept], axis=1),
        jnp.concatenate([kept, got], axis=1),
    )
    live = jnp.arange(slots, dtype=jnp.int32) < counts[0]
    return jnp.where(live[:, None], out, jnp.bfloat16(0.0))


def solution(mesh):
    placed = (
        P(("dp", "tp"), None),
        P(("dp", "tp"), None, None),
        P(("dp", "tp"), None, None),
        P(("dp", "tp")),
        P(("dp", "tp")),
        P("tp", None, None),
        P("tp", None),
        P(),
        P(None, "tp"),
        P(None, "tp"),
        P("tp", "dp"),
    )
    width = mesh.shape["tp"]
    return jax.shard_map(
        lambda *args: on_device(*args, width),
        mesh=mesh,
        in_specs=placed,
        out_specs=P(("dp", "tp"), None),
        check_vma=False,
    )
```

```python
import math

import jax
import jax.numpy as jnp
from jax import lax
from jax.experimental import pallas as pl
from jax.experimental.pallas import tpu as pltpu
from jax.sharding import PartitionSpec as P

score_scale = 1.0 / 192.0**0.5
norm_eps = 1e-06


def core_swap(x, width):
    return lax.ppermute(x, "tp", [(i, i ^ 1) for i in range(width)])


def between_chips(x, width):
    groups = [[2 * chip + core for chip in range(width // 2)] for core in range(2)]
    return lax.all_to_all(x, "tp", 0, 0, tiled=True, axis_index_groups=groups)


def turn(parts, axis, side, sign):
    out = [parts[0]]
    for k in range(1, side):
        pairs = []
        for y in range(side):
            for x in range(side):
                for core in range(2):
                    if axis == core:
                        to = ((y + sign * k) % side) * side + x
                    else:
                        to = y * side + (x + sign * k) % side
                    pairs.append(((y * side + x) * 2 + core, to * 2 + core))
        out.append(lax.ppermute(parts[k], "tp", pairs))
    return out


def total(parts):
    wide = parts[0].astype(jnp.float32)
    for part in parts[1:]:
        wide = wide + part.astype(jnp.float32)
    return wide


def down_pieces(down_weight, width):
    out = []
    for k in range(4):
        pairs = []
        for layer in range(4):
            for place in range(width):
                chip, core = divmod(place, 2)
                cut, row_core = (layer >> 1) ^ (k >> 1), (layer & 1) ^ (k & 1)
                pairs.append(((2 * core + cut) * width + 2 * chip + row_core, layer * width + place))
        out.append(lax.ppermute(down_weight, ("dp", "tp"), pairs))
    return out


in_vmem = pl.BlockSpec(memory_space=pltpu.VMEM)
in_hbm = pl.BlockSpec(memory_space=pltpu.HBM)
in_smem = pl.BlockSpec(memory_space=pltpu.SMEM)
across = (((1,), (1,)), ((), ()))


def product(a, b):
    return jnp.dot(a, b, preferred_element_type=jnp.float32)


def one_hot(source, columns):
    hit = source == lax.broadcasted_iota(jnp.int32, (source.shape[0], columns), 1)
    return jnp.where(hit, 1.0, 0.0).astype(jnp.bfloat16)


def line_numbers(rows):
    return lax.broadcasted_iota(jnp.int32, (rows, 1), 0)


def budget(mib):
    return pltpu.CompilerParams(vmem_limit_bytes=mib * 2**20)


def attend(query, cache, lengths, counts, latent_width, chips):
    slots, heads, wide = query.shape
    ctx = cache.shape[1]
    group = heads // chips
    rows = slots * heads

    def kernel(lengths_ref, counts_ref, q_ref, cache_ref, out_ref, held_ref, sems):
        copies = [
            pltpu.make_async_copy(cache_ref.at[slot], held_ref.at[slot], sems.at[slot])
            for slot in range(slots)
        ]

        def score(slot):
            copies[slot].wait()
            place = lax.broadcasted_iota(jnp.int32, (heads, ctx), 1)
            found = product(q_ref[slot], held_ref[slot]) * score_scale
            return jnp.where(place < lengths_ref[slot], found, -1e30)

        def gather(slot, scores):
            raised = jnp.exp(scores - jnp.max(scores, axis=1, keepdims=True))
            latent = lax.dot_general(
                raised.astype(jnp.bfloat16),
                held_ref[slot, :latent_width],
                across,
                preferred_element_type=jnp.float32,
            )
            latent = latent / jnp.sum(raised, axis=1, keepdims=True)
            return jnp.where(slot < counts_ref[0], latent, 0.0).astype(jnp.bfloat16)

        copies[0].start()
        copies[1].start()
        latents = []
        scores = score(0)
        for slot in range(slots):
            if slot + 2 < slots:
                copies[slot + 2].start()
            following = score(slot + 1) if slot + 1 < slots else None
            latents.append(gather(slot, scores))
            scores = following
        to = line_numbers(rows)
        source = to // group % slots * heads + to // (slots * group) * group + to % group
        out_ref[...] = product(
            one_hot(source, rows), jnp.concatenate(latents, axis=0)
        ).astype(jnp.bfloat16)

    out = pl.pallas_call(
        kernel,
        in_specs=[in_smem, in_smem, in_vmem, in_hbm],
        out_specs=in_vmem,
        out_shape=jax.ShapeDtypeStruct((rows, latent_width), jnp.bfloat16),
        scratch_shapes=[
            pltpu.VMEM((slots, wide, ctx), jnp.bfloat16),
            pltpu.SemaphoreType.DMA((slots,)),
        ],
        compiler_params=budget(60),
        cost_estimate=pl.CostEstimate(
            flops=2 * rows * ctx * (wide + latent_width),
            bytes_accessed=2 * cache.size,
            transcendentals=rows * ctx,
        ),
    )(lengths, counts, query, jnp.swapaxes(cache, 1, 2))
    return out.reshape(chips, slots * group, latent_width)


def project(mine, other, value_mine, value_other, output_mine, output_other, spot, side, slots):
    chips, pairs, latent_width = mine.shape
    heads_here, _, head = value_mine.shape
    heads = 2 * heads_here
    depth, model = output_mine.shape
    half = model // 2
    rows = 2 * chips * slots
    line = rows // side
    lines = chips * pairs
    cuts = 4
    span = half // cuts

    def kernel(spot_ref, mine_ref, other_ref, vm_ref, vo_ref, om_ref, oo_ref, *refs):
        outs, (held_ref, sems) = refs[:side], refs[side:]
        core, first = spot_ref[0], spot_ref[1]
        copies = []
        for cut in range(cuts):
            for k, weight_ref in enumerate((om_ref, oo_ref)):
                start = pl.multiple_of(core * half + cut * span, 128)
                copies.append(
                    pltpu.make_async_copy(
                        weight_ref.at[:, pl.ds(start, span)],
                        held_ref.at[pl.ds(k * depth, depth), pl.ds(cut * span, span)],
                        sems.at[cut, k],
                    )
                )
                copies[-1].start()
        to = line_numbers(rows)
        along = (to // line + first) % side
        second = to // (2 * slots) % side
        chip = jnp.where(core == 0, along * side + second, second * side + along)
        from_other = (to // slots % 2 + core) % 2
        source = from_other * lines + chip * pairs + to % slots * heads
        latents = jnp.concatenate([mine_ref[...], other_ref[...]], axis=0)
        values = []
        for index in range(heads):
            owner, weight_ref = (core, vm_ref) if index < heads_here else (1 - core, vo_ref)
            place = index % heads_here
            pick = one_hot(source + owner * heads_here + place, 2 * lines)
            picked = product(pick, latents).astype(jnp.bfloat16)
            values.append(product(picked, weight_ref[place]).astype(jnp.bfloat16))
        values = jnp.concatenate(values, axis=1)
        for cut in range(cuts):
            copies[2 * cut].wait()
            copies[2 * cut + 1].wait()
            part = slice(cut * span, (cut + 1) * span)
            result = product(values, held_ref[:, part]).astype(jnp.bfloat16)
            for k in range(side):
                outs[k][:, part] = result[k * line : (k + 1) * line]

    return pl.pallas_call(
        kernel,
        in_specs=[in_smem] + [in_vmem] * 4 + [in_hbm] * 2,
        out_specs=[in_vmem] * side,
        out_shape=[jax.ShapeDtypeStruct((line, half), jnp.bfloat16)] * side,
        scratch_shapes=[
            pltpu.VMEM((2 * depth, half), jnp.bfloat16),
            pltpu.SemaphoreType.DMA((cuts, 2)),
        ],
        compiler_params=budget(24),
        cost_estimate=pl.CostEstimate(
            flops=4 * rows * depth * half, bytes_accessed=4 * depth * half, transcendentals=0
        ),
    )(
        spot,
        mine.reshape(lines, latent_width),
        other.reshape(lines, latent_width),
        value_mine,
        value_other,
        output_mine,
        output_other,
    )


def gated(parts, gain, gate_weight, up_weight, spot, before):
    side = len(parts)
    line, half = parts[0].shape
    rows = side * line
    units = gate_weight.shape[1]
    cuts = 4
    span = half // cuts
    finish = before is not None

    def kernel(spot_ref, *refs):
        part_refs, refs = refs[:side], refs[side:]
        gain_ref, gate_ref, up_ref, refs = refs[0], refs[1], refs[2], refs[3:]
        if finish:
            sum_before, square_before, out_ref, held_ref, sems = refs
        else:
            sum_ref, square_ref, held_ref, sems = refs
        core, first, second = spot_ref[0], spot_ref[1], spot_ref[2]
        owner = 1 - core if finish else core
        copies = []
        for cut in range(cuts):
            for k, weight_ref in enumerate((gate_ref, up_ref)):
                start = pl.multiple_of(owner * half + cut * span, 128)
                copies.append(
                    pltpu.make_async_copy(
                        weight_ref.at[:, pl.ds(start, span)],
                        held_ref.at[pl.ds(k * units, units), pl.ds(cut * span, span)],
                        sems.at[cut, k],
                    )
                )
                copies[-1].start()
        if finish:
            pick = one_hot(swapped_rows(rows, line, side, first, second), rows)
        total = jnp.zeros((rows, 2 * units), jnp.float32)
        squares = jnp.zeros((rows, 128), jnp.float32)
        for cut in range(cuts):
            part = slice(cut * span, (cut + 1) * span)
            block = jnp.concatenate([ref[:, part] for ref in part_refs], axis=0)
            wide = block.astype(jnp.float32)
            if finish:
                wide = product(pick, block)
            for k in range(span // 128):
                lanes = wide[:, k * 128 : (k + 1) * 128]
                squares = squares + lanes * lanes
            start = pl.multiple_of(owner * half + cut * span, 128)
            scaled = (wide * gain_ref[:, pl.ds(start, span)]).astype(jnp.bfloat16)
            copies[2 * cut].wait()
            copies[2 * cut + 1].wait()
            total = total + lax.dot_general(
                scaled, held_ref[:, part], across, preferred_element_type=jnp.float32
            )
        if finish:
            total = total + sum_before[...]
            mean = jnp.sum(squares + square_before[...], axis=1, keepdims=True) / (2 * half)
            total = total * lax.rsqrt(mean + norm_eps)
            gate = total[:, :units]
            out_ref[...] = (gate / (1.0 + jnp.exp(-gate)) * total[:, units:]).astype(jnp.bfloat16)
        else:
            sum_ref[...] = total
            square_ref[...] = squares

    sums = [
        jax.ShapeDtypeStruct((rows, 2 * units), jnp.float32),
        jax.ShapeDtypeStruct((rows, 128), jnp.float32),
    ]
    return pl.pallas_call(
        kernel,
        in_specs=[in_smem] + [in_vmem] * (side + 1) + [in_hbm] * 2 + [in_vmem] * (2 * finish),
        out_specs=in_vmem if finish else [in_vmem] * 2,
        out_shape=jax.ShapeDtypeStruct((rows, units), jnp.bfloat16) if finish else sums,
        scratch_shapes=[
            pltpu.VMEM((2 * units, half), jnp.bfloat16),
            pltpu.SemaphoreType.DMA((cuts, 2)),
        ],
        compiler_params=budget(24),
        cost_estimate=pl.CostEstimate(
            flops=4 * rows * half * units, bytes_accessed=4 * half * units, transcendentals=0
        ),
    )(spot, *parts, gain[None, :], gate_weight.T, up_weight.T, *(before or []))


def swapped_rows(rows, line, side, first, second):
    chip_slots = line // side
    to = line_numbers(rows)
    along = (to // line + first) % side
    beside = to // chip_slots % side
    return ((beside - second + side) % side) * line + along * chip_slots + to % chip_slots


def feed_forward(inner, inner_other, pieces, spot, side):
    rows, units = inner.shape
    cut = pieces[0].shape[1]
    line = rows // side

    def kernel(spot_ref, inner_ref, other_ref, a_ref, b_ref, c_ref, d_ref, *outs):
        core, first, second, layer = spot_ref[0], spot_ref[1], spot_ref[2], spot_ref[3]
        pick = one_hot(swapped_rows(rows, line, side, first, second), rows)
        other = product(pick, other_ref[...]).astype(jnp.bfloat16)
        mine = inner_ref[...]
        same = core == layer % 2
        even = jnp.where(same, mine, other)
        odd = jnp.where(same, other, mine)
        for start, first_ref, second_ref in ((0, a_ref, b_ref), (cut, c_ref, d_ref)):
            result = product(even, first_ref[...]) + product(odd, second_ref[...])
            result = result.astype(jnp.bfloat16)
            for k in range(side):
                outs[k][:, start : start + cut] = result[k * line : (k + 1) * line]

    return pl.pallas_call(
        kernel,
        in_specs=[in_smem] + [in_vmem] * 6,
        out_specs=[in_vmem] * side,
        out_shape=[jax.ShapeDtypeStruct((line, 2 * cut), jnp.bfloat16)] * side,
        compiler_params=budget(24),
        cost_estimate=pl.CostEstimate(
            flops=8 * rows * units * cut, bytes_accessed=8 * units * cut, transcendentals=0
        ),
    )(spot, inner, inner_other, *pieces)


def on_device(
    layer_input,
    query,
    cache,
    lengths,
    counts,
    value_weight,
    output_weight,
    norm_gain,
    gate_weight,
    up_weight,
    down_weight,
    width,
):
    slots, model = layer_input.shape
    half = model // 2
    chips = width // 2

    heads_here, latent_width, head = value_weight.shape
    side = math.isqrt(chips)
    chip_slots = 2 * slots
    line = side * chip_slots
    place = lax.axis_index("tp")
    core = place % 2
    upper = core == 1
    at_y, at_x = place // (2 * side), place // 2 % side
    first, second = jnp.where(upper, at_x, at_y), jnp.where(upper, at_y, at_x)
    layer = lax.axis_index("dp")
    spot = jnp.stack([core, first, second, layer])

    pieces = down_pieces(down_weight, width)
    value_other = core_swap(value_weight, width)
    output_other = core_swap(output_weight, width)
    input_mine = lax.dynamic_slice_in_dim(layer_input, core * half, half, 1)
    input_other = core_swap(
        lax.dynamic_slice_in_dim(layer_input, (1 - core) * half, half, 1), width
    )
    input_chip = jnp.where(
        upper,
        jnp.concatenate([input_other, input_mine], axis=0),
        jnp.concatenate([input_mine, input_other], axis=0),
    ).astype(jnp.float32)

    latent = attend(query, cache, lengths, counts, latent_width, chips)
    arrived = between_chips(latent, width)
    arrived, pieces[0], pieces[1] = lax.optimization_barrier((arrived, pieces[0], pieces[1]))
    arrived_other = core_swap(arrived, width)
    attended_parts = project(
        arrived,
        arrived_other,
        value_weight,
        value_other,
        output_weight,
        output_other,
        spot,
        side,
        slots,
    )

    summed = total(turn(attended_parts, 0, side, 1)).reshape(side, chip_slots, half)
    own_rows = (jnp.arange(side) == second)[:, None, None]
    summed = summed + jnp.where(own_rows, input_chip[None], 0.0)
    summed = summed.astype(jnp.bfloat16).reshape(line, half)
    summed, pieces[2], pieces[3] = lax.optimization_barrier((summed, pieces[2], pieces[3]))
    residual_line = total(turn([summed] * side, 1, side, 1)).astype(jnp.bfloat16)
    residual_mine = turn([residual_line] * side, 0, side, -1)
    residual_other = [core_swap(part, width) for part in residual_mine]
    sums = gated(residual_mine, norm_gain, gate_weight, up_weight, spot, None)
    inner = gated(residual_other, norm_gain, gate_weight, up_weight, spot, sums)
    inner_other = core_swap(inner, width)

    feed_parts = feed_forward(inner, inner_other, pieces, spot, side)
    feed_line = total(turn(feed_parts, 0, side, 1)).astype(jnp.bfloat16)
    feed = total(
        turn(
            [
                lax.dynamic_slice_in_dim(
                    feed_line, (second + k) % side * chip_slots, chip_slots, 0
                )
                for k in range(side)
            ],
            1,
            side,
            1,
        )
    )
    residual = lax.dynamic_slice_in_dim(residual_line, second * chip_slots, chip_slots, 0)
    cut = half // 2
    feed = jnp.where(
        layer // 2 == 1, jnp.concatenate([feed[:, cut:], feed[:, :cut]], axis=1), feed
    )
    mixed = (residual.astype(jnp.float32) + feed).astype(jnp.bfloat16)
    kept = lax.dynamic_slice_in_dim(mixed, core * slots, slots, 0)
    got = core_swap(lax.dynamic_slice_in_dim(mixed, (1 - core) * slots, slots, 0), width)
    out = jnp.where(
        upper,
        jnp.concatenate([got, kept], axis=1),
        jnp.concatenate([kept, got], axis=1),
    )
    live = jnp.arange(slots, dtype=jnp.int32) < counts[0]
    return jnp.where(live[:, None], out, jnp.bfloat16(0.0))


def solution(mesh):
    placed = (
        P(("dp", "tp"), None),
        P(("dp", "tp"), None, None),
        P(("dp", "tp"), None, None),
        P(("dp", "tp")),
        P(("dp", "tp")),
        P("tp", None, None),
        P("tp", None),
        P(),
        P(None, "tp"),
        P(None, "tp"),
        P("tp", "dp"),
    )
    width = mesh.shape["tp"]
    return jax.shard_map(
        lambda *args: on_device(*args, width),
        mesh=mesh,
        in_specs=placed,
        out_specs=P(("dp", "tp"), None),
        check_vma=False,
    )
```

```python
import math

import jax
import jax.numpy as jnp
from jax import lax
from jax.experimental import pallas as pl
from jax.experimental.pallas import tpu as pltpu
from jax.sharding import PartitionSpec as P

score_scale = 1.0 / 192.0**0.5
norm_eps = 1e-06


def core_swap(x, width):
    return lax.ppermute(x, "tp", [(i, i ^ 1) for i in range(width)])


def between_chips(x, width):
    groups = [[2 * chip + core for chip in range(width // 2)] for core in range(2)]
    return lax.all_to_all(x, "tp", 0, 0, tiled=True, axis_index_groups=groups)


def turn(parts, axis, side, sign):
    out = [parts[0]]
    for k in range(1, side):
        pairs = []
        for y in range(side):
            for x in range(side):
                for core in range(2):
                    if axis == core:
                        to = ((y + sign * k) % side) * side + x
                    else:
                        to = y * side + (x + sign * k) % side
                    pairs.append(((y * side + x) * 2 + core, to * 2 + core))
        out.append(lax.ppermute(parts[k], "tp", pairs))
    return out


def total(parts):
    wide = parts[0].astype(jnp.float32)
    for part in parts[1:]:
        wide = wide + part.astype(jnp.float32)
    return wide


def down_pieces(down_weight, width):
    out = []
    for k in range(4):
        pairs = []
        for layer in range(4):
            for place in range(width):
                chip, core = divmod(place, 2)
                cut, row_core = (layer >> 1) ^ (k >> 1), (layer & 1) ^ (k & 1)
                pairs.append(((2 * core + cut) * width + 2 * chip + row_core, layer * width + place))
        out.append(lax.ppermute(down_weight, ("dp", "tp"), pairs))
    return out


in_vmem = pl.BlockSpec(memory_space=pltpu.VMEM)
in_hbm = pl.BlockSpec(memory_space=pltpu.HBM)
in_smem = pl.BlockSpec(memory_space=pltpu.SMEM)
across = (((1,), (1,)), ((), ()))


def product(a, b):
    return jnp.dot(a, b, preferred_element_type=jnp.float32)


def one_hot(source, columns):
    hit = source == lax.broadcasted_iota(jnp.int32, (source.shape[0], columns), 1)
    return jnp.where(hit, 1.0, 0.0).astype(jnp.bfloat16)


def line_numbers(rows):
    return lax.broadcasted_iota(jnp.int32, (rows, 1), 0)


def budget(mib):
    return pltpu.CompilerParams(vmem_limit_bytes=mib * 2**20)


def attend(query, cache, lengths, counts, latent_width, chips):
    slots, heads, wide = query.shape
    ctx = cache.shape[1]
    group = heads // chips
    rows = slots * heads

    def kernel(lengths_ref, counts_ref, q_ref, cache_ref, out_ref, held_ref, sems):
        copies = [
            pltpu.make_async_copy(cache_ref.at[slot], held_ref.at[slot], sems.at[slot])
            for slot in range(slots)
        ]

        def score(slot):
            copies[slot].wait()
            place = lax.broadcasted_iota(jnp.int32, (heads, ctx), 1)
            found = product(q_ref[slot], held_ref[slot]) * score_scale
            return jnp.where(place < lengths_ref[slot], found, -1e30)

        def gather(slot, scores):
            raised = jnp.exp(scores - jnp.max(scores, axis=1, keepdims=True))
            latent = lax.dot_general(
                raised.astype(jnp.bfloat16),
                held_ref[slot, :latent_width],
                across,
                preferred_element_type=jnp.float32,
            )
            latent = latent / jnp.sum(raised, axis=1, keepdims=True)
            return jnp.where(slot < counts_ref[0], latent, 0.0).astype(jnp.bfloat16)

        copies[0].start()
        copies[1].start()
        latents = []
        scores = score(0)
        for slot in range(slots):
            if slot + 2 < slots:
                copies[slot + 2].start()
            following = score(slot + 1) if slot + 1 < slots else None
            latents.append(gather(slot, scores))
            scores = following
        to = line_numbers(rows)
        source = to // group % slots * heads + to // (slots * group) * group + to % group
        out_ref[...] = product(
            one_hot(source, rows), jnp.concatenate(latents, axis=0)
        ).astype(jnp.bfloat16)

    out = pl.pallas_call(
        kernel,
        in_specs=[in_smem, in_smem, in_vmem, in_hbm],
        out_specs=in_vmem,
        out_shape=jax.ShapeDtypeStruct((rows, latent_width), jnp.bfloat16),
        scratch_shapes=[
            pltpu.VMEM((slots, wide, ctx), jnp.bfloat16),
            pltpu.SemaphoreType.DMA((slots,)),
        ],
        compiler_params=budget(57),
        cost_estimate=pl.CostEstimate(
            flops=2 * rows * ctx * (wide + latent_width),
            bytes_accessed=2 * cache.size,
            transcendentals=rows * ctx,
        ),
    )(lengths, counts, query, jnp.swapaxes(cache, 1, 2))
    return out.reshape(chips, slots * group, latent_width)


def project(mine, other, value_mine, value_other, output_mine, output_other, spot, side, slots):
    chips, pairs, latent_width = mine.shape
    heads_here, _, head = value_mine.shape
    heads = 2 * heads_here
    depth, model = output_mine.shape
    half = model // 2
    rows = 2 * chips * slots
    line = rows // side
    lines = chips * pairs

    def kernel(spot_ref, mine_ref, other_ref, vm_ref, vo_ref, om_ref, oo_ref, *outs):
        core, first = spot_ref[0], spot_ref[1]
        to = line_numbers(rows)
        along = (to // line + first) % side
        second = to // (2 * slots) % side
        chip = jnp.where(core == 0, along * side + second, second * side + along)
        from_other = (to // slots % 2 + core) % 2
        source = from_other * lines + chip * pairs + to % slots * heads
        latents = jnp.concatenate([mine_ref[...], other_ref[...]], axis=0)
        values = []
        for index in range(heads):
            owner, weight_ref = (core, vm_ref) if index < heads_here else (1 - core, vo_ref)
            place = index % heads_here
            pick = one_hot(source + owner * heads_here + place, 2 * lines)
            picked = product(pick, latents).astype(jnp.bfloat16)
            values.append(product(picked, weight_ref[place]).astype(jnp.bfloat16))
        values = jnp.concatenate(values, axis=1)
        at = pl.ds(pl.multiple_of(core * half, 128), half)
        result = product(values[:, :depth], om_ref[:, at]) + product(values[:, depth:], oo_ref[:, at])
        result = result.astype(jnp.bfloat16)
        for k in range(side):
            outs[k][...] = result[k * line : (k + 1) * line]

    return pl.pallas_call(
        kernel,
        in_specs=[in_smem] + [in_vmem] * 6,
        out_specs=[in_vmem] * side,
        out_shape=[jax.ShapeDtypeStruct((line, half), jnp.bfloat16)] * side,
        compiler_params=budget(24),
        cost_estimate=pl.CostEstimate(
            flops=4 * rows * depth * half, bytes_accessed=4 * depth * half, transcendentals=0
        ),
    )(
        spot,
        mine.reshape(lines, latent_width),
        other.reshape(lines, latent_width),
        value_mine,
        value_other,
        output_mine,
        output_other,
    )


def gated(parts, gain, gate_weight, up_weight, spot, before):
    side = len(parts)
    line, half = parts[0].shape
    rows = side * line
    units = gate_weight.shape[1]
    finish = before is not None

    def kernel(spot_ref, *refs):
        part_refs, refs = refs[:side], refs[side:]
        gain_ref, gate_ref, up_ref, refs = refs[0], refs[1], refs[2], refs[3:]
        if finish:
            sum_before, square_before, out_ref = refs
        else:
            sum_ref, square_ref = refs
        core, first, second = spot_ref[0], spot_ref[1], spot_ref[2]
        owner = 1 - core if finish else core
        at = pl.ds(pl.multiple_of(owner * half, 128), half)
        block = jnp.concatenate([ref[...] for ref in part_refs], axis=0)
        if finish:
            wide = product(one_hot(swapped_rows(rows, line, side, first, second), rows), block)
        else:
            wide = block.astype(jnp.float32)
        squares = jnp.zeros((rows, 128), jnp.float32)
        for k in range(half // 128):
            lanes = wide[:, k * 128 : (k + 1) * 128]
            squares = squares + lanes * lanes
        scaled = (wide * gain_ref[:, at]).astype(jnp.bfloat16).T
        total = jnp.concatenate(
            [product(gate_ref[:, at], scaled), product(up_ref[:, at], scaled)], axis=0
        ).T
        if finish:
            total = total + sum_before[...]
            mean = jnp.sum(squares + square_before[...], axis=1, keepdims=True) / (2 * half)
            total = total * lax.rsqrt(mean + norm_eps)
            gate = total[:, :units]
            out_ref[...] = (gate / (1.0 + jnp.exp(-gate)) * total[:, units:]).astype(jnp.bfloat16)
        else:
            sum_ref[...] = total
            square_ref[...] = squares

    sums = [
        jax.ShapeDtypeStruct((rows, 2 * units), jnp.float32),
        jax.ShapeDtypeStruct((rows, 128), jnp.float32),
    ]
    return pl.pallas_call(
        kernel,
        in_specs=[in_smem] + [in_vmem] * (side + 3 + 2 * finish),
        out_specs=in_vmem if finish else [in_vmem] * 2,
        out_shape=jax.ShapeDtypeStruct((rows, units), jnp.bfloat16) if finish else sums,
        compiler_params=budget(24),
        cost_estimate=pl.CostEstimate(
            flops=4 * rows * half * units, bytes_accessed=4 * half * units, transcendentals=0
        ),
    )(spot, *parts, gain[None, :], gate_weight.T, up_weight.T, *(before or []))


def swapped_rows(rows, line, side, first, second):
    chip_slots = line // side
    to = line_numbers(rows)
    along = (to // line + first) % side
    beside = to // chip_slots % side
    return ((beside - second + side) % side) * line + along * chip_slots + to % chip_slots


def feed_forward(inner, inner_other, pieces, spot, side):
    rows, units = inner.shape
    cut = pieces[0].shape[1]
    line = rows // side

    def kernel(spot_ref, inner_ref, other_ref, a_ref, b_ref, c_ref, d_ref, *outs):
        core, first, second, layer = spot_ref[0], spot_ref[1], spot_ref[2], spot_ref[3]
        pick = one_hot(swapped_rows(rows, line, side, first, second), rows)
        other = product(pick, other_ref[...]).astype(jnp.bfloat16)
        mine = inner_ref[...]
        same = core == layer % 2
        even = jnp.where(same, mine, other)
        odd = jnp.where(same, other, mine)
        for start, first_ref, second_ref in ((0, a_ref, b_ref), (cut, c_ref, d_ref)):
            result = product(even, first_ref[...]) + product(odd, second_ref[...])
            result = result.astype(jnp.bfloat16)
            for k in range(side):
                outs[k][:, start : start + cut] = result[k * line : (k + 1) * line]

    return pl.pallas_call(
        kernel,
        in_specs=[in_smem] + [in_vmem] * 6,
        out_specs=[in_vmem] * side,
        out_shape=[jax.ShapeDtypeStruct((line, 2 * cut), jnp.bfloat16)] * side,
        compiler_params=budget(24),
        cost_estimate=pl.CostEstimate(
            flops=8 * rows * units * cut, bytes_accessed=8 * units * cut, transcendentals=0
        ),
    )(spot, inner, inner_other, *pieces)


def on_device(
    layer_input,
    query,
    cache,
    lengths,
    counts,
    value_weight,
    output_weight,
    norm_gain,
    gate_weight,
    up_weight,
    down_weight,
    width,
):
    slots, model = layer_input.shape
    half = model // 2
    chips = width // 2

    heads_here, latent_width, head = value_weight.shape
    side = math.isqrt(chips)
    chip_slots = 2 * slots
    line = side * chip_slots
    place = lax.axis_index("tp")
    core = place % 2
    upper = core == 1
    at_y, at_x = place // (2 * side), place // 2 % side
    first, second = jnp.where(upper, at_x, at_y), jnp.where(upper, at_y, at_x)
    layer = lax.axis_index("dp")
    spot = jnp.stack([core, first, second, layer])

    pieces = down_pieces(down_weight, width)
    value_other = core_swap(value_weight, width)
    output_other = core_swap(output_weight, width)
    input_mine = lax.dynamic_slice_in_dim(layer_input, core * half, half, 1)
    input_other = core_swap(
        lax.dynamic_slice_in_dim(layer_input, (1 - core) * half, half, 1), width
    )
    input_chip = jnp.where(
        upper,
        jnp.concatenate([input_other, input_mine], axis=0),
        jnp.concatenate([input_mine, input_other], axis=0),
    ).astype(jnp.float32)

    latent = attend(query, cache, lengths, counts, latent_width, chips)
    arrived = between_chips(latent, width)
    arrived, pieces[0], pieces[1] = lax.optimization_barrier((arrived, pieces[0], pieces[1]))
    arrived_other = core_swap(arrived, width)
    attended_parts = project(
        arrived,
        arrived_other,
        value_weight,
        value_other,
        output_weight,
        output_other,
        spot,
        side,
        slots,
    )

    summed = total(turn(attended_parts, 0, side, 1)).reshape(side, chip_slots, half)
    own_rows = (jnp.arange(side) == second)[:, None, None]
    summed = summed + jnp.where(own_rows, input_chip[None], 0.0)
    summed = summed.astype(jnp.bfloat16).reshape(line, half)
    summed, pieces[2], pieces[3] = lax.optimization_barrier((summed, pieces[2], pieces[3]))
    residual_line = total(turn([summed] * side, 1, side, 1)).astype(jnp.bfloat16)
    residual_mine = turn([residual_line] * side, 0, side, -1)
    residual_other = [core_swap(part, width) for part in residual_mine]
    sums = gated(residual_mine, norm_gain, gate_weight, up_weight, spot, None)
    inner = gated(residual_other, norm_gain, gate_weight, up_weight, spot, sums)
    inner_other = core_swap(inner, width)

    feed_parts = feed_forward(inner, inner_other, pieces, spot, side)
    feed_line = total(turn(feed_parts, 0, side, 1)).astype(jnp.bfloat16)
    feed = total(
        turn(
            [
                lax.dynamic_slice_in_dim(
                    feed_line, (second + k) % side * chip_slots, chip_slots, 0
                )
                for k in range(side)
            ],
            1,
            side,
            1,
        )
    )
    residual = lax.dynamic_slice_in_dim(residual_line, second * chip_slots, chip_slots, 0)
    cut = half // 2
    feed = jnp.where(
        layer // 2 == 1, jnp.concatenate([feed[:, cut:], feed[:, :cut]], axis=1), feed
    )
    mixed = (residual.astype(jnp.float32) + feed).astype(jnp.bfloat16)
    kept = lax.dynamic_slice_in_dim(mixed, core * slots, slots, 0)
    got = core_swap(lax.dynamic_slice_in_dim(mixed, (1 - core) * slots, slots, 0), width)
    out = jnp.where(
        upper,
        jnp.concatenate([got, kept], axis=1),
        jnp.concatenate([kept, got], axis=1),
    )
    live = jnp.arange(slots, dtype=jnp.int32) < counts[0]
    return jnp.where(live[:, None], out, jnp.bfloat16(0.0))


def solution(mesh):
    placed = (
        P(("dp", "tp"), None),
        P(("dp", "tp"), None, None),
        P(("dp", "tp"), None, None),
        P(("dp", "tp")),
        P(("dp", "tp")),
        P("tp", None, None),
        P("tp", None),
        P(),
        P(None, "tp"),
        P(None, "tp"),
        P("tp", "dp"),
    )
    width = mesh.shape["tp"]
    return jax.shard_map(
        lambda *args: on_device(*args, width),
        mesh=mesh,
        in_specs=placed,
        out_specs=P(("dp", "tp"), None),
        check_vma=False,
    )
```

```python
import math

import jax
import jax.numpy as jnp
from jax import lax
from jax.experimental import pallas as pl
from jax.experimental.pallas import tpu as pltpu
from jax.sharding import PartitionSpec as P

score_scale = 1.0 / 192.0**0.5
norm_eps = 1e-06


def core_swap(x, width):
    return lax.ppermute(x, "tp", [(i, i ^ 1) for i in range(width)])


def between_chips(x, width):
    groups = [[2 * chip + core for chip in range(width // 2)] for core in range(2)]
    return lax.all_to_all(x, "tp", 0, 0, tiled=True, axis_index_groups=groups)


def turn(parts, axis, side, sign):
    out = [parts[0]]
    for k in range(1, side):
        pairs = []
        for y in range(side):
            for x in range(side):
                for core in range(2):
                    if axis == core:
                        to = ((y + sign * k) % side) * side + x
                    else:
                        to = y * side + (x + sign * k) % side
                    pairs.append(((y * side + x) * 2 + core, to * 2 + core))
        out.append(lax.ppermute(parts[k], "tp", pairs))
    return out


def total(parts):
    wide = parts[0].astype(jnp.float32)
    for part in parts[1:]:
        wide = wide + part.astype(jnp.float32)
    return wide


def down_pieces(down_weight, width):
    out = []
    for k in range(4):
        pairs = []
        for layer in range(4):
            for place in range(width):
                chip, core = divmod(place, 2)
                cut, row_core = (layer >> 1) ^ (k >> 1), (layer & 1) ^ (k & 1)
                pairs.append(((2 * core + cut) * width + 2 * chip + row_core, layer * width + place))
        out.append(lax.ppermute(down_weight, ("dp", "tp"), pairs))
    return out


in_vmem = pl.BlockSpec(memory_space=pltpu.VMEM)
in_hbm = pl.BlockSpec(memory_space=pltpu.HBM)
in_smem = pl.BlockSpec(memory_space=pltpu.SMEM)
across = (((1,), (1,)), ((), ()))


def product(a, b):
    return jnp.dot(a, b, preferred_element_type=jnp.float32)


def one_hot(source, columns):
    hit = source == lax.broadcasted_iota(jnp.int32, (source.shape[0], columns), 1)
    return jnp.where(hit, 1.0, 0.0).astype(jnp.bfloat16)


def line_numbers(rows):
    return lax.broadcasted_iota(jnp.int32, (rows, 1), 0)


def budget(mib):
    return pltpu.CompilerParams(vmem_limit_bytes=mib * 2**20)


def attend(query, cache, lengths, counts, latent_width, chips):
    slots, heads, wide = query.shape
    ctx = cache.shape[1]
    group = heads // chips
    rows = slots * heads

    def kernel(lengths_ref, counts_ref, q_ref, cache_ref, out_ref, held_ref, sems):
        copies = [
            pltpu.make_async_copy(cache_ref.at[slot], held_ref.at[slot], sems.at[slot])
            for slot in range(slots)
        ]

        def score(slot):
            copies[slot].wait()
            place = lax.broadcasted_iota(jnp.int32, (heads, ctx), 1)
            found = product(q_ref[slot], held_ref[slot]) * score_scale
            return jnp.where(place < lengths_ref[slot], found, -1e30)

        def gather(slot, scores):
            raised = jnp.exp(scores - jnp.max(scores, axis=1, keepdims=True))
            latent = lax.dot_general(
                raised.astype(jnp.bfloat16),
                held_ref[slot, :latent_width],
                across,
                preferred_element_type=jnp.float32,
            )
            latent = latent / jnp.sum(raised, axis=1, keepdims=True)
            return jnp.where(slot < counts_ref[0], latent, 0.0).astype(jnp.bfloat16)

        copies[0].start()
        copies[1].start()
        latents = []
        scores = score(0)
        for slot in range(slots):
            if slot + 2 < slots:
                copies[slot + 2].start()
            following = score(slot + 1) if slot + 1 < slots else None
            latents.append(gather(slot, scores))
            scores = following
        to = line_numbers(rows)
        source = to // group % slots * heads + to // (slots * group) * group + to % group
        out_ref[...] = product(
            one_hot(source, rows), jnp.concatenate(latents, axis=0)
        ).astype(jnp.bfloat16)

    out = pl.pallas_call(
        kernel,
        in_specs=[in_smem, in_smem, in_vmem, in_hbm],
        out_specs=in_vmem,
        out_shape=jax.ShapeDtypeStruct((rows, latent_width), jnp.bfloat16),
        scratch_shapes=[
            pltpu.VMEM((slots, wide, ctx), jnp.bfloat16),
            pltpu.SemaphoreType.DMA((slots,)),
        ],
        compiler_params=budget(55),
        cost_estimate=pl.CostEstimate(
            flops=2 * rows * ctx * (wide + latent_width),
            bytes_accessed=2 * cache.size,
            transcendentals=rows * ctx,
        ),
    )(lengths, counts, query, jnp.swapaxes(cache, 1, 2))
    return out.reshape(chips, slots * group, latent_width)


def project(mine, other, value_mine, value_other, output_mine, output_other, spot, side, slots):
    chips, pairs, latent_width = mine.shape
    heads_here, _, head = value_mine.shape
    heads = 2 * heads_here
    depth, model = output_mine.shape
    half = model // 2
    rows = 2 * chips * slots
    line = rows // side
    lines = chips * pairs

    def kernel(spot_ref, mine_ref, other_ref, vm_ref, vo_ref, om_ref, oo_ref, *outs):
        core, first = spot_ref[0], spot_ref[1]
        to = line_numbers(rows)
        along = (to // line + first) % side
        second = to // (2 * slots) % side
        chip = jnp.where(core == 0, along * side + second, second * side + along)
        from_other = (to // slots % 2 + core) % 2
        source = from_other * lines + chip * pairs + to % slots * heads
        latents = jnp.concatenate([mine_ref[...], other_ref[...]], axis=0)
        values = []
        for index in range(heads):
            owner, weight_ref = (core, vm_ref) if index < heads_here else (1 - core, vo_ref)
            place = index % heads_here
            pick = one_hot(source + owner * heads_here + place, 2 * lines)
            picked = product(pick, latents).astype(jnp.bfloat16)
            values.append(product(picked, weight_ref[place]).astype(jnp.bfloat16))
        values = jnp.concatenate(values, axis=1)
        at = pl.ds(pl.multiple_of(core * half, 128), half)
        result = product(values[:, :depth], om_ref[:, at]) + product(values[:, depth:], oo_ref[:, at])
        result = result.astype(jnp.bfloat16)
        for k in range(side):
            outs[k][...] = result[k * line : (k + 1) * line]

    return pl.pallas_call(
        kernel,
        in_specs=[in_smem] + [in_vmem] * 6,
        out_specs=[in_vmem] * side,
        out_shape=[jax.ShapeDtypeStruct((line, half), jnp.bfloat16)] * side,
        compiler_params=budget(24),
        cost_estimate=pl.CostEstimate(
            flops=4 * rows * depth * half, bytes_accessed=4 * depth * half, transcendentals=0
        ),
    )(
        spot,
        mine.reshape(lines, latent_width),
        other.reshape(lines, latent_width),
        value_mine,
        value_other,
        output_mine,
        output_other,
    )


def gated(parts, gain, gate_weight, up_weight, spot, before):
    side = len(parts)
    line, half = parts[0].shape
    rows = side * line
    units = gate_weight.shape[1]
    finish = before is not None

    def kernel(spot_ref, *refs):
        part_refs, refs = refs[:side], refs[side:]
        gain_ref, gate_ref, up_ref, refs = refs[0], refs[1], refs[2], refs[3:]
        if finish:
            sum_before, square_before, out_ref = refs
        else:
            sum_ref, square_ref = refs
        core, first, second = spot_ref[0], spot_ref[1], spot_ref[2]
        owner = 1 - core if finish else core
        at = pl.ds(pl.multiple_of(owner * half, 128), half)
        block = jnp.concatenate([ref[...] for ref in part_refs], axis=0)
        if finish:
            wide = product(one_hot(swapped_rows(rows, line, side, first, second), rows), block)
        else:
            wide = block.astype(jnp.float32)
        squares = jnp.zeros((rows, 128), jnp.float32)
        for k in range(half // 128):
            lanes = wide[:, k * 128 : (k + 1) * 128]
            squares = squares + lanes * lanes
        scaled = (wide * gain_ref[:, at]).astype(jnp.bfloat16).T
        total = jnp.concatenate(
            [product(gate_ref[:, at], scaled), product(up_ref[:, at], scaled)], axis=0
        ).T
        if finish:
            total = total + sum_before[...]
            mean = jnp.sum(squares + square_before[...], axis=1, keepdims=True) / (2 * half)
            total = total * lax.rsqrt(mean + norm_eps)
            gate = total[:, :units]
            out_ref[...] = (gate / (1.0 + jnp.exp(-gate)) * total[:, units:]).astype(jnp.bfloat16)
        else:
            sum_ref[...] = total
            square_ref[...] = squares

    sums = [
        jax.ShapeDtypeStruct((rows, 2 * units), jnp.float32),
        jax.ShapeDtypeStruct((rows, 128), jnp.float32),
    ]
    return pl.pallas_call(
        kernel,
        in_specs=[in_smem] + [in_vmem] * (side + 3 + 2 * finish),
        out_specs=in_vmem if finish else [in_vmem] * 2,
        out_shape=jax.ShapeDtypeStruct((rows, units), jnp.bfloat16) if finish else sums,
        compiler_params=budget(24),
        cost_estimate=pl.CostEstimate(
            flops=4 * rows * half * units, bytes_accessed=4 * half * units, transcendentals=0
        ),
    )(spot, *parts, gain[None, :], gate_weight.T, up_weight.T, *(before or []))


def swapped_rows(rows, line, side, first, second):
    chip_slots = line // side
    to = line_numbers(rows)
    along = (to // line + first) % side
    beside = to // chip_slots % side
    return ((beside - second + side) % side) * line + along * chip_slots + to % chip_slots


def feed_forward(inner, inner_other, pieces, spot, side):
    rows, units = inner.shape
    cut = pieces[0].shape[1]
    line = rows // side

    def kernel(spot_ref, inner_ref, other_ref, a_ref, b_ref, c_ref, d_ref, *outs):
        core, first, second, layer = spot_ref[0], spot_ref[1], spot_ref[2], spot_ref[3]
        pick = one_hot(swapped_rows(rows, line, side, first, second), rows)
        other = product(pick, other_ref[...]).astype(jnp.bfloat16)
        mine = inner_ref[...]
        same = core == layer % 2
        even = jnp.where(same, mine, other)
        odd = jnp.where(same, other, mine)
        for start, first_ref, second_ref in ((0, a_ref, b_ref), (cut, c_ref, d_ref)):
            result = product(even, first_ref[...]) + product(odd, second_ref[...])
            result = result.astype(jnp.bfloat16)
            for k in range(side):
                outs[k][:, start : start + cut] = result[k * line : (k + 1) * line]

    return pl.pallas_call(
        kernel,
        in_specs=[in_smem] + [in_vmem] * 6,
        out_specs=[in_vmem] * side,
        out_shape=[jax.ShapeDtypeStruct((line, 2 * cut), jnp.bfloat16)] * side,
        compiler_params=budget(24),
        cost_estimate=pl.CostEstimate(
            flops=8 * rows * units * cut, bytes_accessed=8 * units * cut, transcendentals=0
        ),
    )(spot, inner, inner_other, *pieces)


def on_device(
    layer_input,
    query,
    cache,
    lengths,
    counts,
    value_weight,
    output_weight,
    norm_gain,
    gate_weight,
    up_weight,
    down_weight,
    width,
):
    slots, model = layer_input.shape
    half = model // 2
    chips = width // 2

    heads_here, latent_width, head = value_weight.shape
    side = math.isqrt(chips)
    chip_slots = 2 * slots
    line = side * chip_slots
    place = lax.axis_index("tp")
    core = place % 2
    upper = core == 1
    at_y, at_x = place // (2 * side), place // 2 % side
    first, second = jnp.where(upper, at_x, at_y), jnp.where(upper, at_y, at_x)
    layer = lax.axis_index("dp")
    spot = jnp.stack([core, first, second, layer])

    pieces = down_pieces(down_weight, width)
    value_other = core_swap(value_weight, width)
    output_other = core_swap(output_weight, width)
    input_mine = lax.dynamic_slice_in_dim(layer_input, core * half, half, 1)
    input_other = core_swap(
        lax.dynamic_slice_in_dim(layer_input, (1 - core) * half, half, 1), width
    )
    latent = attend(query, cache, lengths, counts, latent_width, chips)
    latent, value_other, input_other = lax.optimization_barrier((latent, value_other, input_other))
    input_chip = jnp.where(
        upper,
        jnp.concatenate([input_other, input_mine], axis=0),
        jnp.concatenate([input_mine, input_other], axis=0),
    ).astype(jnp.float32)
    arrived = between_chips(latent, width)
    arrived, pieces[0], pieces[1] = lax.optimization_barrier((arrived, pieces[0], pieces[1]))
    arrived_other = core_swap(arrived, width)
    attended_parts = project(
        arrived,
        arrived_other,
        value_weight,
        value_other,
        output_weight,
        output_other,
        spot,
        side,
        slots,
    )

    summed = total(turn(attended_parts, 0, side, 1)).reshape(side, chip_slots, half)
    own_rows = (jnp.arange(side) == second)[:, None, None]
    summed = summed + jnp.where(own_rows, input_chip[None], 0.0)
    summed = summed.astype(jnp.bfloat16).reshape(line, half)
    summed, pieces[2], pieces[3] = lax.optimization_barrier((summed, pieces[2], pieces[3]))
    residual_line = total(turn([summed] * side, 1, side, 1)).astype(jnp.bfloat16)
    residual_mine = turn([residual_line] * side, 0, side, -1)
    residual_mine = lax.optimization_barrier(residual_mine)
    residual_other = [core_swap(part, width) for part in residual_mine]
    sums = gated(residual_mine, norm_gain, gate_weight, up_weight, spot, None)
    inner = gated(residual_other, norm_gain, gate_weight, up_weight, spot, sums)
    inner_other = core_swap(inner, width)

    feed_parts = feed_forward(inner, inner_other, pieces, spot, side)
    feed_line = total(turn(feed_parts, 0, side, 1)).astype(jnp.bfloat16)
    feed = total(
        turn(
            [
                lax.dynamic_slice_in_dim(
                    feed_line, (second + k) % side * chip_slots, chip_slots, 0
                )
                for k in range(side)
            ],
            1,
            side,
            1,
        )
    )
    residual = lax.dynamic_slice_in_dim(residual_line, second * chip_slots, chip_slots, 0)
    cut = half // 2
    feed = jnp.where(
        layer // 2 == 1, jnp.concatenate([feed[:, cut:], feed[:, :cut]], axis=1), feed
    )
    mixed = (residual.astype(jnp.float32) + feed).astype(jnp.bfloat16)
    kept = lax.dynamic_slice_in_dim(mixed, core * slots, slots, 0)
    got = core_swap(lax.dynamic_slice_in_dim(mixed, (1 - core) * slots, slots, 0), width)
    out = jnp.where(
        upper,
        jnp.concatenate([got, kept], axis=1),
        jnp.concatenate([kept, got], axis=1),
    )
    live = jnp.arange(slots, dtype=jnp.int32) < counts[0]
    return jnp.where(live[:, None], out, jnp.bfloat16(0.0))


def solution(mesh):
    placed = (
        P(("dp", "tp"), None),
        P(("dp", "tp"), None, None),
        P(("dp", "tp"), None, None),
        P(("dp", "tp")),
        P(("dp", "tp")),
        P("tp", None, None),
        P("tp", None),
        P(),
        P(None, "tp"),
        P(None, "tp"),
        P("tp", "dp"),
    )
    width = mesh.shape["tp"]
    return jax.shard_map(
        lambda *args: on_device(*args, width),
        mesh=mesh,
        in_specs=placed,
        out_specs=P(("dp", "tp"), None),
        check_vma=False,
    )
```

```python
import math

import jax
import jax.numpy as jnp
from jax import lax
from jax.experimental import pallas as pl
from jax.experimental.pallas import tpu as pltpu
from jax.sharding import PartitionSpec as P

score_scale = 1.0 / 192.0**0.5
norm_eps = 1e-06


def core_swap(x, width):
    return lax.ppermute(x, "tp", [(i, i ^ 1) for i in range(width)])


def between_chips(x, width):
    groups = [[2 * chip + core for chip in range(width // 2)] for core in range(2)]
    return lax.all_to_all(x, "tp", 0, 0, tiled=True, axis_index_groups=groups)


def turn(parts, axis, side, sign):
    out = [parts[0]]
    for k in range(1, side):
        pairs = []
        for y in range(side):
            for x in range(side):
                for core in range(2):
                    if axis == core:
                        to = ((y + sign * k) % side) * side + x
                    else:
                        to = y * side + (x + sign * k) % side
                    pairs.append(((y * side + x) * 2 + core, to * 2 + core))
        out.append(lax.ppermute(parts[k], "tp", pairs))
    return out


def total(parts):
    wide = parts[0].astype(jnp.float32)
    for part in parts[1:]:
        wide = wide + part.astype(jnp.float32)
    return wide


def down_pieces(down_weight, width):
    out = []
    for k in range(4):
        pairs = []
        for layer in range(4):
            for place in range(width):
                chip, core = divmod(place, 2)
                cut, row_core = (layer >> 1) ^ (k >> 1), (layer & 1) ^ (k & 1)
                pairs.append(((2 * core + cut) * width + 2 * chip + row_core, layer * width + place))
        out.append(lax.ppermute(down_weight, ("dp", "tp"), pairs))
    return out


in_vmem = pl.BlockSpec(memory_space=pltpu.VMEM)
in_hbm = pl.BlockSpec(memory_space=pltpu.HBM)
in_smem = pl.BlockSpec(memory_space=pltpu.SMEM)
across = (((1,), (1,)), ((), ()))


def product(a, b):
    return jnp.dot(a, b, preferred_element_type=jnp.float32)


def one_hot(source, columns):
    hit = source == lax.broadcasted_iota(jnp.int32, (source.shape[0], columns), 1)
    return jnp.where(hit, 1.0, 0.0).astype(jnp.bfloat16)


def line_numbers(rows):
    return lax.broadcasted_iota(jnp.int32, (rows, 1), 0)


def budget(mib):
    return pltpu.CompilerParams(vmem_limit_bytes=mib * 2**20)


def attend(query, cache, lengths, counts, latent_width, chips):
    slots, heads, wide = query.shape
    ctx = cache.shape[1]
    group = heads // chips
    rows = slots * heads

    def kernel(lengths_ref, counts_ref, q_ref, cache_ref, out_ref, held_ref, sems):
        copies = [
            pltpu.make_async_copy(cache_ref.at[slot], held_ref.at[slot], sems.at[slot])
            for slot in range(slots)
        ]

        def score(slot):
            copies[slot].wait()
            place = lax.broadcasted_iota(jnp.int32, (heads, ctx), 1)
            found = product(q_ref[slot], held_ref[slot]) * score_scale
            return jnp.where(place < lengths_ref[slot], found, -1e30)

        def gather(slot, scores):
            raised = jnp.exp(scores - jnp.max(scores, axis=1, keepdims=True))
            latent = lax.dot_general(
                raised.astype(jnp.bfloat16),
                held_ref[slot, :latent_width],
                across,
                preferred_element_type=jnp.float32,
            )
            latent = latent / jnp.sum(raised, axis=1, keepdims=True)
            return jnp.where(slot < counts_ref[0], latent, 0.0).astype(jnp.bfloat16)

        copies[0].start()
        copies[1].start()
        latents = []
        scores = score(0)
        for slot in range(slots):
            if slot + 2 < slots:
                copies[slot + 2].start()
            following = score(slot + 1) if slot + 1 < slots else None
            latents.append(gather(slot, scores))
            scores = following
        to = line_numbers(rows)
        source = to // group % slots * heads + to // (slots * group) * group + to % group
        out_ref[...] = product(
            one_hot(source, rows), jnp.concatenate(latents, axis=0)
        ).astype(jnp.bfloat16)

    out = pl.pallas_call(
        kernel,
        in_specs=[in_smem, in_smem, in_vmem, in_hbm],
        out_specs=in_vmem,
        out_shape=jax.ShapeDtypeStruct((rows, latent_width), jnp.bfloat16),
        scratch_shapes=[
            pltpu.VMEM((slots, wide, ctx), jnp.bfloat16),
            pltpu.SemaphoreType.DMA((slots,)),
        ],
        compiler_params=budget(57),
        cost_estimate=pl.CostEstimate(
            flops=2 * rows * ctx * (wide + latent_width),
            bytes_accessed=2 * cache.size,
            transcendentals=rows * ctx,
        ),
    )(lengths, counts, query, jnp.swapaxes(cache, 1, 2))
    return out.reshape(chips, slots * group, latent_width)


def project(mine, other, value_mine, value_other, output_mine, output_other, spot, side, slots):
    chips, pairs, latent_width = mine.shape
    heads_here, _, head = value_mine.shape
    heads = 2 * heads_here
    depth, model = output_mine.shape
    half = model // 2
    rows = 2 * chips * slots
    line = rows // side
    lines = chips * pairs
    cuts = 4
    span = half // cuts

    def kernel(spot_ref, mine_ref, other_ref, vm_ref, vo_ref, om_ref, oo_ref, *refs):
        outs, (value_ref, held_ref, value_sems, sems) = refs[:side], refs[side:]
        core, first = spot_ref[0], spot_ref[1]
        value_copies, copies = [], []
        for k, weight_ref in enumerate((vm_ref, vo_ref)):
            value_copies.append(
                pltpu.make_async_copy(weight_ref, value_ref.at[k], value_sems.at[k])
            )
            value_copies[-1].start()
        for cut in range(cuts):
            for k, weight_ref in enumerate((om_ref, oo_ref)):
                start = pl.multiple_of(core * half + cut * span, 128)
                copies.append(
                    pltpu.make_async_copy(
                        weight_ref.at[:, pl.ds(start, span)],
                        held_ref.at[pl.ds(k * depth, depth), pl.ds(cut * span, span)],
                        sems.at[cut, k],
                    )
                )
                copies[-1].start()
        to = line_numbers(rows)
        along = (to // line + first) % side
        second = to // (2 * slots) % side
        chip = jnp.where(core == 0, along * side + second, second * side + along)
        from_other = (to // slots % 2 + core) % 2
        source = from_other * lines + chip * pairs + to % slots * heads
        latents = jnp.concatenate([mine_ref[...], other_ref[...]], axis=0)
        values = []
        for index in range(heads):
            whose, place = divmod(index, heads_here)
            owner = (core + whose) % 2
            if place == 0:
                value_copies[whose].wait()
            pick = one_hot(source + owner * heads_here + place, 2 * lines)
            picked = product(pick, latents).astype(jnp.bfloat16)
            values.append(product(picked, value_ref[whose, place]).astype(jnp.bfloat16))
        values = jnp.concatenate(values, axis=1)
        for cut in range(cuts):
            copies[2 * cut].wait()
            copies[2 * cut + 1].wait()
            part = slice(cut * span, (cut + 1) * span)
            result = product(values, held_ref[:, part]).astype(jnp.bfloat16)
            for k in range(side):
                outs[k][:, part] = result[k * line : (k + 1) * line]

    return pl.pallas_call(
        kernel,
        in_specs=[in_smem] + [in_vmem] * 2 + [in_hbm] * 4,
        out_specs=[in_vmem] * side,
        out_shape=[jax.ShapeDtypeStruct((line, half), jnp.bfloat16)] * side,
        scratch_shapes=[
            pltpu.VMEM((2, heads_here, latent_width, head), jnp.bfloat16),
            pltpu.VMEM((2 * depth, half), jnp.bfloat16),
            pltpu.SemaphoreType.DMA((2,)),
            pltpu.SemaphoreType.DMA((cuts, 2)),
        ],
        compiler_params=budget(59),
        cost_estimate=pl.CostEstimate(
            flops=4 * rows * depth * half, bytes_accessed=4 * depth * half, transcendentals=0
        ),
    )(
        spot,
        mine.reshape(lines, latent_width),
        other.reshape(lines, latent_width),
        value_mine,
        value_other,
        output_mine,
        output_other,
    )


def gated(parts, gain, gate_weight, up_weight, spot, before):
    side = len(parts)
    line, half = parts[0].shape
    rows = side * line
    units = gate_weight.shape[1]
    finish = before is not None

    def kernel(spot_ref, *refs):
        part_refs, refs = refs[:side], refs[side:]
        gain_ref, gate_ref, up_ref, refs = refs[0], refs[1], refs[2], refs[3:]
        if finish:
            sum_before, square_before, out_ref = refs
        else:
            sum_ref, square_ref = refs
        core, first, second = spot_ref[0], spot_ref[1], spot_ref[2]
        owner = 1 - core if finish else core
        at = pl.ds(pl.multiple_of(owner * half, 128), half)
        block = jnp.concatenate([ref[...] for ref in part_refs], axis=0)
        if finish:
            wide = product(one_hot(swapped_rows(rows, line, side, first, second), rows), block)
        else:
            wide = block.astype(jnp.float32)
        squares = jnp.zeros((rows, 128), jnp.float32)
        for k in range(half // 128):
            lanes = wide[:, k * 128 : (k + 1) * 128]
            squares = squares + lanes * lanes
        scaled = (wide * gain_ref[:, at]).astype(jnp.bfloat16).T
        total = jnp.concatenate(
            [product(gate_ref[:, at], scaled), product(up_ref[:, at], scaled)], axis=0
        ).T
        if finish:
            total = total + sum_before[...]
            mean = jnp.sum(squares + square_before[...], axis=1, keepdims=True) / (2 * half)
            total = total * lax.rsqrt(mean + norm_eps)
            gate = total[:, :units]
            out_ref[...] = (gate / (1.0 + jnp.exp(-gate)) * total[:, units:]).astype(jnp.bfloat16)
        else:
            sum_ref[...] = total
            square_ref[...] = squares

    sums = [
        jax.ShapeDtypeStruct((rows, 2 * units), jnp.float32),
        jax.ShapeDtypeStruct((rows, 128), jnp.float32),
    ]
    return pl.pallas_call(
        kernel,
        in_specs=[in_smem] + [in_vmem] * (side + 3 + 2 * finish),
        out_specs=in_vmem if finish else [in_vmem] * 2,
        out_shape=jax.ShapeDtypeStruct((rows, units), jnp.bfloat16) if finish else sums,
        compiler_params=budget(24),
        cost_estimate=pl.CostEstimate(
            flops=4 * rows * half * units, bytes_accessed=4 * half * units, transcendentals=0
        ),
    )(spot, *parts, gain[None, :], gate_weight.T, up_weight.T, *(before or []))


def swapped_rows(rows, line, side, first, second):
    chip_slots = line // side
    to = line_numbers(rows)
    along = (to // line + first) % side
    beside = to // chip_slots % side
    return ((beside - second + side) % side) * line + along * chip_slots + to % chip_slots


def feed_forward(inner, inner_other, pieces, spot, side):
    rows, units = inner.shape
    cut = pieces[0].shape[1]
    line = rows // side

    def kernel(spot_ref, inner_ref, other_ref, a_ref, b_ref, c_ref, d_ref, *outs):
        core, first, second, layer = spot_ref[0], spot_ref[1], spot_ref[2], spot_ref[3]
        pick = one_hot(swapped_rows(rows, line, side, first, second), rows)
        other = product(pick, other_ref[...]).astype(jnp.bfloat16)
        mine = inner_ref[...]
        same = core == layer % 2
        even = jnp.where(same, mine, other)
        odd = jnp.where(same, other, mine)
        for start, first_ref, second_ref in ((0, a_ref, b_ref), (cut, c_ref, d_ref)):
            result = product(even, first_ref[...]) + product(odd, second_ref[...])
            result = result.astype(jnp.bfloat16)
            for k in range(side):
                outs[k][:, start : start + cut] = result[k * line : (k + 1) * line]

    return pl.pallas_call(
        kernel,
        in_specs=[in_smem] + [in_vmem] * 6,
        out_specs=[in_vmem] * side,
        out_shape=[jax.ShapeDtypeStruct((line, 2 * cut), jnp.bfloat16)] * side,
        compiler_params=budget(24),
        cost_estimate=pl.CostEstimate(
            flops=8 * rows * units * cut, bytes_accessed=8 * units * cut, transcendentals=0
        ),
    )(spot, inner, inner_other, *pieces)


def on_device(
    layer_input,
    query,
    cache,
    lengths,
    counts,
    value_weight,
    output_weight,
    norm_gain,
    gate_weight,
    up_weight,
    down_weight,
    width,
):
    slots, model = layer_input.shape
    half = model // 2
    chips = width // 2

    heads_here, latent_width, head = value_weight.shape
    side = math.isqrt(chips)
    chip_slots = 2 * slots
    line = side * chip_slots
    place = lax.axis_index("tp")
    core = place % 2
    upper = core == 1
    at_y, at_x = place // (2 * side), place // 2 % side
    first, second = jnp.where(upper, at_x, at_y), jnp.where(upper, at_y, at_x)
    layer = lax.axis_index("dp")
    spot = jnp.stack([core, first, second, layer])

    pieces = down_pieces(down_weight, width)
    value_other = core_swap(value_weight, width)
    output_other = core_swap(output_weight, width)
    input_mine = lax.dynamic_slice_in_dim(layer_input, core * half, half, 1)
    input_other = core_swap(
        lax.dynamic_slice_in_dim(layer_input, (1 - core) * half, half, 1), width
    )
    input_chip = jnp.where(
        upper,
        jnp.concatenate([input_other, input_mine], axis=0),
        jnp.concatenate([input_mine, input_other], axis=0),
    ).astype(jnp.float32)

    latent = attend(query, cache, lengths, counts, latent_width, chips)
    arrived = between_chips(latent, width)
    arrived, pieces[0], pieces[1] = lax.optimization_barrier((arrived, pieces[0], pieces[1]))
    arrived_other = core_swap(arrived, width)
    attended_parts = project(
        arrived,
        arrived_other,
        value_weight,
        value_other,
        output_weight,
        output_other,
        spot,
        side,
        slots,
    )

    summed = total(turn(attended_parts, 0, side, 1)).reshape(side, chip_slots, half)
    own_rows = (jnp.arange(side) == second)[:, None, None]
    summed = summed + jnp.where(own_rows, input_chip[None], 0.0)
    summed = summed.astype(jnp.bfloat16).reshape(line, half)
    summed, pieces[2], pieces[3] = lax.optimization_barrier((summed, pieces[2], pieces[3]))
    residual_line = total(turn([summed] * side, 1, side, 1)).astype(jnp.bfloat16)
    residual_mine = turn([residual_line] * side, 0, side, -1)
    residual_mine = lax.optimization_barrier(residual_mine)
    residual_other = [core_swap(part, width) for part in residual_mine]
    sums = gated(residual_mine, norm_gain, gate_weight, up_weight, spot, None)
    inner = gated(residual_other, norm_gain, gate_weight, up_weight, spot, sums)
    inner_other = core_swap(inner, width)

    feed_parts = feed_forward(inner, inner_other, pieces, spot, side)
    feed_line = total(turn(feed_parts, 0, side, 1)).astype(jnp.bfloat16)
    feed = total(
        turn(
            [
                lax.dynamic_slice_in_dim(
                    feed_line, (second + k) % side * chip_slots, chip_slots, 0
                )
                for k in range(side)
            ],
            1,
            side,
            1,
        )
    )
    residual = lax.dynamic_slice_in_dim(residual_line, second * chip_slots, chip_slots, 0)
    cut = half // 2
    feed = jnp.where(
        layer // 2 == 1, jnp.concatenate([feed[:, cut:], feed[:, :cut]], axis=1), feed
    )
    mixed = (residual.astype(jnp.float32) + feed).astype(jnp.bfloat16)
    kept = lax.dynamic_slice_in_dim(mixed, core * slots, slots, 0)
    got = core_swap(lax.dynamic_slice_in_dim(mixed, (1 - core) * slots, slots, 0), width)
    out = jnp.where(
        upper,
        jnp.concatenate([got, kept], axis=1),
        jnp.concatenate([kept, got], axis=1),
    )
    live = jnp.arange(slots, dtype=jnp.int32) < counts[0]
    return jnp.where(live[:, None], out, jnp.bfloat16(0.0))


def solution(mesh):
    placed = (
        P(("dp", "tp"), None),
        P(("dp", "tp"), None, None),
        P(("dp", "tp"), None, None),
        P(("dp", "tp")),
        P(("dp", "tp")),
        P("tp", None, None),
        P("tp", None),
        P(),
        P(None, "tp"),
        P(None, "tp"),
        P("tp", "dp"),
    )
    width = mesh.shape["tp"]
    return jax.shard_map(
        lambda *args: on_device(*args, width),
        mesh=mesh,
        in_specs=placed,
        out_specs=P(("dp", "tp"), None),
        check_vma=False,
    )
```

```python
import math

import jax
import jax.numpy as jnp
from jax import lax
from jax.experimental import pallas as pl
from jax.experimental.pallas import tpu as pltpu
from jax.sharding import PartitionSpec as P

score_scale = 1.0 / 192.0**0.5
norm_eps = 1e-06


def core_swap(x, width):
    return lax.ppermute(x, "tp", [(i, i ^ 1) for i in range(width)])


def between_chips(x, width):
    groups = [[2 * chip + core for chip in range(width // 2)] for core in range(2)]
    return lax.all_to_all(x, "tp", 0, 0, tiled=True, axis_index_groups=groups)


def turn(parts, axis, side, sign):
    out = [parts[0]]
    for k in range(1, side):
        pairs = []
        for y in range(side):
            for x in range(side):
                for core in range(2):
                    if axis == core:
                        to = ((y + sign * k) % side) * side + x
                    else:
                        to = y * side + (x + sign * k) % side
                    pairs.append(((y * side + x) * 2 + core, to * 2 + core))
        out.append(lax.ppermute(parts[k], "tp", pairs))
    return out


def total(parts):
    wide = parts[0].astype(jnp.float32)
    for part in parts[1:]:
        wide = wide + part.astype(jnp.float32)
    return wide


def down_piece(down_weight, width, k):
    pairs = []
    for layer in range(4):
        for place in range(width):
            chip, core = divmod(place, 2)
            cut, row_core = (layer >> 1) ^ (k >> 1), (layer & 1) ^ (k & 1)
            pairs.append(((2 * core + cut) * width + 2 * chip + row_core, layer * width + place))
    return lax.ppermute(down_weight, ("dp", "tp"), pairs)


in_vmem = pl.BlockSpec(memory_space=pltpu.VMEM)
in_hbm = pl.BlockSpec(memory_space=pltpu.HBM)
in_smem = pl.BlockSpec(memory_space=pltpu.SMEM)
across = (((1,), (1,)), ((), ()))


def product(a, b):
    return jnp.dot(a, b, preferred_element_type=jnp.float32)


def one_hot(source, columns):
    hit = source == lax.broadcasted_iota(jnp.int32, (source.shape[0], columns), 1)
    return jnp.where(hit, 1.0, 0.0).astype(jnp.bfloat16)


def line_numbers(rows):
    return lax.broadcasted_iota(jnp.int32, (rows, 1), 0)


def budget(mib):
    return pltpu.CompilerParams(vmem_limit_bytes=mib * 2**20)


def attend(query, cache, lengths, counts, latent_width, chips):
    slots, heads, wide = query.shape
    ctx = cache.shape[1]
    group = heads // chips
    rows = slots * heads

    def kernel(lengths_ref, counts_ref, q_ref, cache_ref, out_ref, held_ref, sems):
        copies = [
            pltpu.make_async_copy(cache_ref.at[slot], held_ref.at[slot], sems.at[slot])
            for slot in range(slots)
        ]

        def score(slot):
            copies[slot].wait()
            place = lax.broadcasted_iota(jnp.int32, (heads, ctx), 1)
            found = product(q_ref[slot], held_ref[slot]) * score_scale
            return jnp.where(place < lengths_ref[slot], found, -1e30)

        def gather(slot, scores):
            raised = jnp.exp(scores - jnp.max(scores, axis=1, keepdims=True))
            latent = lax.dot_general(
                raised.astype(jnp.bfloat16),
                held_ref[slot, :latent_width],
                across,
                preferred_element_type=jnp.float32,
            )
            latent = latent / jnp.sum(raised, axis=1, keepdims=True)
            return jnp.where(slot < counts_ref[0], latent, 0.0).astype(jnp.bfloat16)

        copies[0].start()
        copies[1].start()
        latents = []
        scores = score(0)
        for slot in range(slots):
            if slot + 2 < slots:
                copies[slot + 2].start()
            following = score(slot + 1) if slot + 1 < slots else None
            latents.append(gather(slot, scores))
            scores = following
        to = line_numbers(rows)
        source = to // group % slots * heads + to // (slots * group) * group + to % group
        out_ref[...] = product(
            one_hot(source, rows), jnp.concatenate(latents, axis=0)
        ).astype(jnp.bfloat16)

    out = pl.pallas_call(
        kernel,
        in_specs=[in_smem, in_smem, in_vmem, in_hbm],
        out_specs=in_vmem,
        out_shape=jax.ShapeDtypeStruct((rows, latent_width), jnp.bfloat16),
        scratch_shapes=[
            pltpu.VMEM((slots, wide, ctx), jnp.bfloat16),
            pltpu.SemaphoreType.DMA((slots,)),
        ],
        compiler_params=budget(57),
        cost_estimate=pl.CostEstimate(
            flops=2 * rows * ctx * (wide + latent_width),
            bytes_accessed=2 * cache.size,
            transcendentals=rows * ctx,
        ),
    )(lengths, counts, query, jnp.swapaxes(cache, 1, 2))
    return out.reshape(chips, slots * group, latent_width)


def project(mine, other, value_mine, value_other, output_mine, output_other, spot, side, slots):
    chips, pairs, latent_width = mine.shape
    heads_here, _, head = value_mine.shape
    heads = 2 * heads_here
    depth, model = output_mine.shape
    half = model // 2
    rows = 2 * chips * slots
    line = rows // side
    lines = chips * pairs

    def kernel(spot_ref, mine_ref, other_ref, vm_ref, vo_ref, om_ref, oo_ref, *outs):
        core, first = spot_ref[0], spot_ref[1]
        to = line_numbers(rows)
        along = (to // line + first) % side
        second = to // (2 * slots) % side
        chip = jnp.where(core == 0, along * side + second, second * side + along)
        from_other = (to // slots % 2 + core) % 2
        source = from_other * lines + chip * pairs + to % slots * heads
        latents = jnp.concatenate([mine_ref[...], other_ref[...]], axis=0)
        values = []
        for index in range(heads):
            owner, weight_ref = (core, vm_ref) if index < heads_here else (1 - core, vo_ref)
            place = index % heads_here
            pick = one_hot(source + owner * heads_here + place, 2 * lines)
            picked = product(pick, latents).astype(jnp.bfloat16)
            values.append(product(picked, weight_ref[place]).astype(jnp.bfloat16))
        values = jnp.concatenate(values, axis=1)
        at = pl.ds(pl.multiple_of(core * half, 128), half)
        result = product(values[:, :depth], om_ref[:, at]) + product(values[:, depth:], oo_ref[:, at])
        result = result.astype(jnp.bfloat16)
        for k in range(side):
            outs[k][...] = result[k * line : (k + 1) * line]

    return pl.pallas_call(
        kernel,
        in_specs=[in_smem] + [in_vmem] * 6,
        out_specs=[in_vmem] * side,
        out_shape=[jax.ShapeDtypeStruct((line, half), jnp.bfloat16)] * side,
        compiler_params=budget(24),
        cost_estimate=pl.CostEstimate(
            flops=4 * rows * depth * half, bytes_accessed=4 * depth * half, transcendentals=0
        ),
    )(
        spot,
        mine.reshape(lines, latent_width),
        other.reshape(lines, latent_width),
        value_mine,
        value_other,
        output_mine,
        output_other,
    )


def gated(parts, gain, gate_weight, up_weight, spot, before):
    side = len(parts)
    line, half = parts[0].shape
    rows = side * line
    units = gate_weight.shape[1]
    finish = before is not None

    def kernel(spot_ref, *refs):
        part_refs, refs = refs[:side], refs[side:]
        gain_ref, gate_ref, up_ref, refs = refs[0], refs[1], refs[2], refs[3:]
        if finish:
            sum_before, square_before, out_ref = refs
        else:
            sum_ref, square_ref = refs
        core, first, second = spot_ref[0], spot_ref[1], spot_ref[2]
        owner = 1 - core if finish else core
        at = pl.ds(pl.multiple_of(owner * half, 128), half)
        block = jnp.concatenate([ref[...] for ref in part_refs], axis=0)
        if finish:
            wide = product(one_hot(swapped_rows(rows, line, side, first, second), rows), block)
        else:
            wide = block.astype(jnp.float32)
        squares = jnp.zeros((rows, 128), jnp.float32)
        for k in range(half // 128):
            lanes = wide[:, k * 128 : (k + 1) * 128]
            squares = squares + lanes * lanes
        scaled = (wide * gain_ref[:, at]).astype(jnp.bfloat16).T
        total = jnp.concatenate(
            [product(gate_ref[:, at], scaled), product(up_ref[:, at], scaled)], axis=0
        ).T
        if finish:
            total = total + sum_before[...]
            mean = jnp.sum(squares + square_before[...], axis=1, keepdims=True) / (2 * half)
            total = total * lax.rsqrt(mean + norm_eps)
            gate = total[:, :units]
            out_ref[...] = (gate / (1.0 + jnp.exp(-gate)) * total[:, units:]).astype(jnp.bfloat16)
        else:
            sum_ref[...] = total
            square_ref[...] = squares

    sums = [
        jax.ShapeDtypeStruct((rows, 2 * units), jnp.float32),
        jax.ShapeDtypeStruct((rows, 128), jnp.float32),
    ]
    return pl.pallas_call(
        kernel,
        in_specs=[in_smem] + [in_vmem] * (side + 3 + 2 * finish),
        out_specs=in_vmem if finish else [in_vmem] * 2,
        out_shape=jax.ShapeDtypeStruct((rows, units), jnp.bfloat16) if finish else sums,
        compiler_params=budget(24),
        cost_estimate=pl.CostEstimate(
            flops=4 * rows * half * units, bytes_accessed=4 * half * units, transcendentals=0
        ),
    )(spot, *parts, gain[None, :], gate_weight.T, up_weight.T, *(before or []))


def swapped_rows(rows, line, side, first, second):
    chip_slots = line // side
    to = line_numbers(rows)
    along = (to // line + first) % side
    beside = to // chip_slots % side
    return ((beside - second + side) % side) * line + along * chip_slots + to % chip_slots


def feed_forward(inner, inner_other, pieces, spot, side):
    rows, units = inner.shape
    cut = pieces[0].shape[1]
    line = rows // side

    def kernel(spot_ref, inner_ref, other_ref, a_ref, b_ref, c_ref, d_ref, *outs):
        core, first, second, layer = spot_ref[0], spot_ref[1], spot_ref[2], spot_ref[3]
        pick = one_hot(swapped_rows(rows, line, side, first, second), rows)
        other = product(pick, other_ref[...]).astype(jnp.bfloat16)
        mine = inner_ref[...]
        same = core == layer % 2
        even = jnp.where(same, mine, other)
        odd = jnp.where(same, other, mine)
        for start, first_ref, second_ref in ((0, a_ref, b_ref), (cut, c_ref, d_ref)):
            result = product(even, first_ref[...]) + product(odd, second_ref[...])
            result = result.astype(jnp.bfloat16)
            for k in range(side):
                outs[k][:, start : start + cut] = result[k * line : (k + 1) * line]

    return pl.pallas_call(
        kernel,
        in_specs=[in_smem] + [in_vmem] * 6,
        out_specs=[in_vmem] * side,
        out_shape=[jax.ShapeDtypeStruct((line, 2 * cut), jnp.bfloat16)] * side,
        compiler_params=budget(24),
        cost_estimate=pl.CostEstimate(
            flops=8 * rows * units * cut, bytes_accessed=8 * units * cut, transcendentals=0
        ),
    )(spot, inner, inner_other, *pieces)


def on_device(
    layer_input,
    query,
    cache,
    lengths,
    counts,
    value_weight,
    output_weight,
    norm_gain,
    gate_weight,
    up_weight,
    down_weight,
    width,
):
    slots, model = layer_input.shape
    half = model // 2
    chips = width // 2

    heads_here, latent_width, head = value_weight.shape
    side = math.isqrt(chips)
    chip_slots = 2 * slots
    line = side * chip_slots
    place = lax.axis_index("tp")
    core = place % 2
    upper = core == 1
    at_y, at_x = place // (2 * side), place // 2 % side
    first, second = jnp.where(upper, at_x, at_y), jnp.where(upper, at_y, at_x)
    layer = lax.axis_index("dp")
    spot = jnp.stack([core, first, second, layer])

    pieces = [down_piece(down_weight, width, k) for k in range(2)]
    value_other = core_swap(value_weight, width)
    output_other = core_swap(output_weight, width)
    input_mine = lax.dynamic_slice_in_dim(layer_input, core * half, half, 1)
    input_other = core_swap(
        lax.dynamic_slice_in_dim(layer_input, (1 - core) * half, half, 1), width
    )
    input_chip = jnp.where(
        upper,
        jnp.concatenate([input_other, input_mine], axis=0),
        jnp.concatenate([input_mine, input_other], axis=0),
    ).astype(jnp.float32)

    latent = attend(query, cache, lengths, counts, latent_width, chips)
    arrived = between_chips(latent, width)
    arrived, pieces[0], pieces[1] = lax.optimization_barrier((arrived, pieces[0], pieces[1]))
    arrived_other = core_swap(arrived, width)
    attended_parts = project(
        arrived,
        arrived_other,
        value_weight,
        value_other,
        output_weight,
        output_other,
        spot,
        side,
        slots,
    )

    later, attended_parts = lax.optimization_barrier((down_weight, attended_parts))
    pieces.append(down_piece(later, width, 2))
    later, pieces[2] = lax.optimization_barrier((down_weight, pieces[2]))
    pieces.append(down_piece(later, width, 3))

    summed = total(turn(attended_parts, 0, side, 1)).reshape(side, chip_slots, half)
    own_rows = (jnp.arange(side) == second)[:, None, None]
    summed = summed + jnp.where(own_rows, input_chip[None], 0.0)
    summed = summed.astype(jnp.bfloat16).reshape(line, half)
    residual_line = total(turn([summed] * side, 1, side, 1)).astype(jnp.bfloat16)
    residual_mine = turn([residual_line] * side, 0, side, -1)
    residual_mine, pieces[2], pieces[3] = lax.optimization_barrier(
        (residual_mine, pieces[2], pieces[3])
    )
    residual_other = [core_swap(part, width) for part in residual_mine]
    sums = gated(residual_mine, norm_gain, gate_weight, up_weight, spot, None)
    inner = gated(residual_other, norm_gain, gate_weight, up_weight, spot, sums)
    inner_other = core_swap(inner, width)

    feed_parts = feed_forward(inner, inner_other, pieces, spot, side)
    feed_line = total(turn(feed_parts, 0, side, 1)).astype(jnp.bfloat16)
    feed = total(
        turn(
            [
                lax.dynamic_slice_in_dim(
                    feed_line, (second + k) % side * chip_slots, chip_slots, 0
                )
                for k in range(side)
            ],
            1,
            side,
            1,
        )
    )
    residual = lax.dynamic_slice_in_dim(residual_line, second * chip_slots, chip_slots, 0)
    cut = half // 2
    feed = jnp.where(
        layer // 2 == 1, jnp.concatenate([feed[:, cut:], feed[:, :cut]], axis=1), feed
    )
    mixed = (residual.astype(jnp.float32) + feed).astype(jnp.bfloat16)
    kept = lax.dynamic_slice_in_dim(mixed, core * slots, slots, 0)
    got = core_swap(lax.dynamic_slice_in_dim(mixed, (1 - core) * slots, slots, 0), width)
    out = jnp.where(
        upper,
        jnp.concatenate([got, kept], axis=1),
        jnp.concatenate([kept, got], axis=1),
    )
    live = jnp.arange(slots, dtype=jnp.int32) < counts[0]
    return jnp.where(live[:, None], out, jnp.bfloat16(0.0))


def solution(mesh):
    placed = (
        P(("dp", "tp"), None),
        P(("dp", "tp"), None, None),
        P(("dp", "tp"), None, None),
        P(("dp", "tp")),
        P(("dp", "tp")),
        P("tp", None, None),
        P("tp", None),
        P(),
        P(None, "tp"),
        P(None, "tp"),
        P("tp", "dp"),
    )
    width = mesh.shape["tp"]
    return jax.shard_map(
        lambda *args: on_device(*args, width),
        mesh=mesh,
        in_specs=placed,
        out_specs=P(("dp", "tp"), None),
        check_vma=False,
    )
```

```python
import math

import jax
import jax.numpy as jnp
from jax import lax
from jax.experimental import pallas as pl
from jax.experimental.pallas import tpu as pltpu
from jax.sharding import PartitionSpec as P

score_scale = 1.0 / 192.0**0.5
norm_eps = 1e-06


def core_swap(x, width):
    return lax.ppermute(x, "tp", [(i, i ^ 1) for i in range(width)])


def between_chips(x, width):
    groups = [[2 * chip + core for chip in range(width // 2)] for core in range(2)]
    return lax.all_to_all(x, "tp", 0, 0, tiled=True, axis_index_groups=groups)


def turn(parts, axis, side, sign):
    out = [parts[0]]
    for k in range(1, side):
        pairs = []
        for y in range(side):
            for x in range(side):
                for core in range(2):
                    if axis == core:
                        to = ((y + sign * k) % side) * side + x
                    else:
                        to = y * side + (x + sign * k) % side
                    pairs.append(((y * side + x) * 2 + core, to * 2 + core))
        out.append(lax.ppermute(parts[k], "tp", pairs))
    return out


def total(parts):
    wide = parts[0].astype(jnp.float32)
    for part in parts[1:]:
        wide = wide + part.astype(jnp.float32)
    return wide


def down_piece(down_weight, width, k):
    pairs = []
    for layer in range(4):
        for place in range(width):
            chip, core = divmod(place, 2)
            cut, row_core = (layer >> 1) ^ (k >> 1), (layer & 1) ^ (k & 1)
            pairs.append(((2 * core + cut) * width + 2 * chip + row_core, layer * width + place))
    return lax.ppermute(down_weight, ("dp", "tp"), pairs)


in_vmem = pl.BlockSpec(memory_space=pltpu.VMEM)
in_hbm = pl.BlockSpec(memory_space=pltpu.HBM)
in_smem = pl.BlockSpec(memory_space=pltpu.SMEM)
across = (((1,), (1,)), ((), ()))


def product(a, b):
    return jnp.dot(a, b, preferred_element_type=jnp.float32)


def one_hot(source, columns):
    hit = source == lax.broadcasted_iota(jnp.int32, (source.shape[0], columns), 1)
    return jnp.where(hit, 1.0, 0.0).astype(jnp.bfloat16)


def line_numbers(rows):
    return lax.broadcasted_iota(jnp.int32, (rows, 1), 0)


def budget(mib):
    return pltpu.CompilerParams(vmem_limit_bytes=mib * 2**20)


def attend(query, cache, lengths, counts, latent_width, chips):
    slots, heads, wide = query.shape
    ctx = cache.shape[1]
    group = heads // chips
    rows = slots * heads

    def kernel(lengths_ref, counts_ref, q_ref, cache_ref, out_ref, held_ref, sems):
        copies = [
            pltpu.make_async_copy(cache_ref.at[slot], held_ref.at[slot], sems.at[slot])
            for slot in range(slots)
        ]

        def score(slot):
            copies[slot].wait()
            place = lax.broadcasted_iota(jnp.int32, (heads, ctx), 1)
            found = product(q_ref[slot], held_ref[slot]) * score_scale
            return jnp.where(place < lengths_ref[slot], found, -1e30)

        def gather(slot, scores):
            raised = jnp.exp(scores - jnp.max(scores, axis=1, keepdims=True))
            latent = lax.dot_general(
                raised.astype(jnp.bfloat16),
                held_ref[slot, :latent_width],
                across,
                preferred_element_type=jnp.float32,
            )
            latent = latent / jnp.sum(raised, axis=1, keepdims=True)
            return jnp.where(slot < counts_ref[0], latent, 0.0).astype(jnp.bfloat16)

        copies[0].start()
        copies[1].start()
        latents = []
        scores = score(0)
        for slot in range(slots):
            if slot + 2 < slots:
                copies[slot + 2].start()
            following = score(slot + 1) if slot + 1 < slots else None
            latents.append(gather(slot, scores))
            scores = following
        to = line_numbers(rows)
        source = to // group % slots * heads + to // (slots * group) * group + to % group
        out_ref[...] = product(
            one_hot(source, rows), jnp.concatenate(latents, axis=0)
        ).astype(jnp.bfloat16)

    out = pl.pallas_call(
        kernel,
        in_specs=[in_smem, in_smem, in_vmem, in_hbm],
        out_specs=in_vmem,
        out_shape=jax.ShapeDtypeStruct((rows, latent_width), jnp.bfloat16),
        scratch_shapes=[
            pltpu.VMEM((slots, wide, ctx), jnp.bfloat16),
            pltpu.SemaphoreType.DMA((slots,)),
        ],
        compiler_params=budget(57),
        cost_estimate=pl.CostEstimate(
            flops=2 * rows * ctx * (wide + latent_width),
            bytes_accessed=2 * cache.size,
            transcendentals=rows * ctx,
        ),
    )(lengths, counts, query, jnp.swapaxes(cache, 1, 2))
    return out.reshape(chips, slots * group, latent_width)


def project(mine, other, value_mine, value_other, spot, side, slots):
    chips, pairs, latent_width = mine.shape
    heads_here, _, head = value_mine.shape
    heads = 2 * heads_here
    rows = 2 * chips * slots
    line = rows // side
    lines = chips * pairs

    def kernel(spot_ref, mine_ref, other_ref, vm_ref, vo_ref, out_ref):
        core, first = spot_ref[0], spot_ref[1]
        to = line_numbers(rows)
        along = (to // line + first) % side
        second = to // (2 * slots) % side
        chip = jnp.where(core == 0, along * side + second, second * side + along)
        from_other = (to // slots % 2 + core) % 2
        source = from_other * lines + chip * pairs + to % slots * heads
        latents = jnp.concatenate([mine_ref[...], other_ref[...]], axis=0)
        for index in range(heads):
            owner, weight_ref = (core, vm_ref) if index < heads_here else (1 - core, vo_ref)
            place = index % heads_here
            pick = one_hot(source + owner * heads_here + place, 2 * lines)
            picked = product(pick, latents).astype(jnp.bfloat16)
            out_ref[:, index * head : (index + 1) * head] = product(
                picked, weight_ref[place]
            ).astype(jnp.bfloat16)

    return pl.pallas_call(
        kernel,
        in_specs=[in_smem] + [in_vmem] * 4,
        out_specs=in_vmem,
        out_shape=jax.ShapeDtypeStruct((rows, heads * head), jnp.bfloat16),
        compiler_params=budget(16),
        cost_estimate=pl.CostEstimate(
            flops=64 * rows * latent_width * (lines + head), bytes_accessed=4 * mine.size, transcendentals=0
        ),
    )(
        spot,
        mine.reshape(lines, latent_width),
        other.reshape(lines, latent_width),
        value_mine,
        value_other,
    )


def sum_heads(values, output_mine, output_other, spot, side):
    rows = values.shape[0]
    depth, model = output_mine.shape
    half = model // 2
    line = rows // side

    def kernel(spot_ref, value_ref, om_ref, oo_ref, *refs):
        outs, (held_ref, sem) = refs[:side], refs[side:]
        at = pl.ds(pl.multiple_of(spot_ref[0] * half, 128), half)
        copy = pltpu.make_async_copy(oo_ref.at[:, at], held_ref, sem)
        copy.start()
        result = product(value_ref[:, :depth], om_ref[:, at])
        copy.wait()
        result = result + product(value_ref[:, depth:], held_ref[...])
        result = result.astype(jnp.bfloat16)
        for k in range(side):
            outs[k][...] = result[k * line : (k + 1) * line]

    return pl.pallas_call(
        kernel,
        in_specs=[in_smem] + [in_vmem] * 2 + [in_hbm],
        out_specs=[in_vmem] * side,
        out_shape=[jax.ShapeDtypeStruct((line, half), jnp.bfloat16)] * side,
        scratch_shapes=[pltpu.VMEM((depth, half), jnp.bfloat16), pltpu.SemaphoreType.DMA],
        compiler_params=budget(24),
        cost_estimate=pl.CostEstimate(
            flops=4 * rows * depth * half, bytes_accessed=4 * depth * half, transcendentals=0
        ),
    )(spot, values, output_mine, output_other)


def gated(parts, gain, gate_weight, up_weight, spot, before):
    side = len(parts)
    line, half = parts[0].shape
    rows = side * line
    units = gate_weight.shape[1]
    finish = before is not None

    def kernel(spot_ref, *refs):
        part_refs, refs = refs[:side], refs[side:]
        gain_ref, gate_ref, up_ref, refs = refs[0], refs[1], refs[2], refs[3:]
        if finish:
            sum_before, square_before, out_ref = refs
        else:
            sum_ref, square_ref = refs
        core, first, second = spot_ref[0], spot_ref[1], spot_ref[2]
        owner = 1 - core if finish else core
        at = pl.ds(pl.multiple_of(owner * half, 128), half)
        block = jnp.concatenate([ref[...] for ref in part_refs], axis=0)
        if finish:
            wide = product(one_hot(swapped_rows(rows, line, side, first, second), rows), block)
        else:
            wide = block.astype(jnp.float32)
        squares = jnp.zeros((rows, 128), jnp.float32)
        for k in range(half // 128):
            lanes = wide[:, k * 128 : (k + 1) * 128]
            squares = squares + lanes * lanes
        scaled = (wide * gain_ref[:, at]).astype(jnp.bfloat16).T
        total = jnp.concatenate(
            [product(gate_ref[:, at], scaled), product(up_ref[:, at], scaled)], axis=0
        ).T
        if finish:
            total = total + sum_before[...]
            mean = jnp.sum(squares + square_before[...], axis=1, keepdims=True) / (2 * half)
            total = total * lax.rsqrt(mean + norm_eps)
            gate = total[:, :units]
            out_ref[...] = (gate / (1.0 + jnp.exp(-gate)) * total[:, units:]).astype(jnp.bfloat16)
        else:
            sum_ref[...] = total
            square_ref[...] = squares

    sums = [
        jax.ShapeDtypeStruct((rows, 2 * units), jnp.float32),
        jax.ShapeDtypeStruct((rows, 128), jnp.float32),
    ]
    return pl.pallas_call(
        kernel,
        in_specs=[in_smem] + [in_vmem] * (side + 3 + 2 * finish),
        out_specs=in_vmem if finish else [in_vmem] * 2,
        out_shape=jax.ShapeDtypeStruct((rows, units), jnp.bfloat16) if finish else sums,
        compiler_params=budget(24),
        cost_estimate=pl.CostEstimate(
            flops=4 * rows * half * units, bytes_accessed=4 * half * units, transcendentals=0
        ),
    )(spot, *parts, gain[None, :], gate_weight.T, up_weight.T, *(before or []))


def swapped_rows(rows, line, side, first, second):
    chip_slots = line // side
    to = line_numbers(rows)
    along = (to // line + first) % side
    beside = to // chip_slots % side
    return ((beside - second + side) % side) * line + along * chip_slots + to % chip_slots


def feed_forward(inner, inner_other, pieces, spot, side):
    rows, units = inner.shape
    cut = pieces[0].shape[1]
    line = rows // side

    def kernel(spot_ref, inner_ref, other_ref, a_ref, b_ref, c_ref, d_ref, *outs):
        core, first, second, layer = spot_ref[0], spot_ref[1], spot_ref[2], spot_ref[3]
        pick = one_hot(swapped_rows(rows, line, side, first, second), rows)
        other = product(pick, other_ref[...]).astype(jnp.bfloat16)
        mine = inner_ref[...]
        same = core == layer % 2
        even = jnp.where(same, mine, other)
        odd = jnp.where(same, other, mine)
        for start, first_ref, second_ref in ((0, a_ref, b_ref), (cut, c_ref, d_ref)):
            result = product(even, first_ref[...]) + product(odd, second_ref[...])
            result = result.astype(jnp.bfloat16)
            for k in range(side):
                outs[k][:, start : start + cut] = result[k * line : (k + 1) * line]

    return pl.pallas_call(
        kernel,
        in_specs=[in_smem] + [in_vmem] * 6,
        out_specs=[in_vmem] * side,
        out_shape=[jax.ShapeDtypeStruct((line, 2 * cut), jnp.bfloat16)] * side,
        compiler_params=budget(24),
        cost_estimate=pl.CostEstimate(
            flops=8 * rows * units * cut, bytes_accessed=8 * units * cut, transcendentals=0
        ),
    )(spot, inner, inner_other, *pieces)


def on_device(
    layer_input,
    query,
    cache,
    lengths,
    counts,
    value_weight,
    output_weight,
    norm_gain,
    gate_weight,
    up_weight,
    down_weight,
    width,
):
    slots, model = layer_input.shape
    half = model // 2
    chips = width // 2

    heads_here, latent_width, head = value_weight.shape
    side = math.isqrt(chips)
    chip_slots = 2 * slots
    line = side * chip_slots
    place = lax.axis_index("tp")
    core = place % 2
    upper = core == 1
    at_y, at_x = place // (2 * side), place // 2 % side
    first, second = jnp.where(upper, at_x, at_y), jnp.where(upper, at_y, at_x)
    layer = lax.axis_index("dp")
    spot = jnp.stack([core, first, second, layer])

    pieces = [down_piece(down_weight, width, k) for k in range(2)]
    value_other = core_swap(value_weight, width)
    output_other = core_swap(output_weight, width)
    input_mine = lax.dynamic_slice_in_dim(layer_input, core * half, half, 1)
    input_other = core_swap(
        lax.dynamic_slice_in_dim(layer_input, (1 - core) * half, half, 1), width
    )
    input_chip = jnp.where(
        upper,
        jnp.concatenate([input_other, input_mine], axis=0),
        jnp.concatenate([input_mine, input_other], axis=0),
    ).astype(jnp.float32)

    latent = attend(query, cache, lengths, counts, latent_width, chips)
    arrived = between_chips(latent, width)
    arrived_other = core_swap(arrived, width)
    values = project(arrived, arrived_other, value_weight, value_other, spot, side, slots)
    attended_parts = sum_heads(values, output_weight, output_other, spot, side)

    attended_parts, pieces[0], pieces[1], later = lax.optimization_barrier(
        (attended_parts, pieces[0], pieces[1], down_weight)
    )
    pieces.append(down_piece(later, width, 2))
    later, pieces[2] = lax.optimization_barrier((down_weight, pieces[2]))
    pieces.append(down_piece(later, width, 3))

    summed = total(turn(attended_parts, 0, side, 1)).reshape(side, chip_slots, half)
    own_rows = (jnp.arange(side) == second)[:, None, None]
    summed = summed + jnp.where(own_rows, input_chip[None], 0.0)
    summed = summed.astype(jnp.bfloat16).reshape(line, half)
    residual_line = total(turn([summed] * side, 1, side, 1)).astype(jnp.bfloat16)
    residual_mine = turn([residual_line] * side, 0, side, -1)
    residual_mine, pieces[2], pieces[3] = lax.optimization_barrier(
        (residual_mine, pieces[2], pieces[3])
    )
    residual_other = [core_swap(part, width) for part in residual_mine]
    sums = gated(residual_mine, norm_gain, gate_weight, up_weight, spot, None)
    inner = gated(residual_other, norm_gain, gate_weight, up_weight, spot, sums)
    inner_other = core_swap(inner, width)

    feed_parts = feed_forward(inner, inner_other, pieces, spot, side)
    feed_line = total(turn(feed_parts, 0, side, 1)).astype(jnp.bfloat16)
    feed = total(
        turn(
            [
                lax.dynamic_slice_in_dim(
                    feed_line, (second + k) % side * chip_slots, chip_slots, 0
                )
                for k in range(side)
            ],
            1,
            side,
            1,
        )
    )
    residual = lax.dynamic_slice_in_dim(residual_line, second * chip_slots, chip_slots, 0)
    cut = half // 2
    feed = jnp.where(
        layer // 2 == 1, jnp.concatenate([feed[:, cut:], feed[:, :cut]], axis=1), feed
    )
    mixed = (residual.astype(jnp.float32) + feed).astype(jnp.bfloat16)
    kept = lax.dynamic_slice_in_dim(mixed, core * slots, slots, 0)
    got = core_swap(lax.dynamic_slice_in_dim(mixed, (1 - core) * slots, slots, 0), width)
    out = jnp.where(
        upper,
        jnp.concatenate([got, kept], axis=1),
        jnp.concatenate([kept, got], axis=1),
    )
    live = jnp.arange(slots, dtype=jnp.int32) < counts[0]
    return jnp.where(live[:, None], out, jnp.bfloat16(0.0))


def solution(mesh):
    placed = (
        P(("dp", "tp"), None),
        P(("dp", "tp"), None, None),
        P(("dp", "tp"), None, None),
        P(("dp", "tp")),
        P(("dp", "tp")),
        P("tp", None, None),
        P("tp", None),
        P(),
        P(None, "tp"),
        P(None, "tp"),
        P("tp", "dp"),
    )
    width = mesh.shape["tp"]
    return jax.shard_map(
        lambda *args: on_device(*args, width),
        mesh=mesh,
        in_specs=placed,
        out_specs=P(("dp", "tp"), None),
        check_vma=False,
    )
```

```python
import math

import jax
import jax.numpy as jnp
from jax import lax
from jax.experimental import pallas as pl
from jax.experimental.pallas import tpu as pltpu
from jax.sharding import PartitionSpec as P

score_scale = 1.0 / 192.0**0.5
norm_eps = 1e-06


def core_swap(x, width):
    return lax.ppermute(x, "tp", [(i, i ^ 1) for i in range(width)])


def between_chips(x, width):
    groups = [[2 * chip + core for chip in range(width // 2)] for core in range(2)]
    return lax.all_to_all(x, "tp", 0, 0, tiled=True, axis_index_groups=groups)


def turn(parts, axis, side, sign):
    out = [parts[0]]
    for k in range(1, side):
        pairs = []
        for y in range(side):
            for x in range(side):
                for core in range(2):
                    if axis == core:
                        to = ((y + sign * k) % side) * side + x
                    else:
                        to = y * side + (x + sign * k) % side
                    pairs.append(((y * side + x) * 2 + core, to * 2 + core))
        out.append(lax.ppermute(parts[k], "tp", pairs))
    return out


def total(parts):
    wide = parts[0].astype(jnp.float32)
    for part in parts[1:]:
        wide = wide + part.astype(jnp.float32)
    return wide


def down_piece(down_weight, width, k):
    pairs = []
    for layer in range(4):
        for place in range(width):
            chip, core = divmod(place, 2)
            cut, row_core = (layer >> 1) ^ (k >> 1), (layer & 1) ^ (k & 1)
            pairs.append(((2 * core + cut) * width + 2 * chip + row_core, layer * width + place))
    return lax.ppermute(down_weight, ("dp", "tp"), pairs)


in_vmem = pl.BlockSpec(memory_space=pltpu.VMEM)
in_hbm = pl.BlockSpec(memory_space=pltpu.HBM)
in_smem = pl.BlockSpec(memory_space=pltpu.SMEM)
across = (((1,), (1,)), ((), ()))


def product(a, b):
    return jnp.dot(a, b, preferred_element_type=jnp.float32)


def one_hot(source, columns):
    hit = source == lax.broadcasted_iota(jnp.int32, (source.shape[0], columns), 1)
    return jnp.where(hit, 1.0, 0.0).astype(jnp.bfloat16)


def line_numbers(rows):
    return lax.broadcasted_iota(jnp.int32, (rows, 1), 0)


def budget(mib):
    return pltpu.CompilerParams(vmem_limit_bytes=mib * 2**20)


def attend(query, cache, lengths, counts, latent_width, chips):
    slots, heads, wide = query.shape
    ctx = cache.shape[1]
    group = heads // chips
    rows = slots * heads

    def kernel(lengths_ref, counts_ref, q_ref, cache_ref, out_ref, held_ref, sems):
        copies = [
            pltpu.make_async_copy(cache_ref.at[slot], held_ref.at[slot], sems.at[slot])
            for slot in range(slots)
        ]

        def score(slot):
            copies[slot].wait()
            place = lax.broadcasted_iota(jnp.int32, (heads, ctx), 1)
            found = product(q_ref[slot], held_ref[slot]) * score_scale
            return jnp.where(place < lengths_ref[slot], found, -1e30)

        def gather(slot, scores):
            raised = jnp.exp(scores - jnp.max(scores, axis=1, keepdims=True))
            latent = lax.dot_general(
                raised.astype(jnp.bfloat16),
                held_ref[slot, :latent_width],
                across,
                preferred_element_type=jnp.float32,
            )
            latent = latent / jnp.sum(raised, axis=1, keepdims=True)
            return jnp.where(slot < counts_ref[0], latent, 0.0).astype(jnp.bfloat16)

        copies[0].start()
        copies[1].start()
        latents = []
        scores = score(0)
        for slot in range(slots):
            if slot + 2 < slots:
                copies[slot + 2].start()
            following = score(slot + 1) if slot + 1 < slots else None
            latents.append(gather(slot, scores))
            scores = following
        to = line_numbers(rows)
        source = to // group % slots * heads + to // (slots * group) * group + to % group
        out_ref[...] = product(
            one_hot(source, rows), jnp.concatenate(latents, axis=0)
        ).astype(jnp.bfloat16)

    out = pl.pallas_call(
        kernel,
        in_specs=[in_smem, in_smem, in_vmem, in_hbm],
        out_specs=in_vmem,
        out_shape=jax.ShapeDtypeStruct((rows, latent_width), jnp.bfloat16),
        scratch_shapes=[
            pltpu.VMEM((slots, wide, ctx), jnp.bfloat16),
            pltpu.SemaphoreType.DMA((slots,)),
        ],
        compiler_params=budget(57),
        cost_estimate=pl.CostEstimate(
            flops=2 * rows * ctx * (wide + latent_width),
            bytes_accessed=2 * cache.size,
            transcendentals=rows * ctx,
        ),
    )(lengths, counts, query, jnp.swapaxes(cache, 1, 2))
    return out.reshape(chips, slots * group, latent_width)


def project(mine, other, value_mine, value_other, spot, side, slots):
    chips, pairs, latent_width = mine.shape
    heads_here, _, head = value_mine.shape
    heads = 2 * heads_here
    rows = 2 * chips * slots
    line = rows // side
    lines = chips * pairs

    def kernel(spot_ref, mine_ref, other_ref, vm_ref, vo_ref, out_ref):
        core, first = spot_ref[0], spot_ref[1]
        to = line_numbers(rows)
        along = (to // line + first) % side
        second = to // (2 * slots) % side
        chip = jnp.where(core == 0, along * side + second, second * side + along)
        from_other = (to // slots % 2 + core) % 2
        source = from_other * lines + chip * pairs + to % slots * heads
        latents = jnp.concatenate([mine_ref[...], other_ref[...]], axis=0)
        for index in range(heads):
            owner, weight_ref = (core, vm_ref) if index < heads_here else (1 - core, vo_ref)
            place = index % heads_here
            pick = one_hot(source + owner * heads_here + place, 2 * lines)
            picked = product(pick, latents).astype(jnp.bfloat16)
            out_ref[:, index * head : (index + 1) * head] = product(
                picked, weight_ref[place]
            ).astype(jnp.bfloat16)

    return pl.pallas_call(
        kernel,
        in_specs=[in_smem] + [in_vmem] * 4,
        out_specs=in_vmem,
        out_shape=jax.ShapeDtypeStruct((rows, heads * head), jnp.bfloat16),
        compiler_params=budget(16),
        cost_estimate=pl.CostEstimate(
            flops=64 * rows * latent_width * (lines + head), bytes_accessed=4 * mine.size, transcendentals=0
        ),
    )(
        spot,
        mine.reshape(lines, latent_width),
        other.reshape(lines, latent_width),
        value_mine,
        value_other,
    )


def sum_heads(values, output_mine, output_other, spot, side):
    rows = values.shape[0]
    depth, model = output_mine.shape
    half = model // 2
    line = rows // side

    def kernel(spot_ref, value_ref, om_ref, oo_ref, *refs):
        outs, (held_ref, sem) = refs[:side], refs[side:]
        at = pl.ds(pl.multiple_of(spot_ref[0] * half, 128), half)
        copy = pltpu.make_async_copy(oo_ref.at[:, at], held_ref, sem)
        copy.start()
        result = product(value_ref[:, :depth], om_ref[:, at])
        copy.wait()
        result = result + product(value_ref[:, depth:], held_ref[...])
        result = result.astype(jnp.bfloat16)
        for k in range(side):
            outs[k][...] = result[k * line : (k + 1) * line]

    return pl.pallas_call(
        kernel,
        in_specs=[in_smem] + [in_vmem] * 2 + [in_hbm],
        out_specs=[in_vmem] * side,
        out_shape=[jax.ShapeDtypeStruct((line, half), jnp.bfloat16)] * side,
        scratch_shapes=[pltpu.VMEM((depth, half), jnp.bfloat16), pltpu.SemaphoreType.DMA],
        compiler_params=budget(24),
        cost_estimate=pl.CostEstimate(
            flops=4 * rows * depth * half, bytes_accessed=4 * depth * half, transcendentals=0
        ),
    )(spot, values, output_mine, output_other)


def gated(parts, gain, gate_weight, up_weight, spot, before):
    side = len(parts)
    line, half = parts[0].shape
    rows = side * line
    units = gate_weight.shape[1]
    finish = before is not None

    def kernel(spot_ref, *refs):
        part_refs, refs = refs[:side], refs[side:]
        gain_ref, gate_ref, up_ref, refs = refs[0], refs[1], refs[2], refs[3:]
        if finish:
            sum_before, square_before, out_ref = refs
        else:
            sum_ref, square_ref = refs
        core, first, second = spot_ref[0], spot_ref[1], spot_ref[2]
        owner = 1 - core if finish else core
        at = pl.ds(pl.multiple_of(owner * half, 128), half)
        block = jnp.concatenate([ref[...] for ref in part_refs], axis=0)
        if finish:
            wide = product(one_hot(swapped_rows(rows, line, side, first, second), rows), block)
        else:
            wide = block.astype(jnp.float32)
        squares = jnp.zeros((rows, 128), jnp.float32)
        for k in range(half // 128):
            lanes = wide[:, k * 128 : (k + 1) * 128]
            squares = squares + lanes * lanes
        scaled = (wide * gain_ref[:, at]).astype(jnp.bfloat16).T
        total = jnp.concatenate(
            [product(gate_ref[:, at], scaled), product(up_ref[:, at], scaled)], axis=0
        ).T
        if finish:
            total = total + sum_before[...]
            mean = jnp.sum(squares + square_before[...], axis=1, keepdims=True) / (2 * half)
            total = total * lax.rsqrt(mean + norm_eps)
            gate = total[:, :units]
            out_ref[...] = (gate / (1.0 + jnp.exp(-gate)) * total[:, units:]).astype(jnp.bfloat16)
        else:
            sum_ref[...] = total
            square_ref[...] = squares

    sums = [
        jax.ShapeDtypeStruct((rows, 2 * units), jnp.float32),
        jax.ShapeDtypeStruct((rows, 128), jnp.float32),
    ]
    return pl.pallas_call(
        kernel,
        in_specs=[in_smem] + [in_vmem] * (side + 3 + 2 * finish),
        out_specs=in_vmem if finish else [in_vmem] * 2,
        out_shape=jax.ShapeDtypeStruct((rows, units), jnp.bfloat16) if finish else sums,
        compiler_params=budget(24),
        cost_estimate=pl.CostEstimate(
            flops=4 * rows * half * units, bytes_accessed=4 * half * units, transcendentals=0
        ),
    )(spot, *parts, gain[None, :], gate_weight.T, up_weight.T, *(before or []))


def swapped_rows(rows, line, side, first, second):
    chip_slots = line // side
    to = line_numbers(rows)
    along = (to // line + first) % side
    beside = to // chip_slots % side
    return ((beside - second + side) % side) * line + along * chip_slots + to % chip_slots


def feed_forward(inner, inner_other, pieces, spot, side):
    rows, units = inner.shape
    cut = pieces[0].shape[1]
    line = rows // side

    def kernel(spot_ref, inner_ref, other_ref, a_ref, b_ref, c_ref, d_ref, *outs):
        core, first, second, layer = spot_ref[0], spot_ref[1], spot_ref[2], spot_ref[3]
        pick = one_hot(swapped_rows(rows, line, side, first, second), rows)
        other = product(pick, other_ref[...]).astype(jnp.bfloat16)
        mine = inner_ref[...]
        same = core == layer % 2
        even = jnp.where(same, mine, other)
        odd = jnp.where(same, other, mine)
        for start, first_ref, second_ref in ((0, a_ref, b_ref), (cut, c_ref, d_ref)):
            result = product(even, first_ref[...]) + product(odd, second_ref[...])
            result = result.astype(jnp.bfloat16)
            for k in range(side):
                outs[k][:, start : start + cut] = result[k * line : (k + 1) * line]

    return pl.pallas_call(
        kernel,
        in_specs=[in_smem] + [in_vmem] * 6,
        out_specs=[in_vmem] * side,
        out_shape=[jax.ShapeDtypeStruct((line, 2 * cut), jnp.bfloat16)] * side,
        compiler_params=budget(24),
        cost_estimate=pl.CostEstimate(
            flops=8 * rows * units * cut, bytes_accessed=8 * units * cut, transcendentals=0
        ),
    )(spot, inner, inner_other, *pieces)


def on_device(
    layer_input,
    query,
    cache,
    lengths,
    counts,
    value_weight,
    output_weight,
    norm_gain,
    gate_weight,
    up_weight,
    down_weight,
    width,
):
    slots, model = layer_input.shape
    half = model // 2
    chips = width // 2

    heads_here, latent_width, head = value_weight.shape
    side = math.isqrt(chips)
    chip_slots = 2 * slots
    line = side * chip_slots
    place = lax.axis_index("tp")
    core = place % 2
    upper = core == 1
    at_y, at_x = place // (2 * side), place // 2 % side
    first, second = jnp.where(upper, at_x, at_y), jnp.where(upper, at_y, at_x)
    layer = lax.axis_index("dp")
    spot = jnp.stack([core, first, second, layer])

    pieces = [down_piece(down_weight, width, k) for k in range(2)]
    value_other = core_swap(value_weight, width)
    output_other = core_swap(output_weight, width)
    input_mine = lax.dynamic_slice_in_dim(layer_input, core * half, half, 1)
    input_other = core_swap(
        lax.dynamic_slice_in_dim(layer_input, (1 - core) * half, half, 1), width
    )
    input_chip = jnp.where(
        upper,
        jnp.concatenate([input_other, input_mine], axis=0),
        jnp.concatenate([input_mine, input_other], axis=0),
    ).astype(jnp.float32)

    latent = attend(query, cache, lengths, counts, latent_width, chips)
    arrived = between_chips(latent, width)
    arrived_other = core_swap(arrived, width)
    arrived_other, pieces[0] = lax.optimization_barrier((arrived_other, pieces[0]))
    values = project(arrived, arrived_other, value_weight, value_other, spot, side, slots)
    attended_parts = sum_heads(values, output_weight, output_other, spot, side)

    attended_parts, later = lax.optimization_barrier((attended_parts, down_weight))
    pieces.append(down_piece(later, width, 2))
    later, pieces[2] = lax.optimization_barrier((down_weight, pieces[2]))
    pieces.append(down_piece(later, width, 3))

    summed = total(turn(attended_parts, 0, side, 1)).reshape(side, chip_slots, half)
    own_rows = (jnp.arange(side) == second)[:, None, None]
    summed = summed + jnp.where(own_rows, input_chip[None], 0.0)
    summed = summed.astype(jnp.bfloat16).reshape(line, half)
    summed, pieces[1] = lax.optimization_barrier((summed, pieces[1]))
    residual_line = total(turn([summed] * side, 1, side, 1)).astype(jnp.bfloat16)
    residual_mine = turn([residual_line] * side, 0, side, -1)
    residual_mine, pieces[2], pieces[3] = lax.optimization_barrier(
        (residual_mine, pieces[2], pieces[3])
    )
    residual_other = [core_swap(part, width) for part in residual_mine]
    sums = gated(residual_mine, norm_gain, gate_weight, up_weight, spot, None)
    inner = gated(residual_other, norm_gain, gate_weight, up_weight, spot, sums)
    inner_other = core_swap(inner, width)

    feed_parts = feed_forward(inner, inner_other, pieces, spot, side)
    feed_line = total(turn(feed_parts, 0, side, 1)).astype(jnp.bfloat16)
    feed = total(
        turn(
            [
                lax.dynamic_slice_in_dim(
                    feed_line, (second + k) % side * chip_slots, chip_slots, 0
                )
                for k in range(side)
            ],
            1,
            side,
            1,
        )
    )
    residual = lax.dynamic_slice_in_dim(residual_line, second * chip_slots, chip_slots, 0)
    cut = half // 2
    feed = jnp.where(
        layer // 2 == 1, jnp.concatenate([feed[:, cut:], feed[:, :cut]], axis=1), feed
    )
    mixed = (residual.astype(jnp.float32) + feed).astype(jnp.bfloat16)
    kept = lax.dynamic_slice_in_dim(mixed, core * slots, slots, 0)
    got = core_swap(lax.dynamic_slice_in_dim(mixed, (1 - core) * slots, slots, 0), width)
    out = jnp.where(
        upper,
        jnp.concatenate([got, kept], axis=1),
        jnp.concatenate([kept, got], axis=1),
    )
    live = jnp.arange(slots, dtype=jnp.int32) < counts[0]
    return jnp.where(live[:, None], out, jnp.bfloat16(0.0))


def solution(mesh):
    placed = (
        P(("dp", "tp"), None),
        P(("dp", "tp"), None, None),
        P(("dp", "tp"), None, None),
        P(("dp", "tp")),
        P(("dp", "tp")),
        P("tp", None, None),
        P("tp", None),
        P(),
        P(None, "tp"),
        P(None, "tp"),
        P("tp", "dp"),
    )
    width = mesh.shape["tp"]
    return jax.shard_map(
        lambda *args: on_device(*args, width),
        mesh=mesh,
        in_specs=placed,
        out_specs=P(("dp", "tp"), None),
        check_vma=False,
    )
```

```python
import math

import jax
import jax.numpy as jnp
from jax import lax
from jax.experimental import pallas as pl
from jax.experimental.pallas import tpu as pltpu
from jax.sharding import PartitionSpec as P

score_scale = 1.0 / 192.0**0.5
norm_eps = 1e-06


def core_swap(x, width):
    return lax.ppermute(x, "tp", [(i, i ^ 1) for i in range(width)])


def between_chips(x, width):
    groups = [[2 * chip + core for chip in range(width // 2)] for core in range(2)]
    return lax.all_to_all(x, "tp", 0, 0, tiled=True, axis_index_groups=groups)


def turn(parts, axis, side, sign):
    out = [parts[0]]
    for k in range(1, side):
        pairs = []
        for y in range(side):
            for x in range(side):
                for core in range(2):
                    if axis == core:
                        to = ((y + sign * k) % side) * side + x
                    else:
                        to = y * side + (x + sign * k) % side
                    pairs.append(((y * side + x) * 2 + core, to * 2 + core))
        out.append(lax.ppermute(parts[k], "tp", pairs))
    return out


def total(parts):
    wide = parts[0].astype(jnp.float32)
    for part in parts[1:]:
        wide = wide + part.astype(jnp.float32)
    return wide


def down_piece(down_weight, width, k):
    pairs = []
    for layer in range(4):
        for place in range(width):
            chip, core = divmod(place, 2)
            cut, row_core = (layer >> 1) ^ (k >> 1), (layer & 1) ^ (k & 1)
            pairs.append(((2 * core + cut) * width + 2 * chip + row_core, layer * width + place))
    return lax.ppermute(down_weight, ("dp", "tp"), pairs)


in_vmem = pl.BlockSpec(memory_space=pltpu.VMEM)
in_hbm = pl.BlockSpec(memory_space=pltpu.HBM)
in_smem = pl.BlockSpec(memory_space=pltpu.SMEM)
across = (((1,), (1,)), ((), ()))


def product(a, b):
    return jnp.dot(a, b, preferred_element_type=jnp.float32)


def one_hot(source, columns):
    hit = source == lax.broadcasted_iota(jnp.int32, (source.shape[0], columns), 1)
    return jnp.where(hit, 1.0, 0.0).astype(jnp.bfloat16)


def line_numbers(rows):
    return lax.broadcasted_iota(jnp.int32, (rows, 1), 0)


def budget(mib):
    return pltpu.CompilerParams(vmem_limit_bytes=mib * 2**20)


def attend(query, cache, lengths, counts, latent_width, chips):
    slots, heads, wide = query.shape
    ctx = cache.shape[1]
    group = heads // chips
    rows = slots * heads

    def kernel(lengths_ref, counts_ref, q_ref, cache_ref, out_ref, held_ref, sems):
        copies = [
            pltpu.make_async_copy(cache_ref.at[slot], held_ref.at[slot], sems.at[slot])
            for slot in range(slots)
        ]

        def score(slot):
            copies[slot].wait()
            place = lax.broadcasted_iota(jnp.int32, (heads, ctx), 1)
            found = product(q_ref[slot], held_ref[slot]) * score_scale
            return jnp.where(place < lengths_ref[slot], found, -1e30)

        def gather(slot, scores):
            raised = jnp.exp(scores - jnp.max(scores, axis=1, keepdims=True))
            latent = lax.dot_general(
                raised.astype(jnp.bfloat16),
                held_ref[slot, :latent_width],
                across,
                preferred_element_type=jnp.float32,
            )
            latent = latent / jnp.sum(raised, axis=1, keepdims=True)
            return jnp.where(slot < counts_ref[0], latent, 0.0).astype(jnp.bfloat16)

        for copy in copies:
            copy.start()
        latents = []
        scores = score(0)
        for slot in range(slots):
            following = score(slot + 1) if slot + 1 < slots else None
            latents.append(gather(slot, scores))
            scores = following
        to = line_numbers(rows)
        source = to // group % slots * heads + to // (slots * group) * group + to % group
        out_ref[...] = product(
            one_hot(source, rows), jnp.concatenate(latents, axis=0)
        ).astype(jnp.bfloat16)

    out = pl.pallas_call(
        kernel,
        in_specs=[in_smem, in_smem, in_vmem, in_hbm],
        out_specs=in_vmem,
        out_shape=jax.ShapeDtypeStruct((rows, latent_width), jnp.bfloat16),
        scratch_shapes=[
            pltpu.VMEM((slots, wide, ctx), jnp.bfloat16),
            pltpu.SemaphoreType.DMA((slots,)),
        ],
        compiler_params=budget(57),
        cost_estimate=pl.CostEstimate(
            flops=2 * rows * ctx * (wide + latent_width),
            bytes_accessed=2 * cache.size,
            transcendentals=rows * ctx,
        ),
    )(lengths, counts, query, jnp.swapaxes(cache, 1, 2))
    return out.reshape(chips, slots * group, latent_width)


def project(mine, other, value_mine, value_other, spot, side, slots):
    chips, pairs, latent_width = mine.shape
    heads_here, _, head = value_mine.shape
    heads = 2 * heads_here
    rows = 2 * chips * slots
    line = rows // side
    lines = chips * pairs

    def kernel(spot_ref, mine_ref, other_ref, vm_ref, vo_ref, out_ref):
        core, first = spot_ref[0], spot_ref[1]
        to = line_numbers(rows)
        along = (to // line + first) % side
        second = to // (2 * slots) % side
        chip = jnp.where(core == 0, along * side + second, second * side + along)
        from_other = (to // slots % 2 + core) % 2
        source = from_other * lines + chip * pairs + to % slots * heads
        latents = jnp.concatenate([mine_ref[...], other_ref[...]], axis=0)
        for index in range(heads):
            owner, weight_ref = (core, vm_ref) if index < heads_here else (1 - core, vo_ref)
            place = index % heads_here
            pick = one_hot(source + owner * heads_here + place, 2 * lines)
            picked = product(pick, latents).astype(jnp.bfloat16)
            out_ref[:, index * head : (index + 1) * head] = product(
                picked, weight_ref[place]
            ).astype(jnp.bfloat16)

    return pl.pallas_call(
        kernel,
        in_specs=[in_smem] + [in_vmem] * 4,
        out_specs=in_vmem,
        out_shape=jax.ShapeDtypeStruct((rows, heads * head), jnp.bfloat16),
        compiler_params=budget(16),
        cost_estimate=pl.CostEstimate(
            flops=64 * rows * latent_width * (lines + head), bytes_accessed=4 * mine.size, transcendentals=0
        ),
    )(
        spot,
        mine.reshape(lines, latent_width),
        other.reshape(lines, latent_width),
        value_mine,
        value_other,
    )


def sum_heads(values, output_mine, output_other, spot, side):
    rows = values.shape[0]
    depth, model = output_mine.shape
    half = model // 2
    line = rows // side

    def kernel(spot_ref, value_ref, om_ref, oo_ref, *refs):
        outs, (held_ref, sem) = refs[:side], refs[side:]
        at = pl.ds(pl.multiple_of(spot_ref[0] * half, 128), half)
        copy = pltpu.make_async_copy(oo_ref.at[:, at], held_ref, sem)
        copy.start()
        result = product(value_ref[:, :depth], om_ref[:, at])
        copy.wait()
        result = result + product(value_ref[:, depth:], held_ref[...])
        result = result.astype(jnp.bfloat16)
        for k in range(side):
            outs[k][...] = result[k * line : (k + 1) * line]

    return pl.pallas_call(
        kernel,
        in_specs=[in_smem] + [in_vmem] * 2 + [in_hbm],
        out_specs=[in_vmem] * side,
        out_shape=[jax.ShapeDtypeStruct((line, half), jnp.bfloat16)] * side,
        scratch_shapes=[pltpu.VMEM((depth, half), jnp.bfloat16), pltpu.SemaphoreType.DMA],
        compiler_params=budget(24),
        cost_estimate=pl.CostEstimate(
            flops=4 * rows * depth * half, bytes_accessed=4 * depth * half, transcendentals=0
        ),
    )(spot, values, output_mine, output_other)


def gated(parts, gain, gate_weight, up_weight, spot, before):
    side = len(parts)
    line, half = parts[0].shape
    rows = side * line
    units = gate_weight.shape[1]
    finish = before is not None

    def kernel(spot_ref, *refs):
        part_refs, refs = refs[:side], refs[side:]
        gain_ref, gate_ref, up_ref, refs = refs[0], refs[1], refs[2], refs[3:]
        if finish:
            sum_before, square_before, out_ref = refs
        else:
            sum_ref, square_ref = refs
        core, first, second = spot_ref[0], spot_ref[1], spot_ref[2]
        owner = 1 - core if finish else core
        at = pl.ds(pl.multiple_of(owner * half, 128), half)
        block = jnp.concatenate([ref[...] for ref in part_refs], axis=0)
        if finish:
            wide = product(one_hot(swapped_rows(rows, line, side, first, second), rows), block)
        else:
            wide = block.astype(jnp.float32)
        squares = jnp.zeros((rows, 128), jnp.float32)
        for k in range(half // 128):
            lanes = wide[:, k * 128 : (k + 1) * 128]
            squares = squares + lanes * lanes
        scaled = (wide * gain_ref[:, at]).astype(jnp.bfloat16).T
        total = jnp.concatenate(
            [product(gate_ref[:, at], scaled), product(up_ref[:, at], scaled)], axis=0
        ).T
        if finish:
            total = total + sum_before[...]
            mean = jnp.sum(squares + square_before[...], axis=1, keepdims=True) / (2 * half)
            total = total * lax.rsqrt(mean + norm_eps)
            gate = total[:, :units]
            out_ref[...] = (gate / (1.0 + jnp.exp(-gate)) * total[:, units:]).astype(jnp.bfloat16)
        else:
            sum_ref[...] = total
            square_ref[...] = squares

    sums = [
        jax.ShapeDtypeStruct((rows, 2 * units), jnp.float32),
        jax.ShapeDtypeStruct((rows, 128), jnp.float32),
    ]
    return pl.pallas_call(
        kernel,
        in_specs=[in_smem] + [in_vmem] * (side + 3 + 2 * finish),
        out_specs=in_vmem if finish else [in_vmem] * 2,
        out_shape=jax.ShapeDtypeStruct((rows, units), jnp.bfloat16) if finish else sums,
        compiler_params=budget(24),
        cost_estimate=pl.CostEstimate(
            flops=4 * rows * half * units, bytes_accessed=4 * half * units, transcendentals=0
        ),
    )(spot, *parts, gain[None, :], gate_weight.T, up_weight.T, *(before or []))


def swapped_rows(rows, line, side, first, second):
    chip_slots = line // side
    to = line_numbers(rows)
    along = (to // line + first) % side
    beside = to // chip_slots % side
    return ((beside - second + side) % side) * line + along * chip_slots + to % chip_slots


def feed_forward(inner, inner_other, pieces, spot, side):
    rows, units = inner.shape
    cut = pieces[0].shape[1]
    line = rows // side

    def kernel(spot_ref, inner_ref, other_ref, a_ref, b_ref, c_ref, d_ref, *outs):
        core, first, second, layer = spot_ref[0], spot_ref[1], spot_ref[2], spot_ref[3]
        pick = one_hot(swapped_rows(rows, line, side, first, second), rows)
        other = product(pick, other_ref[...]).astype(jnp.bfloat16)
        mine = inner_ref[...]
        same = core == layer % 2
        even = jnp.where(same, mine, other)
        odd = jnp.where(same, other, mine)
        for start, first_ref, second_ref in ((0, a_ref, b_ref), (cut, c_ref, d_ref)):
            result = product(even, first_ref[...]) + product(odd, second_ref[...])
            result = result.astype(jnp.bfloat16)
            for k in range(side):
                outs[k][:, start : start + cut] = result[k * line : (k + 1) * line]

    return pl.pallas_call(
        kernel,
        in_specs=[in_smem] + [in_vmem] * 6,
        out_specs=[in_vmem] * side,
        out_shape=[jax.ShapeDtypeStruct((line, 2 * cut), jnp.bfloat16)] * side,
        compiler_params=budget(24),
        cost_estimate=pl.CostEstimate(
            flops=8 * rows * units * cut, bytes_accessed=8 * units * cut, transcendentals=0
        ),
    )(spot, inner, inner_other, *pieces)


def on_device(
    layer_input,
    query,
    cache,
    lengths,
    counts,
    value_weight,
    output_weight,
    norm_gain,
    gate_weight,
    up_weight,
    down_weight,
    width,
):
    slots, model = layer_input.shape
    half = model // 2
    chips = width // 2

    heads_here, latent_width, head = value_weight.shape
    side = math.isqrt(chips)
    chip_slots = 2 * slots
    line = side * chip_slots
    place = lax.axis_index("tp")
    core = place % 2
    upper = core == 1
    at_y, at_x = place // (2 * side), place // 2 % side
    first, second = jnp.where(upper, at_x, at_y), jnp.where(upper, at_y, at_x)
    layer = lax.axis_index("dp")
    spot = jnp.stack([core, first, second, layer])

    pieces = [down_piece(down_weight, width, k) for k in range(2)]
    value_other = core_swap(value_weight, width)
    output_other = core_swap(output_weight, width)
    input_mine = lax.dynamic_slice_in_dim(layer_input, core * half, half, 1)
    input_other = core_swap(
        lax.dynamic_slice_in_dim(layer_input, (1 - core) * half, half, 1), width
    )
    input_chip = jnp.where(
        upper,
        jnp.concatenate([input_other, input_mine], axis=0),
        jnp.concatenate([input_mine, input_other], axis=0),
    ).astype(jnp.float32)

    query, spot = lax.optimization_barrier((query, spot))
    latent = attend(query, cache, lengths, counts, latent_width, chips)
    arrived = between_chips(latent, width)
    arrived_other = core_swap(arrived, width)
    arrived_other, pieces[0] = lax.optimization_barrier((arrived_other, pieces[0]))
    values = project(arrived, arrived_other, value_weight, value_other, spot, side, slots)
    attended_parts = sum_heads(values, output_weight, output_other, spot, side)

    attended_parts, later = lax.optimization_barrier((attended_parts, down_weight))
    pieces.append(down_piece(later, width, 2))
    later, pieces[2] = lax.optimization_barrier((down_weight, pieces[2]))
    pieces.append(down_piece(later, width, 3))

    summed = total(turn(attended_parts, 0, side, 1)).reshape(side, chip_slots, half)
    own_rows = (jnp.arange(side) == second)[:, None, None]
    summed = summed + jnp.where(own_rows, input_chip[None], 0.0)
    summed = summed.astype(jnp.bfloat16).reshape(line, half)
    summed, pieces[1] = lax.optimization_barrier((summed, pieces[1]))
    residual_line = total(turn([summed] * side, 1, side, 1)).astype(jnp.bfloat16)
    residual_mine = turn([residual_line] * side, 0, side, -1)
    residual_mine = lax.optimization_barrier(residual_mine)
    residual_other = [core_swap(part, width) for part in residual_mine]
    sums = gated(residual_mine, norm_gain, gate_weight, up_weight, spot, None)
    inner = gated(residual_other, norm_gain, gate_weight, up_weight, spot, sums)
    inner, pieces[3] = lax.optimization_barrier((inner, pieces[3]))
    inner_other = core_swap(inner, width)

    feed_parts = feed_forward(inner, inner_other, pieces, spot, side)
    feed_line = total(turn(feed_parts, 0, side, 1)).astype(jnp.bfloat16)
    feed = total(
        turn(
            [
                lax.dynamic_slice_in_dim(
                    feed_line, (second + k) % side * chip_slots, chip_slots, 0
                )
                for k in range(side)
            ],
            1,
            side,
            1,
        )
    )
    residual = lax.dynamic_slice_in_dim(residual_line, second * chip_slots, chip_slots, 0)
    cut = half // 2
    feed = jnp.where(
        layer // 2 == 1, jnp.concatenate([feed[:, cut:], feed[:, :cut]], axis=1), feed
    )
    mixed = (residual.astype(jnp.float32) + feed).astype(jnp.bfloat16)
    kept = lax.dynamic_slice_in_dim(mixed, core * slots, slots, 0)
    got = core_swap(lax.dynamic_slice_in_dim(mixed, (1 - core) * slots, slots, 0), width)
    out = jnp.where(
        upper,
        jnp.concatenate([got, kept], axis=1),
        jnp.concatenate([kept, got], axis=1),
    )
    live = jnp.arange(slots, dtype=jnp.int32) < counts[0]
    return jnp.where(live[:, None], out, jnp.bfloat16(0.0))


def solution(mesh):
    placed = (
        P(("dp", "tp"), None),
        P(("dp", "tp"), None, None),
        P(("dp", "tp"), None, None),
        P(("dp", "tp")),
        P(("dp", "tp")),
        P("tp", None, None),
        P("tp", None),
        P(),
        P(None, "tp"),
        P(None, "tp"),
        P("tp", "dp"),
    )
    width = mesh.shape["tp"]
    return jax.shard_map(
        lambda *args: on_device(*args, width),
        mesh=mesh,
        in_specs=placed,
        out_specs=P(("dp", "tp"), None),
        check_vma=False,
    )
```

```python
import math

import jax
import jax.numpy as jnp
from jax import lax
from jax.experimental import pallas as pl
from jax.experimental.pallas import tpu as pltpu
from jax.sharding import PartitionSpec as P

score_scale = 1.0 / 192.0**0.5
norm_eps = 1e-06


def core_swap(x, width):
    return lax.ppermute(x, "tp", [(i, i ^ 1) for i in range(width)])


def between_chips(x, width):
    groups = [[2 * chip + core for chip in range(width // 2)] for core in range(2)]
    return lax.all_to_all(x, "tp", 0, 0, tiled=True, axis_index_groups=groups)


def turn(parts, axis, side, sign):
    out = [parts[0]]
    for k in range(1, side):
        pairs = []
        for y in range(side):
            for x in range(side):
                for core in range(2):
                    if axis != core:
                        to = ((y + sign * k) % side) * side + x
                    else:
                        to = y * side + (x + sign * k) % side
                    pairs.append(((y * side + x) * 2 + core, to * 2 + core))
        out.append(lax.ppermute(parts[k], "tp", pairs))
    return out


def total(parts):
    wide = parts[0].astype(jnp.float32)
    for part in parts[1:]:
        wide = wide + part.astype(jnp.float32)
    return wide


def down_piece(down_weight, width, k):
    pairs = []
    for layer in range(4):
        for place in range(width):
            chip, core = divmod(place, 2)
            cut, row_core = (layer >> 1) ^ (k >> 1), (layer & 1) ^ (k & 1)
            pairs.append(((2 * core + cut) * width + 2 * chip + row_core, layer * width + place))
    return lax.ppermute(down_weight, ("dp", "tp"), pairs)


in_vmem = pl.BlockSpec(memory_space=pltpu.VMEM)
in_hbm = pl.BlockSpec(memory_space=pltpu.HBM)
in_smem = pl.BlockSpec(memory_space=pltpu.SMEM)
across = (((1,), (1,)), ((), ()))


def product(a, b):
    return jnp.dot(a, b, preferred_element_type=jnp.float32)


def one_hot(source, columns):
    hit = source == lax.broadcasted_iota(jnp.int32, (source.shape[0], columns), 1)
    return jnp.where(hit, 1.0, 0.0).astype(jnp.bfloat16)


def line_numbers(rows):
    return lax.broadcasted_iota(jnp.int32, (rows, 1), 0)


def budget(mib):
    return pltpu.CompilerParams(vmem_limit_bytes=mib * 2**20)


def attend(query, cache, lengths, counts, latent_width, chips):
    slots, heads, wide = query.shape
    ctx = cache.shape[1]
    group = heads // chips
    rows = slots * heads

    def kernel(lengths_ref, counts_ref, q_ref, cache_ref, out_ref, held_ref, sems):
        copies = [
            pltpu.make_async_copy(cache_ref.at[slot], held_ref.at[slot], sems.at[slot])
            for slot in range(slots)
        ]

        def score(slot):
            copies[slot].wait()
            place = lax.broadcasted_iota(jnp.int32, (heads, ctx), 1)
            found = product(q_ref[slot], held_ref[slot]) * score_scale
            return jnp.where(place < lengths_ref[slot], found, -1e30)

        def gather(slot, scores):
            raised = jnp.exp(scores - jnp.max(scores, axis=1, keepdims=True))
            latent = lax.dot_general(
                raised.astype(jnp.bfloat16),
                held_ref[slot, :latent_width],
                across,
                preferred_element_type=jnp.float32,
            )
            latent = latent / jnp.sum(raised, axis=1, keepdims=True)
            return jnp.where(slot < counts_ref[0], latent, 0.0).astype(jnp.bfloat16)

        for copy in copies:
            copy.start()
        latents = []
        scores = score(0)
        for slot in range(slots):
            following = score(slot + 1) if slot + 1 < slots else None
            latents.append(gather(slot, scores))
            scores = following
        to = line_numbers(rows)
        source = to // group % slots * heads + to // (slots * group) * group + to % group
        out_ref[...] = product(
            one_hot(source, rows), jnp.concatenate(latents, axis=0)
        ).astype(jnp.bfloat16)

    out = pl.pallas_call(
        kernel,
        in_specs=[in_smem, in_smem, in_vmem, in_hbm],
        out_specs=in_vmem,
        out_shape=jax.ShapeDtypeStruct((rows, latent_width), jnp.bfloat16),
        scratch_shapes=[
            pltpu.VMEM((slots, wide, ctx), jnp.bfloat16),
            pltpu.SemaphoreType.DMA((slots,)),
        ],
        compiler_params=budget(57),
        cost_estimate=pl.CostEstimate(
            flops=2 * rows * ctx * (wide + latent_width),
            bytes_accessed=2 * cache.size,
            transcendentals=rows * ctx,
        ),
    )(lengths, counts, query, jnp.swapaxes(cache, 1, 2))
    return out.reshape(chips, slots * group, latent_width)


def project(mine, other, value_mine, value_other, spot, side, slots):
    chips, pairs, latent_width = mine.shape
    heads_here, _, head = value_mine.shape
    heads = 2 * heads_here
    rows = 2 * chips * slots
    line = rows // side
    lines = chips * pairs

    def kernel(spot_ref, mine_ref, other_ref, vm_ref, vo_ref, out_ref):
        core, first = spot_ref[0], spot_ref[1]
        to = line_numbers(rows)
        along = (to // line + first) % side
        second = to // (2 * slots) % side
        chip = jnp.where(core == 1, along * side + second, second * side + along)
        from_other = (to // slots % 2 + core) % 2
        source = from_other * lines + chip * pairs + to % slots * heads
        latents = jnp.concatenate([mine_ref[...], other_ref[...]], axis=0)
        for index in range(heads):
            owner, weight_ref = (core, vm_ref) if index < heads_here else (1 - core, vo_ref)
            place = index % heads_here
            pick = one_hot(source + owner * heads_here + place, 2 * lines)
            picked = product(pick, latents).astype(jnp.bfloat16)
            out_ref[:, index * head : (index + 1) * head] = product(
                picked, weight_ref[place]
            ).astype(jnp.bfloat16)

    return pl.pallas_call(
        kernel,
        in_specs=[in_smem] + [in_vmem] * 4,
        out_specs=in_vmem,
        out_shape=jax.ShapeDtypeStruct((rows, heads * head), jnp.bfloat16),
        compiler_params=budget(16),
        cost_estimate=pl.CostEstimate(
            flops=64 * rows * latent_width * (lines + head), bytes_accessed=4 * mine.size, transcendentals=0
        ),
    )(
        spot,
        mine.reshape(lines, latent_width),
        other.reshape(lines, latent_width),
        value_mine,
        value_other,
    )


def sum_heads(values, output_mine, output_other, spot, side):
    rows = values.shape[0]
    depth, model = output_mine.shape
    half = model // 2
    line = rows // side

    def kernel(spot_ref, value_ref, om_ref, oo_ref, *refs):
        outs, (held_ref, sem) = refs[:side], refs[side:]
        at = pl.ds(pl.multiple_of(spot_ref[0] * half, 128), half)
        copy = pltpu.make_async_copy(oo_ref.at[:, at], held_ref, sem)
        copy.start()
        result = product(value_ref[:, :depth], om_ref[:, at])
        copy.wait()
        result = result + product(value_ref[:, depth:], held_ref[...])
        result = result.astype(jnp.bfloat16)
        for k in range(side):
            outs[k][...] = result[k * line : (k + 1) * line]

    return pl.pallas_call(
        kernel,
        in_specs=[in_smem] + [in_vmem] * 2 + [in_hbm],
        out_specs=[in_vmem] * side,
        out_shape=[jax.ShapeDtypeStruct((line, half), jnp.bfloat16)] * side,
        scratch_shapes=[pltpu.VMEM((depth, half), jnp.bfloat16), pltpu.SemaphoreType.DMA],
        compiler_params=budget(24),
        cost_estimate=pl.CostEstimate(
            flops=4 * rows * depth * half, bytes_accessed=4 * depth * half, transcendentals=0
        ),
    )(spot, values, output_mine, output_other)


def gated(parts, gain, gate_weight, up_weight, spot, before):
    side = len(parts)
    line, half = parts[0].shape
    rows = side * line
    units = gate_weight.shape[1]
    finish = before is not None

    def kernel(spot_ref, *refs):
        part_refs, refs = refs[:side], refs[side:]
        gain_ref, gate_ref, up_ref, refs = refs[0], refs[1], refs[2], refs[3:]
        if finish:
            sum_before, square_before, out_ref = refs
        else:
            sum_ref, square_ref = refs
        core, first, second = spot_ref[0], spot_ref[1], spot_ref[2]
        owner = 1 - core if finish else core
        at = pl.ds(pl.multiple_of(owner * half, 128), half)
        block = jnp.concatenate([ref[...] for ref in part_refs], axis=0)
        if finish:
            wide = product(one_hot(swapped_rows(rows, line, side, first, second), rows), block)
        else:
            wide = block.astype(jnp.float32)
        squares = jnp.zeros((rows, 128), jnp.float32)
        for k in range(half // 128):
            lanes = wide[:, k * 128 : (k + 1) * 128]
            squares = squares + lanes * lanes
        scaled = (wide * gain_ref[:, at]).astype(jnp.bfloat16).T
        total = jnp.concatenate(
            [product(gate_ref[:, at], scaled), product(up_ref[:, at], scaled)], axis=0
        ).T
        if finish:
            total = total + sum_before[...]
            mean = jnp.sum(squares + square_before[...], axis=1, keepdims=True) / (2 * half)
            total = total * lax.rsqrt(mean + norm_eps)
            gate = total[:, :units]
            out_ref[...] = (gate / (1.0 + jnp.exp(-gate)) * total[:, units:]).astype(jnp.bfloat16)
        else:
            sum_ref[...] = total
            square_ref[...] = squares

    sums = [
        jax.ShapeDtypeStruct((rows, 2 * units), jnp.float32),
        jax.ShapeDtypeStruct((rows, 128), jnp.float32),
    ]
    return pl.pallas_call(
        kernel,
        in_specs=[in_smem] + [in_vmem] * (side + 3 + 2 * finish),
        out_specs=in_vmem if finish else [in_vmem] * 2,
        out_shape=jax.ShapeDtypeStruct((rows, units), jnp.bfloat16) if finish else sums,
        compiler_params=budget(24),
        cost_estimate=pl.CostEstimate(
            flops=4 * rows * half * units, bytes_accessed=4 * half * units, transcendentals=0
        ),
    )(spot, *parts, gain[None, :], gate_weight.T, up_weight.T, *(before or []))


def swapped_rows(rows, line, side, first, second):
    chip_slots = line // side
    to = line_numbers(rows)
    along = (to // line + first) % side
    beside = to // chip_slots % side
    return ((beside - second + side) % side) * line + along * chip_slots + to % chip_slots


def feed_forward(inner, inner_other, pieces, spot, side):
    rows, units = inner.shape
    cut = pieces[0].shape[1]
    line = rows // side

    def kernel(spot_ref, inner_ref, other_ref, a_ref, b_ref, c_ref, d_ref, *outs):
        core, first, second, layer = spot_ref[0], spot_ref[1], spot_ref[2], spot_ref[3]
        pick = one_hot(swapped_rows(rows, line, side, first, second), rows)
        other = product(pick, other_ref[...]).astype(jnp.bfloat16)
        mine = inner_ref[...]
        same = core == layer % 2
        even = jnp.where(same, mine, other)
        odd = jnp.where(same, other, mine)
        for start, first_ref, second_ref in ((0, a_ref, b_ref), (cut, c_ref, d_ref)):
            result = product(even, first_ref[...]) + product(odd, second_ref[...])
            result = result.astype(jnp.bfloat16)
            for k in range(side):
                outs[k][:, start : start + cut] = result[k * line : (k + 1) * line]

    return pl.pallas_call(
        kernel,
        in_specs=[in_smem] + [in_vmem] * 6,
        out_specs=[in_vmem] * side,
        out_shape=[jax.ShapeDtypeStruct((line, 2 * cut), jnp.bfloat16)] * side,
        compiler_params=budget(24),
        cost_estimate=pl.CostEstimate(
            flops=8 * rows * units * cut, bytes_accessed=8 * units * cut, transcendentals=0
        ),
    )(spot, inner, inner_other, *pieces)


def on_device(
    layer_input,
    query,
    cache,
    lengths,
    counts,
    value_weight,
    output_weight,
    norm_gain,
    gate_weight,
    up_weight,
    down_weight,
    width,
):
    slots, model = layer_input.shape
    half = model // 2
    chips = width // 2

    heads_here, latent_width, head = value_weight.shape
    side = math.isqrt(chips)
    chip_slots = 2 * slots
    line = side * chip_slots
    place = lax.axis_index("tp")
    core = place % 2
    upper = core == 1
    at_y, at_x = place // (2 * side), place // 2 % side
    first, second = jnp.where(upper, at_y, at_x), jnp.where(upper, at_x, at_y)
    layer = lax.axis_index("dp")
    spot = jnp.stack([core, first, second, layer])

    pieces = [down_piece(down_weight, width, k) for k in range(2)]
    value_other = core_swap(value_weight, width)
    output_other = core_swap(output_weight, width)
    input_mine = lax.dynamic_slice_in_dim(layer_input, core * half, half, 1)
    input_other = core_swap(
        lax.dynamic_slice_in_dim(layer_input, (1 - core) * half, half, 1), width
    )
    input_chip = jnp.where(
        upper,
        jnp.concatenate([input_other, input_mine], axis=0),
        jnp.concatenate([input_mine, input_other], axis=0),
    ).astype(jnp.float32)

    query, spot = lax.optimization_barrier((query, spot))
    latent = attend(query, cache, lengths, counts, latent_width, chips)
    arrived = between_chips(latent, width)
    arrived_other = core_swap(arrived, width)
    arrived_other, pieces[0] = lax.optimization_barrier((arrived_other, pieces[0]))
    values = project(arrived, arrived_other, value_weight, value_other, spot, side, slots)
    attended_parts = sum_heads(values, output_weight, output_other, spot, side)

    attended_parts, later = lax.optimization_barrier((attended_parts, down_weight))
    pieces.append(down_piece(later, width, 2))
    later, pieces[2] = lax.optimization_barrier((down_weight, pieces[2]))
    pieces.append(down_piece(later, width, 3))

    summed = total(turn(attended_parts, 0, side, 1)).reshape(side, chip_slots, half)
    own_rows = (jnp.arange(side) == second)[:, None, None]
    summed = summed + jnp.where(own_rows, input_chip[None], 0.0)
    summed = summed.astype(jnp.bfloat16).reshape(line, half)
    summed, pieces[1] = lax.optimization_barrier((summed, pieces[1]))
    residual_line = total(turn([summed] * side, 1, side, 1)).astype(jnp.bfloat16)
    residual_mine = turn([residual_line] * side, 0, side, -1)
    residual_mine = lax.optimization_barrier(residual_mine)
    residual_other = [core_swap(part, width) for part in residual_mine]
    sums = gated(residual_mine, norm_gain, gate_weight, up_weight, spot, None)
    inner = gated(residual_other, norm_gain, gate_weight, up_weight, spot, sums)
    inner, pieces[3] = lax.optimization_barrier((inner, pieces[3]))
    inner_other = core_swap(inner, width)

    feed_parts = feed_forward(inner, inner_other, pieces, spot, side)
    feed_line = total(turn(feed_parts, 0, side, 1)).astype(jnp.bfloat16)
    feed = total(
        turn(
            [
                lax.dynamic_slice_in_dim(
                    feed_line, (second + k) % side * chip_slots, chip_slots, 0
                )
                for k in range(side)
            ],
            1,
            side,
            1,
        )
    )
    residual = lax.dynamic_slice_in_dim(residual_line, second * chip_slots, chip_slots, 0)
    cut = half // 2
    feed = jnp.where(
        layer // 2 == 1, jnp.concatenate([feed[:, cut:], feed[:, :cut]], axis=1), feed
    )
    mixed = (residual.astype(jnp.float32) + feed).astype(jnp.bfloat16)
    kept = lax.dynamic_slice_in_dim(mixed, core * slots, slots, 0)
    got = core_swap(lax.dynamic_slice_in_dim(mixed, (1 - core) * slots, slots, 0), width)
    out = jnp.where(
        upper,
        jnp.concatenate([got, kept], axis=1),
        jnp.concatenate([kept, got], axis=1),
    )
    live = jnp.arange(slots, dtype=jnp.int32) < counts[0]
    return jnp.where(live[:, None], out, jnp.bfloat16(0.0))


def solution(mesh):
    placed = (
        P(("dp", "tp"), None),
        P(("dp", "tp"), None, None),
        P(("dp", "tp"), None, None),
        P(("dp", "tp")),
        P(("dp", "tp")),
        P("tp", None, None),
        P("tp", None),
        P(),
        P(None, "tp"),
        P(None, "tp"),
        P("tp", "dp"),
    )
    width = mesh.shape["tp"]
    return jax.shard_map(
        lambda *args: on_device(*args, width),
        mesh=mesh,
        in_specs=placed,
        out_specs=P(("dp", "tp"), None),
        check_vma=False,
    )
```

```python
import math

import jax
import jax.numpy as jnp
from jax import lax
from jax.experimental import pallas as pl
from jax.experimental.pallas import tpu as pltpu
from jax.sharding import PartitionSpec as P

score_scale = 1.0 / 192.0**0.5
norm_eps = 1e-06


def core_swap(x, width):
    return lax.ppermute(x, "tp", [(i, i ^ 1) for i in range(width)])


def between_chips(x, width):
    groups = [[2 * chip + core for chip in range(width // 2)] for core in range(2)]
    return lax.all_to_all(x, "tp", 0, 0, tiled=True, axis_index_groups=groups)


def turn(parts, axis, side, sign):
    out = list(parts)
    for k in sorted(range(1, side), key=lambda step: min(step, side - step)):
        pairs = []
        for y in range(side):
            for x in range(side):
                for core in range(2):
                    if axis == core:
                        to = ((y + sign * k) % side) * side + x
                    else:
                        to = y * side + (x + sign * k) % side
                    pairs.append(((y * side + x) * 2 + core, to * 2 + core))
        out[k] = lax.ppermute(parts[k], "tp", pairs)
    return out


def total(parts):
    wide = parts[0].astype(jnp.float32)
    for part in parts[1:]:
        wide = wide + part.astype(jnp.float32)
    return wide


def down_piece(down_weight, width, k):
    pairs = []
    for layer in range(4):
        for place in range(width):
            chip, core = divmod(place, 2)
            cut, row_core = (layer >> 1) ^ (k >> 1), (layer & 1) ^ (k & 1)
            pairs.append(((2 * core + cut) * width + 2 * chip + row_core, layer * width + place))
    return lax.ppermute(down_weight, ("dp", "tp"), pairs)


in_vmem = pl.BlockSpec(memory_space=pltpu.VMEM)
in_hbm = pl.BlockSpec(memory_space=pltpu.HBM)
in_smem = pl.BlockSpec(memory_space=pltpu.SMEM)
across = (((1,), (1,)), ((), ()))


def product(a, b):
    return jnp.dot(a, b, preferred_element_type=jnp.float32)


def one_hot(source, columns):
    hit = source == lax.broadcasted_iota(jnp.int32, (source.shape[0], columns), 1)
    return jnp.where(hit, 1.0, 0.0).astype(jnp.bfloat16)


def line_numbers(rows):
    return lax.broadcasted_iota(jnp.int32, (rows, 1), 0)


def budget(mib):
    return pltpu.CompilerParams(vmem_limit_bytes=mib * 2**20)


def attend(query, cache, lengths, counts, latent_width, chips):
    slots, heads, wide = query.shape
    ctx = cache.shape[1]
    group = heads // chips
    rows = slots * heads

    def kernel(lengths_ref, counts_ref, q_ref, cache_ref, out_ref, held_ref, sems):
        copies = [
            pltpu.make_async_copy(cache_ref.at[slot], held_ref.at[slot], sems.at[slot])
            for slot in range(slots)
        ]

        def score(slot):
            copies[slot].wait()
            place = lax.broadcasted_iota(jnp.int32, (heads, ctx), 1)
            found = product(q_ref[slot], held_ref[slot]) * score_scale
            return jnp.where(place < lengths_ref[slot], found, -1e30)

        def gather(slot, scores):
            raised = jnp.exp(scores - jnp.max(scores, axis=1, keepdims=True))
            latent = lax.dot_general(
                raised.astype(jnp.bfloat16),
                held_ref[slot, :latent_width],
                across,
                preferred_element_type=jnp.float32,
            )
            latent = latent / jnp.sum(raised, axis=1, keepdims=True)
            return jnp.where(slot < counts_ref[0], latent, 0.0).astype(jnp.bfloat16)

        for copy in copies:
            copy.start()
        latents = []
        scores = score(0)
        for slot in range(slots):
            following = score(slot + 1) if slot + 1 < slots else None
            latents.append(gather(slot, scores))
            scores = following
        to = line_numbers(rows)
        source = to // group % slots * heads + to // (slots * group) * group + to % group
        out_ref[...] = product(
            one_hot(source, rows), jnp.concatenate(latents, axis=0)
        ).astype(jnp.bfloat16)

    out = pl.pallas_call(
        kernel,
        in_specs=[in_smem, in_smem, in_vmem, in_hbm],
        out_specs=in_vmem,
        out_shape=jax.ShapeDtypeStruct((rows, latent_width), jnp.bfloat16),
        scratch_shapes=[
            pltpu.VMEM((slots, wide, ctx), jnp.bfloat16),
            pltpu.SemaphoreType.DMA((slots,)),
        ],
        compiler_params=budget(57),
        cost_estimate=pl.CostEstimate(
            flops=2 * rows * ctx * (wide + latent_width),
            bytes_accessed=2 * cache.size,
            transcendentals=rows * ctx,
        ),
    )(lengths, counts, query, jnp.swapaxes(cache, 1, 2))
    return out.reshape(chips, slots * group, latent_width)


def project(mine, other, value_mine, value_other, spot, side, slots):
    chips, pairs, latent_width = mine.shape
    heads_here, _, head = value_mine.shape
    heads = 2 * heads_here
    rows = 2 * chips * slots
    line = rows // side
    lines = chips * pairs

    def kernel(spot_ref, mine_ref, other_ref, vm_ref, vo_ref, out_ref):
        core, first = spot_ref[0], spot_ref[1]
        to = line_numbers(rows)
        along = (to // line + first) % side
        second = to // (2 * slots) % side
        chip = jnp.where(core == 0, along * side + second, second * side + along)
        from_other = (to // slots % 2 + core) % 2
        source = from_other * lines + chip * pairs + to % slots * heads
        latents = jnp.concatenate([mine_ref[...], other_ref[...]], axis=0)
        for index in range(heads):
            owner, weight_ref = (core, vm_ref) if index < heads_here else (1 - core, vo_ref)
            place = index % heads_here
            pick = one_hot(source + owner * heads_here + place, 2 * lines)
            picked = product(pick, latents).astype(jnp.bfloat16)
            out_ref[:, index * head : (index + 1) * head] = product(
                picked, weight_ref[place]
            ).astype(jnp.bfloat16)

    return pl.pallas_call(
        kernel,
        in_specs=[in_smem] + [in_vmem] * 4,
        out_specs=in_vmem,
        out_shape=jax.ShapeDtypeStruct((rows, heads * head), jnp.bfloat16),
        compiler_params=budget(16),
        cost_estimate=pl.CostEstimate(
            flops=64 * rows * latent_width * (lines + head), bytes_accessed=4 * mine.size, transcendentals=0
        ),
    )(
        spot,
        mine.reshape(lines, latent_width),
        other.reshape(lines, latent_width),
        value_mine,
        value_other,
    )


def sum_heads(values, output_mine, output_other, spot, side):
    rows = values.shape[0]
    depth, model = output_mine.shape
    half = model // 2
    line = rows // side

    def kernel(spot_ref, value_ref, om_ref, oo_ref, *refs):
        outs, (held_ref, sem) = refs[:side], refs[side:]
        at = pl.ds(pl.multiple_of(spot_ref[0] * half, 128), half)
        copy = pltpu.make_async_copy(oo_ref.at[:, at], held_ref, sem)
        copy.start()
        result = product(value_ref[:, :depth], om_ref[:, at])
        copy.wait()
        result = result + product(value_ref[:, depth:], held_ref[...])
        result = result.astype(jnp.bfloat16)
        for k in range(side):
            outs[k][...] = result[k * line : (k + 1) * line]

    return pl.pallas_call(
        kernel,
        in_specs=[in_smem] + [in_vmem] * 2 + [in_hbm],
        out_specs=[in_vmem] * side,
        out_shape=[jax.ShapeDtypeStruct((line, half), jnp.bfloat16)] * side,
        scratch_shapes=[pltpu.VMEM((depth, half), jnp.bfloat16), pltpu.SemaphoreType.DMA],
        compiler_params=budget(24),
        cost_estimate=pl.CostEstimate(
            flops=4 * rows * depth * half, bytes_accessed=4 * depth * half, transcendentals=0
        ),
    )(spot, values, output_mine, output_other)


def gated(parts, gain, gate_weight, up_weight, spot, before):
    side = len(parts)
    line, half = parts[0].shape
    rows = side * line
    units = gate_weight.shape[1]
    finish = before is not None

    def kernel(spot_ref, *refs):
        part_refs, refs = refs[:side], refs[side:]
        gain_ref, gate_ref, up_ref, refs = refs[0], refs[1], refs[2], refs[3:]
        if finish:
            sum_before, square_before, out_ref = refs
        else:
            sum_ref, square_ref = refs
        core, first, second = spot_ref[0], spot_ref[1], spot_ref[2]
        owner = 1 - core if finish else core
        at = pl.ds(pl.multiple_of(owner * half, 128), half)
        block = jnp.concatenate([ref[...] for ref in part_refs], axis=0)
        if finish:
            wide = product(one_hot(swapped_rows(rows, line, side, first, second), rows), block)
        else:
            wide = block.astype(jnp.float32)
        squares = jnp.zeros((rows, 128), jnp.float32)
        for k in range(half // 128):
            lanes = wide[:, k * 128 : (k + 1) * 128]
            squares = squares + lanes * lanes
        scaled = (wide * gain_ref[:, at]).astype(jnp.bfloat16).T
        total = jnp.concatenate(
            [product(gate_ref[:, at], scaled), product(up_ref[:, at], scaled)], axis=0
        ).T
        if finish:
            total = total + sum_before[...]
            mean = jnp.sum(squares + square_before[...], axis=1, keepdims=True) / (2 * half)
            total = total * lax.rsqrt(mean + norm_eps)
            gate = total[:, :units]
            out_ref[...] = (gate / (1.0 + jnp.exp(-gate)) * total[:, units:]).astype(jnp.bfloat16)
        else:
            sum_ref[...] = total
            square_ref[...] = squares

    sums = [
        jax.ShapeDtypeStruct((rows, 2 * units), jnp.float32),
        jax.ShapeDtypeStruct((rows, 128), jnp.float32),
    ]
    return pl.pallas_call(
        kernel,
        in_specs=[in_smem] + [in_vmem] * (side + 3 + 2 * finish),
        out_specs=in_vmem if finish else [in_vmem] * 2,
        out_shape=jax.ShapeDtypeStruct((rows, units), jnp.bfloat16) if finish else sums,
        compiler_params=budget(24),
        cost_estimate=pl.CostEstimate(
            flops=4 * rows * half * units, bytes_accessed=4 * half * units, transcendentals=0
        ),
    )(spot, *parts, gain[None, :], gate_weight.T, up_weight.T, *(before or []))


def swapped_rows(rows, line, side, first, second):
    chip_slots = line // side
    to = line_numbers(rows)
    along = (to // line + first) % side
    beside = to // chip_slots % side
    return ((beside - second + side) % side) * line + along * chip_slots + to % chip_slots


def feed_forward(inner, inner_other, pieces, spot, side):
    rows, units = inner.shape
    cut = pieces[0].shape[1]
    line = rows // side

    def kernel(spot_ref, inner_ref, other_ref, a_ref, b_ref, c_ref, d_ref, *outs):
        core, first, second, layer = spot_ref[0], spot_ref[1], spot_ref[2], spot_ref[3]
        pick = one_hot(swapped_rows(rows, line, side, first, second), rows)
        other = product(pick, other_ref[...]).astype(jnp.bfloat16)
        mine = inner_ref[...]
        same = core == layer % 2
        even = jnp.where(same, mine, other)
        odd = jnp.where(same, other, mine)
        for start, first_ref, second_ref in ((0, a_ref, b_ref), (cut, c_ref, d_ref)):
            result = product(even, first_ref[...]) + product(odd, second_ref[...])
            result = result.astype(jnp.bfloat16)
            for k in range(side):
                outs[k][:, start : start + cut] = result[k * line : (k + 1) * line]

    return pl.pallas_call(
        kernel,
        in_specs=[in_smem] + [in_vmem] * 6,
        out_specs=[in_vmem] * side,
        out_shape=[jax.ShapeDtypeStruct((line, 2 * cut), jnp.bfloat16)] * side,
        compiler_params=budget(24),
        cost_estimate=pl.CostEstimate(
            flops=8 * rows * units * cut, bytes_accessed=8 * units * cut, transcendentals=0
        ),
    )(spot, inner, inner_other, *pieces)


def on_device(
    layer_input,
    query,
    cache,
    lengths,
    counts,
    value_weight,
    output_weight,
    norm_gain,
    gate_weight,
    up_weight,
    down_weight,
    width,
):
    slots, model = layer_input.shape
    half = model // 2
    chips = width // 2

    heads_here, latent_width, head = value_weight.shape
    side = math.isqrt(chips)
    chip_slots = 2 * slots
    line = side * chip_slots
    place = lax.axis_index("tp")
    core = place % 2
    upper = core == 1
    at_y, at_x = place // (2 * side), place // 2 % side
    first, second = jnp.where(upper, at_x, at_y), jnp.where(upper, at_y, at_x)
    layer = lax.axis_index("dp")
    spot = jnp.stack([core, first, second, layer])

    pieces = [down_piece(down_weight, width, k) for k in range(2)]
    value_other = core_swap(value_weight, width)
    output_other = core_swap(output_weight, width)
    input_mine = lax.dynamic_slice_in_dim(layer_input, core * half, half, 1)
    input_other = core_swap(
        lax.dynamic_slice_in_dim(layer_input, (1 - core) * half, half, 1), width
    )
    input_chip = jnp.where(
        upper,
        jnp.concatenate([input_other, input_mine], axis=0),
        jnp.concatenate([input_mine, input_other], axis=0),
    ).astype(jnp.float32)

    query, spot = lax.optimization_barrier((query, spot))
    latent = attend(query, cache, lengths, counts, latent_width, chips)
    arrived = between_chips(latent, width)
    arrived_other = core_swap(arrived, width)
    arrived_other, pieces[0] = lax.optimization_barrier((arrived_other, pieces[0]))
    values = project(arrived, arrived_other, value_weight, value_other, spot, side, slots)
    attended_parts = sum_heads(values, output_weight, output_other, spot, side)

    attended_parts, later = lax.optimization_barrier((attended_parts, down_weight))
    pieces.append(down_piece(later, width, 2))
    later, pieces[2] = lax.optimization_barrier((down_weight, pieces[2]))
    pieces.append(down_piece(later, width, 3))

    summed = total(turn(attended_parts, 0, side, 1)).reshape(side, chip_slots, half)
    own_rows = (jnp.arange(side) == second)[:, None, None]
    summed = summed + jnp.where(own_rows, input_chip[None], 0.0)
    summed = summed.astype(jnp.bfloat16).reshape(line, half)
    summed, pieces[1] = lax.optimization_barrier((summed, pieces[1]))
    residual_line = total(turn([summed] * side, 1, side, 1)).astype(jnp.bfloat16)
    residual_mine = turn([residual_line] * side, 0, side, -1)
    residual_mine = lax.optimization_barrier(residual_mine)
    residual_other = [core_swap(part, width) for part in residual_mine]
    sums = gated(residual_mine, norm_gain, gate_weight, up_weight, spot, None)
    inner = gated(residual_other, norm_gain, gate_weight, up_weight, spot, sums)
    inner, pieces[3] = lax.optimization_barrier((inner, pieces[3]))
    inner_other = core_swap(inner, width)

    feed_parts = feed_forward(inner, inner_other, pieces, spot, side)
    feed_line = total(turn(feed_parts, 0, side, 1)).astype(jnp.bfloat16)
    feed = total(
        turn(
            [
                lax.dynamic_slice_in_dim(
                    feed_line, (second + k) % side * chip_slots, chip_slots, 0
                )
                for k in range(side)
            ],
            1,
            side,
            1,
        )
    )
    residual = lax.dynamic_slice_in_dim(residual_line, second * chip_slots, chip_slots, 0)
    cut = half // 2
    feed = jnp.where(
        layer // 2 == 1, jnp.concatenate([feed[:, cut:], feed[:, :cut]], axis=1), feed
    )
    mixed = (residual.astype(jnp.float32) + feed).astype(jnp.bfloat16)
    kept = lax.dynamic_slice_in_dim(mixed, core * slots, slots, 0)
    got = core_swap(lax.dynamic_slice_in_dim(mixed, (1 - core) * slots, slots, 0), width)
    out = jnp.where(
        upper,
        jnp.concatenate([got, kept], axis=1),
        jnp.concatenate([kept, got], axis=1),
    )
    live = jnp.arange(slots, dtype=jnp.int32) < counts[0]
    return jnp.where(live[:, None], out, jnp.bfloat16(0.0))


def solution(mesh):
    placed = (
        P(("dp", "tp"), None),
        P(("dp", "tp"), None, None),
        P(("dp", "tp"), None, None),
        P(("dp", "tp")),
        P(("dp", "tp")),
        P("tp", None, None),
        P("tp", None),
        P(),
        P(None, "tp"),
        P(None, "tp"),
        P("tp", "dp"),
    )
    width = mesh.shape["tp"]
    return jax.shard_map(
        lambda *args: on_device(*args, width),
        mesh=mesh,
        in_specs=placed,
        out_specs=P(("dp", "tp"), None),
        check_vma=False,
    )
```

```python
import math

import jax
import jax.numpy as jnp
from jax import lax
from jax.experimental import pallas as pl
from jax.experimental.pallas import tpu as pltpu
from jax.sharding import PartitionSpec as P

score_scale = 1.0 / 192.0**0.5
norm_eps = 1e-06


def core_swap(x, width):
    return lax.ppermute(x, "tp", [(i, i ^ 1) for i in range(width)])


def between_chips(x, width):
    groups = [[2 * chip + core for chip in range(width // 2)] for core in range(2)]
    return lax.all_to_all(x, "tp", 0, 0, tiled=True, axis_index_groups=groups)


def turn(parts, axis, side, sign):
    out = list(parts)
    for k in sorted(range(1, side), key=lambda step: min(step, side - step)):
        pairs = []
        for y in range(side):
            for x in range(side):
                for core in range(2):
                    if axis == core:
                        to = ((y + sign * k) % side) * side + x
                    else:
                        to = y * side + (x + sign * k) % side
                    pairs.append(((y * side + x) * 2 + core, to * 2 + core))
        out[k] = lax.ppermute(parts[k], "tp", pairs)
    return out


def total(parts):
    wide = parts[0].astype(jnp.float32)
    for part in parts[1:]:
        wide = wide + part.astype(jnp.float32)
    return wide


def down_piece(down_weight, width, k):
    pairs = []
    for layer in range(4):
        for place in range(width):
            chip, core = divmod(place, 2)
            cut, row_core = (layer >> 1) ^ (k >> 1), (layer & 1) ^ (k & 1)
            pairs.append(((2 * core + cut) * width + 2 * chip + row_core, layer * width + place))
    return lax.ppermute(down_weight, ("dp", "tp"), pairs)


in_vmem = pl.BlockSpec(memory_space=pltpu.VMEM)
in_hbm = pl.BlockSpec(memory_space=pltpu.HBM)
in_smem = pl.BlockSpec(memory_space=pltpu.SMEM)
across = (((1,), (1,)), ((), ()))


def product(a, b):
    return jnp.dot(a, b, preferred_element_type=jnp.float32)


def one_hot(source, columns):
    hit = source == lax.broadcasted_iota(jnp.int32, (source.shape[0], columns), 1)
    return jnp.where(hit, 1.0, 0.0).astype(jnp.bfloat16)


def line_numbers(rows):
    return lax.broadcasted_iota(jnp.int32, (rows, 1), 0)


def budget(mib):
    return pltpu.CompilerParams(vmem_limit_bytes=mib * 2**20)


def attend(query, cache, lengths, counts, latent_width, chips):
    slots, heads, wide = query.shape
    ctx = cache.shape[1]
    group = heads // chips
    rows = slots * heads

    def kernel(lengths_ref, counts_ref, q_ref, cache_ref, out_ref, held_ref, sems):
        copies = [
            pltpu.make_async_copy(cache_ref.at[slot], held_ref.at[slot], sems.at[slot])
            for slot in range(slots)
        ]

        def score(slot):
            copies[slot].wait()
            place = lax.broadcasted_iota(jnp.int32, (1, ctx), 1)
            hidden = jnp.where(place < lengths_ref[slot], 0.0, -1e30)
            return product(q_ref[slot], held_ref[slot]) * (score_scale * math.log2(math.e)) + hidden

        def gather(slot, scores):
            raised = jnp.exp2(scores - jnp.max(scores, axis=1, keepdims=True))
            latent = lax.dot_general(
                raised.astype(jnp.bfloat16),
                held_ref[slot, :latent_width],
                across,
                preferred_element_type=jnp.float32,
            )
            latent = latent / jnp.sum(raised, axis=1, keepdims=True)
            return jnp.where(slot < counts_ref[0], latent, 0.0).astype(jnp.bfloat16)

        for copy in copies:
            copy.start()
        latents = []
        scores = score(0)
        for slot in range(slots):
            following = score(slot + 1) if slot + 1 < slots else None
            latents.append(gather(slot, scores))
            scores = following
        to = line_numbers(rows)
        source = to // group % slots * heads + to // (slots * group) * group + to % group
        out_ref[...] = product(
            one_hot(source, rows), jnp.concatenate(latents, axis=0)
        ).astype(jnp.bfloat16)

    out = pl.pallas_call(
        kernel,
        in_specs=[in_smem, in_smem, in_vmem, in_hbm],
        out_specs=in_vmem,
        out_shape=jax.ShapeDtypeStruct((rows, latent_width), jnp.bfloat16),
        scratch_shapes=[
            pltpu.VMEM((slots, wide, ctx), jnp.bfloat16),
            pltpu.SemaphoreType.DMA((slots,)),
        ],
        compiler_params=budget(57),
        cost_estimate=pl.CostEstimate(
            flops=2 * rows * ctx * (wide + latent_width),
            bytes_accessed=2 * cache.size,
            transcendentals=rows * ctx,
        ),
    )(lengths, counts, query, jnp.swapaxes(cache, 1, 2))
    return out.reshape(chips, slots * group, latent_width)


def project(mine, other, value_mine, value_other, spot, side, slots):
    chips, pairs, latent_width = mine.shape
    heads_here, _, head = value_mine.shape
    heads = 2 * heads_here
    rows = 2 * chips * slots
    line = rows // side
    lines = chips * pairs

    def kernel(spot_ref, mine_ref, other_ref, vm_ref, vo_ref, out_ref):
        core, first = spot_ref[0], spot_ref[1]
        to = line_numbers(rows)
        along = (to // line + first) % side
        second = to // (2 * slots) % side
        chip = jnp.where(core == 0, along * side + second, second * side + along)
        from_other = (to // slots % 2 + core) % 2
        source = from_other * lines + chip * pairs + to % slots * heads
        latents = jnp.concatenate([mine_ref[...], other_ref[...]], axis=0)
        for index in range(heads):
            owner, weight_ref = (core, vm_ref) if index < heads_here else (1 - core, vo_ref)
            place = index % heads_here
            pick = one_hot(source + owner * heads_here + place, 2 * lines)
            picked = product(pick, latents).astype(jnp.bfloat16)
            out_ref[:, index * head : (index + 1) * head] = product(
                picked, weight_ref[place]
            ).astype(jnp.bfloat16)

    return pl.pallas_call(
        kernel,
        in_specs=[in_smem] + [in_vmem] * 4,
        out_specs=in_vmem,
        out_shape=jax.ShapeDtypeStruct((rows, heads * head), jnp.bfloat16),
        compiler_params=budget(16),
        cost_estimate=pl.CostEstimate(
            flops=64 * rows * latent_width * (lines + head), bytes_accessed=4 * mine.size, transcendentals=0
        ),
    )(
        spot,
        mine.reshape(lines, latent_width),
        other.reshape(lines, latent_width),
        value_mine,
        value_other,
    )


def sum_heads(values, output_mine, output_other, spot, side):
    rows = values.shape[0]
    depth, model = output_mine.shape
    half = model // 2
    line = rows // side
    cuts = 2
    span = half // cuts

    def kernel(spot_ref, value_ref, om_ref, oo_ref, *refs):
        outs, (held_ref, sems) = refs[:side], refs[side:]
        copies = []
        for cut in range(cuts):
            start = pl.multiple_of(spot_ref[0] * half + cut * span, 128)
            copies.append(
                pltpu.make_async_copy(
                    oo_ref.at[:, pl.ds(start, span)], held_ref.at[cut], sems.at[cut]
                )
            )
            copies[-1].start()
        at = pl.ds(pl.multiple_of(spot_ref[0] * half, 128), half)
        mine = product(value_ref[:, :depth], om_ref[:, at])
        for cut in range(cuts):
            part = slice(cut * span, (cut + 1) * span)
            copies[cut].wait()
            result = mine[:, part] + product(value_ref[:, depth:], held_ref[cut])
            result = result.astype(jnp.bfloat16)
            for k in range(side):
                outs[k][:, part] = result[k * line : (k + 1) * line]

    return pl.pallas_call(
        kernel,
        in_specs=[in_smem] + [in_vmem] * 2 + [in_hbm],
        out_specs=[in_vmem] * side,
        out_shape=[jax.ShapeDtypeStruct((line, half), jnp.bfloat16)] * side,
        scratch_shapes=[
            pltpu.VMEM((cuts, depth, span), jnp.bfloat16),
            pltpu.SemaphoreType.DMA((cuts,)),
        ],
        compiler_params=budget(24),
        cost_estimate=pl.CostEstimate(
            flops=4 * rows * depth * half, bytes_accessed=4 * depth * half, transcendentals=0
        ),
    )(spot, values, output_mine, output_other)


def gated(parts, gain, gate_weight, up_weight, spot, before):
    side = len(parts)
    line, half = parts[0].shape
    rows = side * line
    units = gate_weight.shape[1]
    finish = before is not None

    def kernel(spot_ref, *refs):
        part_refs, refs = refs[:side], refs[side:]
        gain_ref, gate_ref, up_ref, refs = refs[0], refs[1], refs[2], refs[3:]
        if finish:
            sum_before, square_before, out_ref = refs
        else:
            sum_ref, square_ref = refs
        core, first, second = spot_ref[0], spot_ref[1], spot_ref[2]
        owner = 1 - core if finish else core
        at = pl.ds(pl.multiple_of(owner * half, 128), half)
        block = jnp.concatenate([ref[...] for ref in part_refs], axis=0)
        if finish:
            wide = product(one_hot(swapped_rows(rows, line, side, first, second), rows), block)
        else:
            wide = block.astype(jnp.float32)
        squares = jnp.zeros((rows, 128), jnp.float32)
        for k in range(half // 128):
            lanes = wide[:, k * 128 : (k + 1) * 128]
            squares = squares + lanes * lanes
        scaled = (wide * gain_ref[:, at]).astype(jnp.bfloat16).T
        total = jnp.concatenate(
            [product(gate_ref[:, at], scaled), product(up_ref[:, at], scaled)], axis=0
        ).T
        if finish:
            total = total + sum_before[...]
            mean = jnp.sum(squares + square_before[...], axis=1, keepdims=True) / (2 * half)
            total = total * lax.rsqrt(mean + norm_eps)
            gate = total[:, :units]
            out_ref[...] = (gate / (1.0 + jnp.exp(-gate)) * total[:, units:]).astype(jnp.bfloat16)
        else:
            sum_ref[...] = total
            square_ref[...] = squares

    sums = [
        jax.ShapeDtypeStruct((rows, 2 * units), jnp.float32),
        jax.ShapeDtypeStruct((rows, 128), jnp.float32),
    ]
    return pl.pallas_call(
        kernel,
        in_specs=[in_smem] + [in_vmem] * (side + 3 + 2 * finish),
        out_specs=in_vmem if finish else [in_vmem] * 2,
        out_shape=jax.ShapeDtypeStruct((rows, units), jnp.bfloat16) if finish else sums,
        compiler_params=budget(24),
        cost_estimate=pl.CostEstimate(
            flops=4 * rows * half * units, bytes_accessed=4 * half * units, transcendentals=0
        ),
    )(spot, *parts, gain[None, :], gate_weight.T, up_weight.T, *(before or []))


def swapped_rows(rows, line, side, first, second):
    chip_slots = line // side
    to = line_numbers(rows)
    along = (to // line + first) % side
    beside = to // chip_slots % side
    return ((beside - second + side) % side) * line + along * chip_slots + to % chip_slots


def feed_forward(inner, inner_other, pieces, spot, side):
    rows, units = inner.shape
    cut = pieces[0].shape[1]
    line = rows // side

    def kernel(spot_ref, inner_ref, other_ref, a_ref, b_ref, c_ref, d_ref, *outs):
        core, first, second, layer = spot_ref[0], spot_ref[1], spot_ref[2], spot_ref[3]
        pick = one_hot(swapped_rows(rows, line, side, first, second), rows)
        other = product(pick, other_ref[...]).astype(jnp.bfloat16)
        mine = inner_ref[...]
        same = core == layer % 2
        even = jnp.where(same, mine, other)
        odd = jnp.where(same, other, mine)
        for start, first_ref, second_ref in ((0, a_ref, b_ref), (cut, c_ref, d_ref)):
            result = product(even, first_ref[...]) + product(odd, second_ref[...])
            result = result.astype(jnp.bfloat16)
            for k in range(side):
                outs[k][:, start : start + cut] = result[k * line : (k + 1) * line]

    return pl.pallas_call(
        kernel,
        in_specs=[in_smem] + [in_vmem] * 6,
        out_specs=[in_vmem] * side,
        out_shape=[jax.ShapeDtypeStruct((line, 2 * cut), jnp.bfloat16)] * side,
        compiler_params=budget(24),
        cost_estimate=pl.CostEstimate(
            flops=8 * rows * units * cut, bytes_accessed=8 * units * cut, transcendentals=0
        ),
    )(spot, inner, inner_other, *pieces)


def on_device(
    layer_input,
    query,
    cache,
    lengths,
    counts,
    value_weight,
    output_weight,
    norm_gain,
    gate_weight,
    up_weight,
    down_weight,
    width,
):
    slots, model = layer_input.shape
    half = model // 2
    chips = width // 2

    heads_here, latent_width, head = value_weight.shape
    side = math.isqrt(chips)
    chip_slots = 2 * slots
    line = side * chip_slots
    place = lax.axis_index("tp")
    core = place % 2
    upper = core == 1
    at_y, at_x = place // (2 * side), place // 2 % side
    first, second = jnp.where(upper, at_x, at_y), jnp.where(upper, at_y, at_x)
    layer = lax.axis_index("dp")
    spot = jnp.stack([core, first, second, layer])

    pieces = [down_piece(down_weight, width, k) for k in range(2)]
    value_other = core_swap(value_weight, width)
    output_other = core_swap(output_weight, width)
    input_mine = lax.dynamic_slice_in_dim(layer_input, core * half, half, 1)
    input_other = core_swap(
        lax.dynamic_slice_in_dim(layer_input, (1 - core) * half, half, 1), width
    )
    input_chip = jnp.where(
        upper,
        jnp.concatenate([input_other, input_mine], axis=0),
        jnp.concatenate([input_mine, input_other], axis=0),
    ).astype(jnp.float32)

    query, spot = lax.optimization_barrier((query, spot))
    latent = attend(query, cache, lengths, counts, latent_width, chips)
    arrived = between_chips(latent, width)
    arrived_other = core_swap(arrived, width)
    arrived_other, pieces[0] = lax.optimization_barrier((arrived_other, pieces[0]))
    values = project(arrived, arrived_other, value_weight, value_other, spot, side, slots)
    attended_parts = sum_heads(values, output_weight, output_other, spot, side)

    attended_parts, later = lax.optimization_barrier((attended_parts, down_weight))
    pieces.append(down_piece(later, width, 2))
    later, pieces[2] = lax.optimization_barrier((down_weight, pieces[2]))
    pieces.append(down_piece(later, width, 3))

    summed = total(turn(attended_parts, 0, side, 1)).reshape(side, chip_slots, half)
    own_rows = (jnp.arange(side) == second)[:, None, None]
    summed = summed + jnp.where(own_rows, input_chip[None], 0.0)
    summed = summed.astype(jnp.bfloat16).reshape(line, half)
    summed, pieces[1] = lax.optimization_barrier((summed, pieces[1]))
    residual_line = total(turn([summed] * side, 1, side, 1)).astype(jnp.bfloat16)
    residual_mine = turn([residual_line] * side, 0, side, -1)
    residual_mine = lax.optimization_barrier(residual_mine)
    residual_other = [core_swap(part, width) for part in residual_mine]
    sums = gated(residual_mine, norm_gain, gate_weight, up_weight, spot, None)
    inner = gated(residual_other, norm_gain, gate_weight, up_weight, spot, sums)
    inner, pieces[3] = lax.optimization_barrier((inner, pieces[3]))
    inner_other = core_swap(inner, width)

    feed_parts = feed_forward(inner, inner_other, pieces, spot, side)
    feed_line = total(turn(feed_parts, 0, side, 1)).astype(jnp.bfloat16)
    feed = total(
        turn(
            [
                lax.dynamic_slice_in_dim(
                    feed_line, (second + k) % side * chip_slots, chip_slots, 0
                )
                for k in range(side)
            ],
            1,
            side,
            1,
        )
    )
    residual = lax.dynamic_slice_in_dim(residual_line, second * chip_slots, chip_slots, 0)
    cut = half // 2
    feed = jnp.where(
        layer // 2 == 1, jnp.concatenate([feed[:, cut:], feed[:, :cut]], axis=1), feed
    )
    mixed = (residual.astype(jnp.float32) + feed).astype(jnp.bfloat16)
    kept = lax.dynamic_slice_in_dim(mixed, core * slots, slots, 0)
    got = core_swap(lax.dynamic_slice_in_dim(mixed, (1 - core) * slots, slots, 0), width)
    out = jnp.where(
        upper,
        jnp.concatenate([got, kept], axis=1),
        jnp.concatenate([kept, got], axis=1),
    )
    live = jnp.arange(slots, dtype=jnp.int32) < counts[0]
    return jnp.where(live[:, None], out, jnp.bfloat16(0.0))


def solution(mesh):
    placed = (
        P(("dp", "tp"), None),
        P(("dp", "tp"), None, None),
        P(("dp", "tp"), None, None),
        P(("dp", "tp")),
        P(("dp", "tp")),
        P("tp", None, None),
        P("tp", None),
        P(),
        P(None, "tp"),
        P(None, "tp"),
        P("tp", "dp"),
    )
    width = mesh.shape["tp"]
    return jax.shard_map(
        lambda *args: on_device(*args, width),
        mesh=mesh,
        in_specs=placed,
        out_specs=P(("dp", "tp"), None),
        check_vma=False,
    )
```

```python
import math

import jax
import jax.numpy as jnp
from jax import lax
from jax.experimental import pallas as pl
from jax.experimental.pallas import tpu as pltpu
from jax.sharding import PartitionSpec as P

score_scale = 1.0 / 192.0**0.5
norm_eps = 1e-06


def core_swap(x, width):
    return lax.ppermute(x, "tp", [(i, i ^ 1) for i in range(width)])


def between_chips(x, width):
    groups = [[2 * chip + core for chip in range(width // 2)] for core in range(2)]
    return lax.all_to_all(x, "tp", 0, 0, tiled=True, axis_index_groups=groups)


def turn(parts, axis, side, sign):
    out = list(parts)
    for k in sorted(range(1, side), key=lambda step: min(step, side - step)):
        pairs = []
        for y in range(side):
            for x in range(side):
                for core in range(2):
                    if axis == core:
                        to = ((y + sign * k) % side) * side + x
                    else:
                        to = y * side + (x + sign * k) % side
                    pairs.append(((y * side + x) * 2 + core, to * 2 + core))
        out[k] = lax.ppermute(parts[k], "tp", pairs)
    return out


def total(parts):
    wide = parts[0].astype(jnp.float32)
    for part in parts[1:]:
        wide = wide + part.astype(jnp.float32)
    return wide


def down_piece(down_weight, width, k):
    pairs = []
    for layer in range(4):
        for place in range(width):
            chip, core = divmod(place, 2)
            cut, row_core = (layer >> 1) ^ (k >> 1), (layer & 1) ^ (k & 1)
            pairs.append(((2 * core + cut) * width + 2 * chip + row_core, layer * width + place))
    return lax.ppermute(down_weight, ("dp", "tp"), pairs)


in_vmem = pl.BlockSpec(memory_space=pltpu.VMEM)
in_hbm = pl.BlockSpec(memory_space=pltpu.HBM)
in_smem = pl.BlockSpec(memory_space=pltpu.SMEM)
across = (((1,), (1,)), ((), ()))


def product(a, b):
    return jnp.dot(a, b, preferred_element_type=jnp.float32)


def one_hot(source, columns):
    hit = source == lax.broadcasted_iota(jnp.int32, (source.shape[0], columns), 1)
    return jnp.where(hit, 1.0, 0.0).astype(jnp.bfloat16)


def line_numbers(rows):
    return lax.broadcasted_iota(jnp.int32, (rows, 1), 0)


def budget(mib):
    return pltpu.CompilerParams(vmem_limit_bytes=mib * 2**20)


def attend(query, cache, lengths, latent_width, chips):
    slots, heads, wide = query.shape
    ctx = cache.shape[1]
    group = heads // chips
    rows = slots * heads

    def kernel(lengths_ref, q_ref, cache_ref, out_ref, held_ref, sems):
        copies = [
            pltpu.make_async_copy(cache_ref.at[slot], held_ref.at[slot], sems.at[slot])
            for slot in range(slots)
        ]

        def score(slot):
            copies[slot].wait()
            place = lax.broadcasted_iota(jnp.int32, (1, ctx), 1)
            hidden = jnp.where(place < lengths_ref[slot], 0.0, -1e30)
            return product(q_ref[slot], held_ref[slot]) * (score_scale * math.log2(math.e)) + hidden

        def gather(slot, scores):
            raised = jnp.exp2(scores - jnp.max(scores, axis=1, keepdims=True))
            latent = lax.dot_general(
                raised.astype(jnp.bfloat16),
                held_ref[slot, :latent_width],
                across,
                preferred_element_type=jnp.float32,
            )
            latent = latent / jnp.sum(raised, axis=1, keepdims=True)
            return latent.astype(jnp.bfloat16)

        for copy in copies:
            copy.start()
        latents = []
        scores = score(0)
        for slot in range(slots):
            following = score(slot + 1) if slot + 1 < slots else None
            latents.append(gather(slot, scores))
            scores = following
        to = line_numbers(rows)
        source = to // group % slots * heads + to // (slots * group) * group + to % group
        out_ref[...] = product(
            one_hot(source, rows), jnp.concatenate(latents, axis=0)
        ).astype(jnp.bfloat16)

    out = pl.pallas_call(
        kernel,
        in_specs=[in_smem, in_vmem, in_hbm],
        out_specs=in_vmem,
        out_shape=jax.ShapeDtypeStruct((rows, latent_width), jnp.bfloat16),
        scratch_shapes=[
            pltpu.VMEM((slots, wide, ctx), jnp.bfloat16),
            pltpu.SemaphoreType.DMA((slots,)),
        ],
        compiler_params=budget(57),
        cost_estimate=pl.CostEstimate(
            flops=2 * rows * ctx * (wide + latent_width),
            bytes_accessed=2 * cache.size,
            transcendentals=rows * ctx,
        ),
    )(lengths, query, jnp.swapaxes(cache, 1, 2))
    return out.reshape(chips, slots * group, latent_width)


def project(mine, other, value_mine, value_other, spot, side, slots):
    chips, pairs, latent_width = mine.shape
    heads_here, _, head = value_mine.shape
    heads = 2 * heads_here
    rows = 2 * chips * slots
    line = rows // side
    lines = chips * pairs

    def kernel(spot_ref, mine_ref, other_ref, vm_ref, vo_ref, out_ref):
        core, first = spot_ref[0], spot_ref[1]
        to = line_numbers(rows)
        along = (to // line + first) % side
        second = to // (2 * slots) % side
        chip = jnp.where(core == 0, along * side + second, second * side + along)
        from_other = (to // slots % 2 + core) % 2
        source = from_other * lines + chip * pairs + to % slots * heads
        latents = jnp.concatenate([mine_ref[...], other_ref[...]], axis=0)
        for index in range(heads):
            owner, weight_ref = (core, vm_ref) if index < heads_here else (1 - core, vo_ref)
            place = index % heads_here
            pick = one_hot(source + owner * heads_here + place, 2 * lines)
            picked = product(pick, latents).astype(jnp.bfloat16)
            out_ref[:, index * head : (index + 1) * head] = product(
                picked, weight_ref[place]
            ).astype(jnp.bfloat16)

    return pl.pallas_call(
        kernel,
        in_specs=[in_smem] + [in_vmem] * 4,
        out_specs=in_vmem,
        out_shape=jax.ShapeDtypeStruct((rows, heads * head), jnp.bfloat16),
        compiler_params=budget(16),
        cost_estimate=pl.CostEstimate(
            flops=64 * rows * latent_width * (lines + head), bytes_accessed=4 * mine.size, transcendentals=0
        ),
    )(
        spot,
        mine.reshape(lines, latent_width),
        other.reshape(lines, latent_width),
        value_mine,
        value_other,
    )


def sum_heads(values, output_mine, output_other, spot, side):
    rows = values.shape[0]
    depth, model = output_mine.shape
    half = model // 2
    line = rows // side
    cuts = 2
    span = half // cuts

    def kernel(spot_ref, value_ref, om_ref, oo_ref, *refs):
        outs, (held_ref, sems) = refs[:side], refs[side:]
        copies = []
        for cut in range(cuts):
            start = pl.multiple_of(spot_ref[0] * half + cut * span, 128)
            copies.append(
                pltpu.make_async_copy(
                    oo_ref.at[:, pl.ds(start, span)], held_ref.at[cut], sems.at[cut]
                )
            )
            copies[-1].start()
        at = pl.ds(pl.multiple_of(spot_ref[0] * half, 128), half)
        mine = product(value_ref[:, :depth], om_ref[:, at])
        for cut in range(cuts):
            part = slice(cut * span, (cut + 1) * span)
            copies[cut].wait()
            result = mine[:, part] + product(value_ref[:, depth:], held_ref[cut])
            result = result.astype(jnp.bfloat16)
            for k in range(side):
                outs[k][:, part] = result[k * line : (k + 1) * line]

    return pl.pallas_call(
        kernel,
        in_specs=[in_smem] + [in_vmem] * 2 + [in_hbm],
        out_specs=[in_vmem] * side,
        out_shape=[jax.ShapeDtypeStruct((line, half), jnp.bfloat16)] * side,
        scratch_shapes=[
            pltpu.VMEM((cuts, depth, span), jnp.bfloat16),
            pltpu.SemaphoreType.DMA((cuts,)),
        ],
        compiler_params=budget(24),
        cost_estimate=pl.CostEstimate(
            flops=4 * rows * depth * half, bytes_accessed=4 * depth * half, transcendentals=0
        ),
    )(spot, values, output_mine, output_other)


def gated(parts, gain, gate_weight, up_weight, spot, before):
    side = len(parts)
    line, half = parts[0].shape
    rows = side * line
    units = gate_weight.shape[1]
    finish = before is not None

    def kernel(spot_ref, *refs):
        part_refs, refs = refs[:side], refs[side:]
        gain_ref, gate_ref, up_ref, refs = refs[0], refs[1], refs[2], refs[3:]
        if finish:
            sum_before, square_before, out_ref = refs
        else:
            sum_ref, square_ref = refs
        core, first, second = spot_ref[0], spot_ref[1], spot_ref[2]
        owner = 1 - core if finish else core
        at = pl.ds(pl.multiple_of(owner * half, 128), half)
        block = jnp.concatenate([ref[...] for ref in part_refs], axis=0)
        if finish:
            wide = product(one_hot(swapped_rows(rows, line, side, first, second), rows), block)
        else:
            wide = block.astype(jnp.float32)
        squares = jnp.zeros((rows, 128), jnp.float32)
        for k in range(half // 128):
            lanes = wide[:, k * 128 : (k + 1) * 128]
            squares = squares + lanes * lanes
        scaled = (wide * gain_ref[:, at]).astype(jnp.bfloat16).T
        total = jnp.concatenate(
            [product(gate_ref[:, at], scaled), product(up_ref[:, at], scaled)], axis=0
        ).T
        if finish:
            total = total + sum_before[...]
            mean = jnp.sum(squares + square_before[...], axis=1, keepdims=True) / (2 * half)
            total = total * lax.rsqrt(mean + norm_eps)
            gate = total[:, :units]
            out_ref[...] = (gate / (1.0 + jnp.exp(-gate)) * total[:, units:]).astype(jnp.bfloat16)
        else:
            sum_ref[...] = total
            square_ref[...] = squares

    sums = [
        jax.ShapeDtypeStruct((rows, 2 * units), jnp.float32),
        jax.ShapeDtypeStruct((rows, 128), jnp.float32),
    ]
    return pl.pallas_call(
        kernel,
        in_specs=[in_smem] + [in_vmem] * (side + 3 + 2 * finish),
        out_specs=in_vmem if finish else [in_vmem] * 2,
        out_shape=jax.ShapeDtypeStruct((rows, units), jnp.bfloat16) if finish else sums,
        compiler_params=budget(24),
        cost_estimate=pl.CostEstimate(
            flops=4 * rows * half * units, bytes_accessed=4 * half * units, transcendentals=0
        ),
    )(spot, *parts, gain[None, :], gate_weight.T, up_weight.T, *(before or []))


def swapped_rows(rows, line, side, first, second):
    chip_slots = line // side
    to = line_numbers(rows)
    along = (to // line + first) % side
    beside = to // chip_slots % side
    return ((beside - second + side) % side) * line + along * chip_slots + to % chip_slots


def feed_forward(inner, inner_other, pieces, spot, side):
    rows, units = inner.shape
    cut = pieces[0].shape[1]
    line = rows // side

    def kernel(spot_ref, inner_ref, other_ref, a_ref, b_ref, c_ref, d_ref, *outs):
        core, first, second, layer = spot_ref[0], spot_ref[1], spot_ref[2], spot_ref[3]
        pick = one_hot(swapped_rows(rows, line, side, first, second), rows)
        other = product(pick, other_ref[...]).astype(jnp.bfloat16)
        mine = inner_ref[...]
        same = core == layer % 2
        even = jnp.where(same, mine, other)
        odd = jnp.where(same, other, mine)
        for start, first_ref, second_ref in ((0, a_ref, b_ref), (cut, c_ref, d_ref)):
            result = product(even, first_ref[...]) + product(odd, second_ref[...])
            result = result.astype(jnp.bfloat16)
            for k in range(side):
                outs[k][:, start : start + cut] = result[k * line : (k + 1) * line]

    return pl.pallas_call(
        kernel,
        in_specs=[in_smem] + [in_vmem] * 6,
        out_specs=[in_vmem] * side,
        out_shape=[jax.ShapeDtypeStruct((line, 2 * cut), jnp.bfloat16)] * side,
        compiler_params=budget(24),
        cost_estimate=pl.CostEstimate(
            flops=8 * rows * units * cut, bytes_accessed=8 * units * cut, transcendentals=0
        ),
    )(spot, inner, inner_other, *pieces)


def on_device(
    layer_input,
    query,
    cache,
    lengths,
    counts,
    value_weight,
    output_weight,
    norm_gain,
    gate_weight,
    up_weight,
    down_weight,
    width,
):
    slots, model = layer_input.shape
    half = model // 2
    chips = width // 2

    heads_here, latent_width, head = value_weight.shape
    side = math.isqrt(chips)
    chip_slots = 2 * slots
    line = side * chip_slots
    place = lax.axis_index("tp")
    core = place % 2
    upper = core == 1
    at_y, at_x = place // (2 * side), place // 2 % side
    first, second = jnp.where(upper, at_x, at_y), jnp.where(upper, at_y, at_x)
    layer = lax.axis_index("dp")
    spot = jnp.stack([core, first, second, layer])

    pieces = [down_piece(down_weight, width, k) for k in range(2)]
    value_other = core_swap(value_weight, width)
    output_other = core_swap(output_weight, width)
    input_mine = lax.dynamic_slice_in_dim(layer_input, core * half, half, 1)
    input_other = core_swap(
        lax.dynamic_slice_in_dim(layer_input, (1 - core) * half, half, 1), width
    )
    input_chip = jnp.where(
        upper,
        jnp.concatenate([input_other, input_mine], axis=0),
        jnp.concatenate([input_mine, input_other], axis=0),
    ).astype(jnp.float32)

    query, spot = lax.optimization_barrier((query, spot))
    latent = attend(query, cache, lengths, latent_width, chips)
    arrived = between_chips(latent, width)
    arrived_other = core_swap(arrived, width)
    arrived_other, pieces[0] = lax.optimization_barrier((arrived_other, pieces[0]))
    values = project(arrived, arrived_other, value_weight, value_other, spot, side, slots)
    attended_parts = sum_heads(values, output_weight, output_other, spot, side)

    attended_parts, later = lax.optimization_barrier((attended_parts, down_weight))
    pieces.append(down_piece(later, width, 2))
    later, pieces[2] = lax.optimization_barrier((down_weight, pieces[2]))
    pieces.append(down_piece(later, width, 3))

    summed = total(turn(attended_parts, 0, side, 1)).reshape(side, chip_slots, half)
    own_rows = (jnp.arange(side) == second)[:, None, None]
    summed = summed + jnp.where(own_rows, input_chip[None], 0.0)
    summed = summed.astype(jnp.bfloat16).reshape(line, half)
    summed, pieces[1] = lax.optimization_barrier((summed, pieces[1]))
    residual_line = total(turn([summed] * side, 1, side, 1)).astype(jnp.bfloat16)
    residual_mine = turn([residual_line] * side, 0, side, -1)
    residual_mine = lax.optimization_barrier(residual_mine)
    residual_other = [core_swap(part, width) for part in residual_mine]
    sums = gated(residual_mine, norm_gain, gate_weight, up_weight, spot, None)
    inner = gated(residual_other, norm_gain, gate_weight, up_weight, spot, sums)
    inner, pieces[3] = lax.optimization_barrier((inner, pieces[3]))
    inner_other = core_swap(inner, width)

    feed_parts = feed_forward(inner, inner_other, pieces, spot, side)
    feed_line = total(turn(feed_parts, 0, side, 1)).astype(jnp.bfloat16)
    feed = total(
        turn(
            [
                lax.dynamic_slice_in_dim(
                    feed_line, (second + k) % side * chip_slots, chip_slots, 0
                )
                for k in range(side)
            ],
            1,
            side,
            1,
        )
    )
    residual = lax.dynamic_slice_in_dim(residual_line, second * chip_slots, chip_slots, 0)
    cut = half // 2
    feed = jnp.where(
        layer // 2 == 1, jnp.concatenate([feed[:, cut:], feed[:, :cut]], axis=1), feed
    )
    mixed = (residual.astype(jnp.float32) + feed).astype(jnp.bfloat16)
    kept = lax.dynamic_slice_in_dim(mixed, core * slots, slots, 0)
    got = core_swap(lax.dynamic_slice_in_dim(mixed, (1 - core) * slots, slots, 0), width)
    out = jnp.where(
        upper,
        jnp.concatenate([got, kept], axis=1),
        jnp.concatenate([kept, got], axis=1),
    )
    live = jnp.arange(slots, dtype=jnp.int32) < counts[0]
    return jnp.where(live[:, None], out, jnp.bfloat16(0.0))


def solution(mesh):
    placed = (
        P(("dp", "tp"), None),
        P(("dp", "tp"), None, None),
        P(("dp", "tp"), None, None),
        P(("dp", "tp")),
        P(("dp", "tp")),
        P("tp", None, None),
        P("tp", None),
        P(),
        P(None, "tp"),
        P(None, "tp"),
        P("tp", "dp"),
    )
    width = mesh.shape["tp"]
    return jax.shard_map(
        lambda *args: on_device(*args, width),
        mesh=mesh,
        in_specs=placed,
        out_specs=P(("dp", "tp"), None),
        check_vma=False,
    )
```

```python
import math

import jax
import jax.numpy as jnp
from jax import lax
from jax.experimental import pallas as pl
from jax.experimental.pallas import tpu as pltpu
from jax.sharding import PartitionSpec as P

score_scale = 1.0 / 192.0**0.5
norm_eps = 1e-06


def core_swap(x, width):
    return lax.ppermute(x, "tp", [(i, i ^ 1) for i in range(width)])


def between_chips(x, width):
    groups = [[2 * chip + core for chip in range(width // 2)] for core in range(2)]
    return lax.all_to_all(x, "tp", 0, 0, tiled=True, axis_index_groups=groups)


def turn(parts, axis, side, sign):
    out = list(parts)
    for k in sorted(range(1, side), key=lambda step: min(step, side - step)):
        pairs = []
        for y in range(side):
            for x in range(side):
                for core in range(2):
                    if axis == core:
                        to = ((y + sign * k) % side) * side + x
                    else:
                        to = y * side + (x + sign * k) % side
                    pairs.append(((y * side + x) * 2 + core, to * 2 + core))
        out[k] = lax.ppermute(parts[k], "tp", pairs)
    return out


def total(parts):
    wide = parts[0].astype(jnp.float32)
    for part in parts[1:]:
        wide = wide + part.astype(jnp.float32)
    return wide


def down_piece(down_weight, width, k):
    pairs = []
    for layer in range(4):
        for place in range(width):
            chip, core = divmod(place, 2)
            cut, row_core = (layer >> 1) ^ (k >> 1), (layer & 1) ^ (k & 1)
            pairs.append(((2 * core + cut) * width + 2 * chip + row_core, layer * width + place))
    return lax.ppermute(down_weight, ("dp", "tp"), pairs)


in_vmem = pl.BlockSpec(memory_space=pltpu.VMEM)
in_hbm = pl.BlockSpec(memory_space=pltpu.HBM)
in_smem = pl.BlockSpec(memory_space=pltpu.SMEM)
across = (((1,), (1,)), ((), ()))


def product(a, b):
    return jnp.dot(a, b, preferred_element_type=jnp.float32)


def one_hot(source, columns):
    hit = source == lax.broadcasted_iota(jnp.int32, (source.shape[0], columns), 1)
    return jnp.where(hit, 1.0, 0.0).astype(jnp.bfloat16)


def line_numbers(rows):
    return lax.broadcasted_iota(jnp.int32, (rows, 1), 0)


def budget(mib):
    return pltpu.CompilerParams(vmem_limit_bytes=mib * 2**20)


def attend(query, cache, lengths, latent_width, chips):
    slots, heads, wide = query.shape
    ctx = cache.shape[1]
    group = heads // chips
    rows = slots * heads

    def kernel(lengths_ref, q_ref, cache_ref, out_ref, held_ref, sems):
        copies = [
            pltpu.make_async_copy(cache_ref.at[slot], held_ref.at[slot], sems.at[slot])
            for slot in range(slots)
        ]

        def score(slot):
            copies[slot].wait()
            place = lax.broadcasted_iota(jnp.int32, (1, ctx), 1)
            hidden = jnp.where(place < lengths_ref[slot], 0.0, -1e30)
            return product(q_ref[slot], held_ref[slot]) * (score_scale * math.log2(math.e)) + hidden

        def gather(slot, scores):
            raised = jnp.exp2(scores - jnp.max(scores, axis=1, keepdims=True))
            latent = lax.dot_general(
                raised.astype(jnp.bfloat16),
                held_ref[slot, :latent_width],
                across,
                preferred_element_type=jnp.float32,
            )
            latent = latent / jnp.sum(raised, axis=1, keepdims=True)
            return latent.astype(jnp.bfloat16)

        for copy in copies:
            copy.start()
        latents = []
        scores = score(0)
        for slot in range(slots):
            following = score(slot + 1) if slot + 1 < slots else None
            latents.append(gather(slot, scores))
            scores = following
        to = line_numbers(rows)
        source = to // group % slots * heads + to // (slots * group) * group + to % group
        out_ref[...] = product(
            one_hot(source, rows), jnp.concatenate(latents, axis=0)
        ).astype(jnp.bfloat16)

    out = pl.pallas_call(
        kernel,
        in_specs=[in_smem, in_vmem, in_hbm],
        out_specs=in_vmem,
        out_shape=jax.ShapeDtypeStruct((rows, latent_width), jnp.bfloat16),
        scratch_shapes=[
            pltpu.VMEM((slots, wide, ctx), jnp.bfloat16),
            pltpu.SemaphoreType.DMA((slots,)),
        ],
        compiler_params=budget(57),
        cost_estimate=pl.CostEstimate(
            flops=2 * rows * ctx * (wide + latent_width),
            bytes_accessed=2 * cache.size,
            transcendentals=rows * ctx,
        ),
    )(lengths, query, jnp.swapaxes(cache, 1, 2))
    return out.reshape(chips, slots * group, latent_width)


def project(latents, swapped, value_mine, value_other, spot, side, slots, before):
    chips, pairs, latent_width = latents.shape
    heads_here, _, head = value_mine.shape
    heads = 2 * heads_here
    rows = 2 * chips * slots
    line = rows // side
    lines = chips * pairs

    def kernel(spot_ref, latent_ref, vm_ref, vo_ref, *refs):
        out_ref = refs[-1]
        core, first = spot_ref[0], spot_ref[1]
        to = line_numbers(rows)
        along = (to // line + first) % side
        second = to // (2 * slots) % side
        chip = jnp.where(core == 0, along * side + second, second * side + along)
        from_other = (to // slots % 2 + core) % 2
        source = chip * pairs + to % slots * heads + (from_other != swapped) * (2 * lines)
        for index in range(heads):
            owner, weight_ref = (core, vm_ref) if index < heads_here else (1 - core, vo_ref)
            place = index % heads_here
            pick = one_hot(source + owner * heads_here + place, lines)
            picked = product(pick, latent_ref[...]).astype(jnp.bfloat16)
            value = product(picked, weight_ref[place]).astype(jnp.bfloat16)
            part = slice(index * head, (index + 1) * head)
            if swapped:
                value = jnp.where(from_other == swapped, value, refs[0][:, part])
            out_ref[:, part] = value

    return pl.pallas_call(
        kernel,
        in_specs=[in_smem] + [in_vmem] * (3 + swapped),
        out_specs=in_vmem,
        out_shape=jax.ShapeDtypeStruct((rows, heads * head), jnp.bfloat16),
        compiler_params=budget(16),
        cost_estimate=pl.CostEstimate(
            flops=64 * rows * latent_width * (lines + head), bytes_accessed=2 * latents.size, transcendentals=0
        ),
    )(
        spot,
        latents.reshape(lines, latent_width),
        value_mine,
        value_other,
        *([before] if swapped else []),
    )


def sum_heads(values, output_mine, output_other, spot, side):
    rows = values.shape[0]
    depth, model = output_mine.shape
    half = model // 2
    line = rows // side
    cuts = 2
    span = half // cuts

    def kernel(spot_ref, value_ref, om_ref, oo_ref, *refs):
        outs, (held_ref, sems) = refs[:side], refs[side:]
        copies = []
        for cut in range(cuts):
            start = pl.multiple_of(spot_ref[0] * half + cut * span, 128)
            copies.append(
                pltpu.make_async_copy(
                    oo_ref.at[:, pl.ds(start, span)], held_ref.at[cut], sems.at[cut]
                )
            )
            copies[-1].start()
        at = pl.ds(pl.multiple_of(spot_ref[0] * half, 128), half)
        mine = product(value_ref[:, :depth], om_ref[:, at])
        for cut in range(cuts):
            part = slice(cut * span, (cut + 1) * span)
            copies[cut].wait()
            result = mine[:, part] + product(value_ref[:, depth:], held_ref[cut])
            result = result.astype(jnp.bfloat16)
            for k in range(side):
                outs[k][:, part] = result[k * line : (k + 1) * line]

    return pl.pallas_call(
        kernel,
        in_specs=[in_smem] + [in_vmem] * 2 + [in_hbm],
        out_specs=[in_vmem] * side,
        out_shape=[jax.ShapeDtypeStruct((line, half), jnp.bfloat16)] * side,
        scratch_shapes=[
            pltpu.VMEM((cuts, depth, span), jnp.bfloat16),
            pltpu.SemaphoreType.DMA((cuts,)),
        ],
        compiler_params=budget(24),
        cost_estimate=pl.CostEstimate(
            flops=4 * rows * depth * half, bytes_accessed=4 * depth * half, transcendentals=0
        ),
    )(spot, values, output_mine, output_other)


def gated(parts, gain, gate_weight, up_weight, spot, before):
    side = len(parts)
    line, half = parts[0].shape
    rows = side * line
    units = gate_weight.shape[1]
    finish = before is not None

    def kernel(spot_ref, *refs):
        part_refs, refs = refs[:side], refs[side:]
        gain_ref, gate_ref, up_ref, refs = refs[0], refs[1], refs[2], refs[3:]
        if finish:
            sum_before, square_before, out_ref = refs
        else:
            sum_ref, square_ref = refs
        core, first, second = spot_ref[0], spot_ref[1], spot_ref[2]
        owner = 1 - core if finish else core
        at = pl.ds(pl.multiple_of(owner * half, 128), half)
        block = jnp.concatenate([ref[...] for ref in part_refs], axis=0)
        if finish:
            wide = product(one_hot(swapped_rows(rows, line, side, first, second), rows), block)
        else:
            wide = block.astype(jnp.float32)
        squares = jnp.zeros((rows, 128), jnp.float32)
        for k in range(half // 128):
            lanes = wide[:, k * 128 : (k + 1) * 128]
            squares = squares + lanes * lanes
        scaled = (wide * gain_ref[:, at]).astype(jnp.bfloat16).T
        total = jnp.concatenate(
            [product(gate_ref[:, at], scaled), product(up_ref[:, at], scaled)], axis=0
        ).T
        if finish:
            total = total + sum_before[...]
            mean = jnp.sum(squares + square_before[...], axis=1, keepdims=True) / (2 * half)
            total = total * lax.rsqrt(mean + norm_eps)
            gate = total[:, :units]
            out_ref[...] = (gate / (1.0 + jnp.exp(-gate)) * total[:, units:]).astype(jnp.bfloat16)
        else:
            sum_ref[...] = total
            square_ref[...] = squares

    sums = [
        jax.ShapeDtypeStruct((rows, 2 * units), jnp.float32),
        jax.ShapeDtypeStruct((rows, 128), jnp.float32),
    ]
    return pl.pallas_call(
        kernel,
        in_specs=[in_smem] + [in_vmem] * (side + 3 + 2 * finish),
        out_specs=in_vmem if finish else [in_vmem] * 2,
        out_shape=jax.ShapeDtypeStruct((rows, units), jnp.bfloat16) if finish else sums,
        compiler_params=budget(24),
        cost_estimate=pl.CostEstimate(
            flops=4 * rows * half * units, bytes_accessed=4 * half * units, transcendentals=0
        ),
    )(spot, *parts, gain[None, :], gate_weight.T, up_weight.T, *(before or []))


def swapped_rows(rows, line, side, first, second):
    chip_slots = line // side
    to = line_numbers(rows)
    along = (to // line + first) % side
    beside = to // chip_slots % side
    return ((beside - second + side) % side) * line + along * chip_slots + to % chip_slots


def feed_forward(inner, inner_other, pieces, spot, side):
    rows, units = inner.shape
    cut = pieces[0].shape[1]
    line = rows // side

    def kernel(spot_ref, inner_ref, other_ref, a_ref, b_ref, c_ref, d_ref, *outs):
        core, first, second, layer = spot_ref[0], spot_ref[1], spot_ref[2], spot_ref[3]
        pick = one_hot(swapped_rows(rows, line, side, first, second), rows)
        other = product(pick, other_ref[...]).astype(jnp.bfloat16)
        mine = inner_ref[...]
        same = core == layer % 2
        even = jnp.where(same, mine, other)
        odd = jnp.where(same, other, mine)
        for start, first_ref, second_ref in ((0, a_ref, b_ref), (cut, c_ref, d_ref)):
            result = product(even, first_ref[...]) + product(odd, second_ref[...])
            result = result.astype(jnp.bfloat16)
            for k in range(side):
                outs[k][:, start : start + cut] = result[k * line : (k + 1) * line]

    return pl.pallas_call(
        kernel,
        in_specs=[in_smem] + [in_vmem] * 6,
        out_specs=[in_vmem] * side,
        out_shape=[jax.ShapeDtypeStruct((line, 2 * cut), jnp.bfloat16)] * side,
        compiler_params=budget(24),
        cost_estimate=pl.CostEstimate(
            flops=8 * rows * units * cut, bytes_accessed=8 * units * cut, transcendentals=0
        ),
    )(spot, inner, inner_other, *pieces)


def on_device(
    layer_input,
    query,
    cache,
    lengths,
    counts,
    value_weight,
    output_weight,
    norm_gain,
    gate_weight,
    up_weight,
    down_weight,
    width,
):
    slots, model = layer_input.shape
    half = model // 2
    chips = width // 2

    heads_here, latent_width, head = value_weight.shape
    side = math.isqrt(chips)
    chip_slots = 2 * slots
    line = side * chip_slots
    place = lax.axis_index("tp")
    core = place % 2
    upper = core == 1
    at_y, at_x = place // (2 * side), place // 2 % side
    first, second = jnp.where(upper, at_x, at_y), jnp.where(upper, at_y, at_x)
    layer = lax.axis_index("dp")
    spot = jnp.stack([core, first, second, layer])

    pieces = [down_piece(down_weight, width, k) for k in range(2)]
    value_other = core_swap(value_weight, width)
    output_other = core_swap(output_weight, width)
    input_mine = lax.dynamic_slice_in_dim(layer_input, core * half, half, 1)
    input_other = core_swap(
        lax.dynamic_slice_in_dim(layer_input, (1 - core) * half, half, 1), width
    )
    input_chip = jnp.where(
        upper,
        jnp.concatenate([input_other, input_mine], axis=0),
        jnp.concatenate([input_mine, input_other], axis=0),
    ).astype(jnp.float32)

    query, spot = lax.optimization_barrier((query, spot))
    latent = attend(query, cache, lengths, latent_width, chips)
    arrived = between_chips(latent, width)
    arrived_other = core_swap(arrived, width)
    arrived_other, pieces[0] = lax.optimization_barrier((arrived_other, pieces[0]))
    values = project(arrived, 0, value_weight, value_other, spot, side, slots, None)
    values = project(arrived_other, 1, value_weight, value_other, spot, side, slots, values)
    attended_parts = sum_heads(values, output_weight, output_other, spot, side)

    attended_parts, later = lax.optimization_barrier((attended_parts, down_weight))
    pieces.append(down_piece(later, width, 2))
    later, pieces[2] = lax.optimization_barrier((down_weight, pieces[2]))
    pieces.append(down_piece(later, width, 3))

    summed = total(turn(attended_parts, 0, side, 1)).reshape(side, chip_slots, half)
    own_rows = (jnp.arange(side) == second)[:, None, None]
    summed = summed + jnp.where(own_rows, input_chip[None], 0.0)
    summed = summed.astype(jnp.bfloat16).reshape(line, half)
    summed, pieces[1] = lax.optimization_barrier((summed, pieces[1]))
    residual_line = total(turn([summed] * side, 1, side, 1)).astype(jnp.bfloat16)
    residual_mine = turn([residual_line] * side, 0, side, -1)
    residual_mine = lax.optimization_barrier(residual_mine)
    residual_other = [core_swap(part, width) for part in residual_mine]
    sums = gated(residual_mine, norm_gain, gate_weight, up_weight, spot, None)
    inner = gated(residual_other, norm_gain, gate_weight, up_weight, spot, sums)
    inner, pieces[3] = lax.optimization_barrier((inner, pieces[3]))
    inner_other = core_swap(inner, width)

    feed_parts = feed_forward(inner, inner_other, pieces, spot, side)
    feed_line = total(turn(feed_parts, 0, side, 1)).astype(jnp.bfloat16)
    feed = total(
        turn(
            [
                lax.dynamic_slice_in_dim(
                    feed_line, (second + k) % side * chip_slots, chip_slots, 0
                )
                for k in range(side)
            ],
            1,
            side,
            1,
        )
    )
    residual = lax.dynamic_slice_in_dim(residual_line, second * chip_slots, chip_slots, 0)
    cut = half // 2
    feed = jnp.where(
        layer // 2 == 1, jnp.concatenate([feed[:, cut:], feed[:, :cut]], axis=1), feed
    )
    mixed = (residual.astype(jnp.float32) + feed).astype(jnp.bfloat16)
    kept = lax.dynamic_slice_in_dim(mixed, core * slots, slots, 0)
    got = core_swap(lax.dynamic_slice_in_dim(mixed, (1 - core) * slots, slots, 0), width)
    out = jnp.where(
        upper,
        jnp.concatenate([got, kept], axis=1),
        jnp.concatenate([kept, got], axis=1),
    )
    live = jnp.arange(slots, dtype=jnp.int32) < counts[0]
    return jnp.where(live[:, None], out, jnp.bfloat16(0.0))


def solution(mesh):
    placed = (
        P(("dp", "tp"), None),
        P(("dp", "tp"), None, None),
        P(("dp", "tp"), None, None),
        P(("dp", "tp")),
        P(("dp", "tp")),
        P("tp", None, None),
        P("tp", None),
        P(),
        P(None, "tp"),
        P(None, "tp"),
        P("tp", "dp"),
    )
    width = mesh.shape["tp"]
    return jax.shard_map(
        lambda *args: on_device(*args, width),
        mesh=mesh,
        in_specs=placed,
        out_specs=P(("dp", "tp"), None),
        check_vma=False,
    )
```

```python
import math

import jax
import jax.numpy as jnp
from jax import lax
from jax.experimental import pallas as pl
from jax.experimental.pallas import tpu as pltpu
from jax.sharding import PartitionSpec as P

score_scale = 1.0 / 192.0**0.5
norm_eps = 1e-06


def core_swap(x, width):
    return lax.ppermute(x, "tp", [(i, i ^ 1) for i in range(width)])


def between_chips(x, width):
    groups = [[2 * chip + core for chip in range(width // 2)] for core in range(2)]
    return lax.all_to_all(x, "tp", 0, 0, tiled=True, axis_index_groups=groups)


def turn(parts, axis, side, sign):
    out = list(parts)
    for k in sorted(range(1, side), key=lambda step: min(step, side - step)):
        pairs = []
        for y in range(side):
            for x in range(side):
                for core in range(2):
                    if axis == core:
                        to = ((y + sign * k) % side) * side + x
                    else:
                        to = y * side + (x + sign * k) % side
                    pairs.append(((y * side + x) * 2 + core, to * 2 + core))
        out[k] = lax.ppermute(parts[k], "tp", pairs)
    return out


def total(parts):
    wide = parts[0].astype(jnp.float32)
    for part in parts[1:]:
        wide = wide + part.astype(jnp.float32)
    return wide


def down_piece(down_weight, width, k):
    pairs = []
    for layer in range(4):
        for place in range(width):
            chip, core = divmod(place, 2)
            cut, row_core = (layer >> 1) ^ (k >> 1), (layer & 1) ^ (k & 1)
            pairs.append(((2 * core + cut) * width + 2 * chip + row_core, layer * width + place))
    return lax.ppermute(down_weight, ("dp", "tp"), pairs)


in_vmem = pl.BlockSpec(memory_space=pltpu.VMEM)
in_hbm = pl.BlockSpec(memory_space=pltpu.HBM)
in_smem = pl.BlockSpec(memory_space=pltpu.SMEM)
across = (((1,), (1,)), ((), ()))


def product(a, b):
    return jnp.dot(a, b, preferred_element_type=jnp.float32)


def one_hot(source, columns):
    hit = source == lax.broadcasted_iota(jnp.int32, (source.shape[0], columns), 1)
    return jnp.where(hit, 1.0, 0.0).astype(jnp.bfloat16)


def line_numbers(rows):
    return lax.broadcasted_iota(jnp.int32, (rows, 1), 0)


def budget(mib):
    return pltpu.CompilerParams(vmem_limit_bytes=mib * 2**20)


def attend(query, cache, lengths, latent_width, chips):
    slots, heads, wide = query.shape
    ctx = cache.shape[1]
    group = heads // chips
    rows = slots * heads

    def kernel(lengths_ref, q_ref, cache_ref, out_ref, held_ref, sems):
        copies = [
            pltpu.make_async_copy(cache_ref.at[slot], held_ref.at[slot], sems.at[slot])
            for slot in range(slots)
        ]

        def score(slot):
            copies[slot].wait()
            place = lax.broadcasted_iota(jnp.int32, (1, ctx), 1)
            hidden = jnp.where(place < lengths_ref[slot], 0.0, -1e30)
            return product(q_ref[slot], held_ref[slot]) * (score_scale * math.log2(math.e)) + hidden

        def gather(slot, scores):
            raised = jnp.exp2(scores - jnp.max(scores, axis=1, keepdims=True))
            latent = lax.dot_general(
                raised.astype(jnp.bfloat16),
                held_ref[slot, :latent_width],
                across,
                preferred_element_type=jnp.float32,
            )
            latent = latent / jnp.sum(raised, axis=1, keepdims=True)
            return latent.astype(jnp.bfloat16)

        for copy in copies:
            copy.start()
        latents = []
        scores = score(0)
        for slot in range(slots):
            following = score(slot + 1) if slot + 1 < slots else None
            latents.append(gather(slot, scores))
            scores = following
        to = line_numbers(rows)
        source = to // group % slots * heads + to // (slots * group) * group + to % group
        out_ref[...] = product(
            one_hot(source, rows), jnp.concatenate(latents, axis=0)
        ).astype(jnp.bfloat16)

    out = pl.pallas_call(
        kernel,
        in_specs=[in_smem, in_vmem, in_hbm],
        out_specs=in_vmem,
        out_shape=jax.ShapeDtypeStruct((rows, latent_width), jnp.bfloat16),
        scratch_shapes=[
            pltpu.VMEM((slots, wide, ctx), jnp.bfloat16),
            pltpu.SemaphoreType.DMA((slots,)),
        ],
        compiler_params=budget(57),
        cost_estimate=pl.CostEstimate(
            flops=2 * rows * ctx * (wide + latent_width),
            bytes_accessed=2 * cache.size,
            transcendentals=rows * ctx,
        ),
    )(lengths, query, jnp.swapaxes(cache, 1, 2))
    return out.reshape(chips, slots * group, latent_width)


def project(mine, other, value_mine, value_other, spot, side, slots):
    chips, pairs, latent_width = mine.shape
    heads_here, _, head = value_mine.shape
    heads = 2 * heads_here
    rows = 2 * chips * slots
    line = rows // side
    lines = chips * pairs

    def kernel(spot_ref, mine_ref, other_ref, vm_ref, vo_ref, out_ref):
        core, first = spot_ref[0], spot_ref[1]
        to = line_numbers(rows)
        along = (to // line + first) % side
        second = to // (2 * slots) % side
        chip = jnp.where(core == 0, along * side + second, second * side + along)
        from_other = (to // slots % 2 + core) % 2
        source = from_other * lines + chip * pairs + to % slots * heads
        latents = jnp.concatenate([mine_ref[...], other_ref[...]], axis=0)
        for index in range(heads):
            owner, weight_ref = (core, vm_ref) if index < heads_here else (1 - core, vo_ref)
            place = index % heads_here
            pick = one_hot(source + owner * heads_here + place, 2 * lines)
            picked = product(pick, latents).astype(jnp.bfloat16)
            out_ref[:, index * head : (index + 1) * head] = product(
                picked, weight_ref[place]
            ).astype(jnp.bfloat16)

    return pl.pallas_call(
        kernel,
        in_specs=[in_smem] + [in_vmem] * 4,
        out_specs=in_vmem,
        out_shape=jax.ShapeDtypeStruct((rows, heads * head), jnp.bfloat16),
        compiler_params=budget(16),
        cost_estimate=pl.CostEstimate(
            flops=64 * rows * latent_width * (lines + head), bytes_accessed=4 * mine.size, transcendentals=0
        ),
    )(
        spot,
        mine.reshape(lines, latent_width),
        other.reshape(lines, latent_width),
        value_mine,
        value_other,
    )


def sum_heads(values, output_mine, output_other, spot, side):
    rows = values.shape[0]
    depth, model = output_mine.shape
    half = model // 2
    line = rows // side
    cuts = 4
    span = half // cuts

    def kernel(spot_ref, value_ref, om_ref, oo_ref, *refs):
        outs, (held_ref, sems) = refs[:side], refs[side:]
        copies = []
        for cut in range(cuts):
            start = pl.multiple_of(spot_ref[0] * half + cut * span, 128)
            copies.append(
                pltpu.make_async_copy(
                    oo_ref.at[:, pl.ds(start, span)], held_ref.at[cut], sems.at[cut]
                )
            )
            copies[-1].start()
        at = pl.ds(pl.multiple_of(spot_ref[0] * half, 128), half)
        mine = product(value_ref[:, :depth], om_ref[:, at])
        for cut in range(cuts):
            part = slice(cut * span, (cut + 1) * span)
            copies[cut].wait()
            result = mine[:, part] + product(value_ref[:, depth:], held_ref[cut])
            result = result.astype(jnp.bfloat16)
            for k in range(side):
                outs[k][:, part] = result[k * line : (k + 1) * line]

    return pl.pallas_call(
        kernel,
        in_specs=[in_smem] + [in_vmem] * 2 + [in_hbm],
        out_specs=[in_vmem] * side,
        out_shape=[jax.ShapeDtypeStruct((line, half), jnp.bfloat16)] * side,
        scratch_shapes=[
            pltpu.VMEM((cuts, depth, span), jnp.bfloat16),
            pltpu.SemaphoreType.DMA((cuts,)),
        ],
        compiler_params=budget(24),
        cost_estimate=pl.CostEstimate(
            flops=4 * rows * depth * half, bytes_accessed=4 * depth * half, transcendentals=0
        ),
    )(spot, values, output_mine, output_other)


def gated(parts, gain, gate_weight, up_weight, spot, before):
    side = len(parts)
    line, half = parts[0].shape
    rows = side * line
    units = gate_weight.shape[1]
    finish = before is not None

    def kernel(spot_ref, *refs):
        part_refs, refs = refs[:side], refs[side:]
        gain_ref, gate_ref, up_ref, refs = refs[0], refs[1], refs[2], refs[3:]
        if finish:
            sum_before, square_before, out_ref = refs
        else:
            sum_ref, square_ref = refs
        core, first, second = spot_ref[0], spot_ref[1], spot_ref[2]
        owner = 1 - core if finish else core
        at = pl.ds(pl.multiple_of(owner * half, 128), half)
        block = jnp.concatenate([ref[...] for ref in part_refs], axis=0)
        if finish:
            wide = product(one_hot(swapped_rows(rows, line, side, first, second), rows), block)
        else:
            wide = block.astype(jnp.float32)
        squares = jnp.zeros((rows, 128), jnp.float32)
        for k in range(half // 128):
            lanes = wide[:, k * 128 : (k + 1) * 128]
            squares = squares + lanes * lanes
        scaled = (wide * gain_ref[:, at]).astype(jnp.bfloat16).T
        total = jnp.concatenate(
            [product(gate_ref[:, at], scaled), product(up_ref[:, at], scaled)], axis=0
        ).T
        if finish:
            total = total + sum_before[...]
            mean = jnp.sum(squares + square_before[...], axis=1, keepdims=True) / (2 * half)
            total = total * lax.rsqrt(mean + norm_eps)
            gate = total[:, :units]
            out_ref[...] = (gate / (1.0 + jnp.exp(-gate)) * total[:, units:]).astype(jnp.bfloat16)
        else:
            sum_ref[...] = total
            square_ref[...] = squares

    sums = [
        jax.ShapeDtypeStruct((rows, 2 * units), jnp.float32),
        jax.ShapeDtypeStruct((rows, 128), jnp.float32),
    ]
    return pl.pallas_call(
        kernel,
        in_specs=[in_smem] + [in_vmem] * (side + 3 + 2 * finish),
        out_specs=in_vmem if finish else [in_vmem] * 2,
        out_shape=jax.ShapeDtypeStruct((rows, units), jnp.bfloat16) if finish else sums,
        compiler_params=budget(24),
        cost_estimate=pl.CostEstimate(
            flops=4 * rows * half * units, bytes_accessed=4 * half * units, transcendentals=0
        ),
    )(spot, *parts, gain[None, :], gate_weight.T, up_weight.T, *(before or []))


def swapped_rows(rows, line, side, first, second):
    chip_slots = line // side
    to = line_numbers(rows)
    along = (to // line + first) % side
    beside = to // chip_slots % side
    return ((beside - second + side) % side) * line + along * chip_slots + to % chip_slots


def feed_forward(inner, inner_other, pieces, spot, side):
    rows, units = inner.shape
    cut = pieces[0].shape[1]
    line = rows // side

    def kernel(spot_ref, inner_ref, other_ref, a_ref, b_ref, c_ref, d_ref, *outs):
        core, first, second, layer = spot_ref[0], spot_ref[1], spot_ref[2], spot_ref[3]
        pick = one_hot(swapped_rows(rows, line, side, first, second), rows)
        other = product(pick, other_ref[...]).astype(jnp.bfloat16)
        mine = inner_ref[...]
        same = core == layer % 2
        even = jnp.where(same, mine, other)
        odd = jnp.where(same, other, mine)
        for start, first_ref, second_ref in ((0, a_ref, b_ref), (cut, c_ref, d_ref)):
            result = product(even, first_ref[...]) + product(odd, second_ref[...])
            result = result.astype(jnp.bfloat16)
            for k in range(side):
                outs[k][:, start : start + cut] = result[k * line : (k + 1) * line]

    return pl.pallas_call(
        kernel,
        in_specs=[in_smem] + [in_vmem] * 6,
        out_specs=[in_vmem] * side,
        out_shape=[jax.ShapeDtypeStruct((line, 2 * cut), jnp.bfloat16)] * side,
        compiler_params=budget(24),
        cost_estimate=pl.CostEstimate(
            flops=8 * rows * units * cut, bytes_accessed=8 * units * cut, transcendentals=0
        ),
    )(spot, inner, inner_other, *pieces)


def on_device(
    layer_input,
    query,
    cache,
    lengths,
    counts,
    value_weight,
    output_weight,
    norm_gain,
    gate_weight,
    up_weight,
    down_weight,
    width,
):
    slots, model = layer_input.shape
    half = model // 2
    chips = width // 2

    heads_here, latent_width, head = value_weight.shape
    side = math.isqrt(chips)
    chip_slots = 2 * slots
    line = side * chip_slots
    place = lax.axis_index("tp")
    core = place % 2
    upper = core == 1
    at_y, at_x = place // (2 * side), place // 2 % side
    first, second = jnp.where(upper, at_x, at_y), jnp.where(upper, at_y, at_x)
    layer = lax.axis_index("dp")
    spot = jnp.stack([core, first, second, layer])

    pieces = [down_piece(down_weight, width, k) for k in range(2)]
    value_other = core_swap(value_weight, width)
    output_other = core_swap(output_weight, width)
    input_mine = lax.dynamic_slice_in_dim(layer_input, core * half, half, 1)
    input_other = core_swap(
        lax.dynamic_slice_in_dim(layer_input, (1 - core) * half, half, 1), width
    )
    input_chip = jnp.where(
        upper,
        jnp.concatenate([input_other, input_mine], axis=0),
        jnp.concatenate([input_mine, input_other], axis=0),
    ).astype(jnp.float32)

    query, spot = lax.optimization_barrier((query, spot))
    latent = attend(query, cache, lengths, latent_width, chips)
    arrived = between_chips(latent, width)
    arrived_other = core_swap(arrived, width)
    arrived_other, pieces[0] = lax.optimization_barrier((arrived_other, pieces[0]))
    values = project(arrived, arrived_other, value_weight, value_other, spot, side, slots)
    attended_parts = sum_heads(values, output_weight, output_other, spot, side)

    attended_parts, later = lax.optimization_barrier((attended_parts, down_weight))
    pieces.append(down_piece(later, width, 2))
    later, pieces[2] = lax.optimization_barrier((down_weight, pieces[2]))
    pieces.append(down_piece(later, width, 3))

    summed = total(turn(attended_parts, 0, side, 1)).reshape(side, chip_slots, half)
    own_rows = (jnp.arange(side) == second)[:, None, None]
    summed = summed + jnp.where(own_rows, input_chip[None], 0.0)
    summed = summed.astype(jnp.bfloat16).reshape(line, half)
    summed, pieces[1] = lax.optimization_barrier((summed, pieces[1]))
    residual_line = total(turn([summed] * side, 1, side, 1)).astype(jnp.bfloat16)
    residual_mine = turn([residual_line] * side, 0, side, -1)
    residual_mine = lax.optimization_barrier(residual_mine)
    residual_other = [core_swap(part, width) for part in residual_mine]
    sums = gated(residual_mine, norm_gain, gate_weight, up_weight, spot, None)
    inner = gated(residual_other, norm_gain, gate_weight, up_weight, spot, sums)
    inner, pieces[3] = lax.optimization_barrier((inner, pieces[3]))
    inner_other = core_swap(inner, width)

    feed_parts = feed_forward(inner, inner_other, pieces, spot, side)
    feed_line = total(turn(feed_parts, 0, side, 1)).astype(jnp.bfloat16)
    feed = total(
        turn(
            [
                lax.dynamic_slice_in_dim(
                    feed_line, (second + k) % side * chip_slots, chip_slots, 0
                )
                for k in range(side)
            ],
            1,
            side,
            1,
        )
    )
    residual = lax.dynamic_slice_in_dim(residual_line, second * chip_slots, chip_slots, 0)
    cut = half // 2
    feed = jnp.where(
        layer // 2 == 1, jnp.concatenate([feed[:, cut:], feed[:, :cut]], axis=1), feed
    )
    mixed = (residual.astype(jnp.float32) + feed).astype(jnp.bfloat16)
    kept = lax.dynamic_slice_in_dim(mixed, core * slots, slots, 0)
    got = core_swap(lax.dynamic_slice_in_dim(mixed, (1 - core) * slots, slots, 0), width)
    out = jnp.where(
        upper,
        jnp.concatenate([got, kept], axis=1),
        jnp.concatenate([kept, got], axis=1),
    )
    live = jnp.arange(slots, dtype=jnp.int32) < counts[0]
    return jnp.where(live[:, None], out, jnp.bfloat16(0.0))


def solution(mesh):
    placed = (
        P(("dp", "tp"), None),
        P(("dp", "tp"), None, None),
        P(("dp", "tp"), None, None),
        P(("dp", "tp")),
        P(("dp", "tp")),
        P("tp", None, None),
        P("tp", None),
        P(),
        P(None, "tp"),
        P(None, "tp"),
        P("tp", "dp"),
    )
    width = mesh.shape["tp"]
    return jax.shard_map(
        lambda *args: on_device(*args, width),
        mesh=mesh,
        in_specs=placed,
        out_specs=P(("dp", "tp"), None),
        check_vma=False,
    )
```
